32 devices in a mesh: tm: 4 (over x, core), space: 8 (over z, y).
Axes of the slice: x: 2, y: 2, z: 4, core: 2. Of those that a mesh axis runs over, the one named last changes fastest.
Arguments:
- forcing: bfloat16 [4, 4, 6, 256, 1024], P('tm', None, None, None, 'space'), may hold values from -6 to 6
- zonal_courant: float32 [4, 256, 1024], P('tm', None, 'space'), may hold values from -0.3 to 0.3
- meridional_courant: float32 [4, 256, 1024], P('tm', None, 'space'), may hold values from -0.3 to 0.3
- zonal_faces: float32 [4, 256, 1024], P('tm', None, 'space'), may hold values from 0.1 to 0.4
- meridional_faces: float32 [4, 256, 1024], P('tm', None, 'space'), may hold values from 0.1 to 0.4
- coupling: float32 [4, 6, 6], P('tm'), may hold values from -0.375 to 0.375
Outputs:
- adjoint_start: float32 [4, 6, 256, 1024], P('tm', None, None, 'space')
The draws below stay inside these ranges and needn't reach their ends.
All inputs are finite; a program needn't handle non-finite values.
Results may differ from the reference program's by a relative error of at most 0.0015.
Values may be sent and summed in bfloat16 or wider, within the bound.
No kernel may reach another device: no remote copies, remote signals or barrier semaphores. Data moves between devices by JAX's collectives and lax.ppermute only.
A program may use at most 64 MiB of HBM per device.

```python
import math
import jax
import jax.numpy as jnp
from jax import lax

F = 6
NLAT = 256
STEPS = 4
SWEEPS = 2
NSUB = 4
NLON = 1024


def steps_of(stream_key, dims, pieces, least, high):
    loudness = 1.0
    for position, parts in pieces:
        draws = jax.random.uniform(jax.random.fold_in(jax.random.fold_in(stream_key, 6), position), (parts,), jnp.float32, least / len(pieces), high / len(pieces))
        loudness = loudness * jnp.repeat(jnp.exp(draws), dims[position] // parts).reshape((-1,) + (1,) * (len(dims) - 1 - position))
    return loudness


def scatter_about(rng, extent, deviation, bound, cuts=(), kind=jnp.bfloat16):
    array = jax.random.normal(rng, extent, jnp.float32) * deviation
    if len(cuts) > 0:
        array = steps_of(rng, extent, cuts, -0.22, 0.18) * array
    return jnp.clip(array, min=-bound, max=bound).astype(kind)


def setup_inputs(seed: int = 0) -> dict:
    key_of = jax.random.split(jax.random.key(seed), 7)
    return {
        "forcing": scatter_about(key_of[0], (NSUB, STEPS, F, NLAT, NLON), 1.0, 6.0, ((0, 4), (4, 8))),
        "zonal_courant": jnp.clip(jax.random.uniform(key_of[1], (NSUB, NLAT, NLON), jnp.float32, -0.3, 0.3) * steps_of(key_of[1], (NSUB, NLAT, NLON), ((0, 4), (2, 8)), -0.4, 0.0), -0.3, 0.3),
        "meridional_courant": jnp.clip(jax.random.uniform(key_of[2], (NSUB, NLAT, NLON), jnp.float32, -0.3, 0.3) * steps_of(key_of[2], (NSUB, NLAT, NLON), ((0, 4), (2, 8)), -0.4, 0.0), -0.3, 0.3),
        "zonal_faces": jnp.clip(jnp.exp(math.log(0.4) - 1.3862944 * jax.random.uniform(key_of[3], (NSUB, NLAT, NLON), jnp.float32) ** steps_of(key_of[3], (NSUB, NLAT, NLON), ((0, 4), (2, 8)), -0.2, 0.2)), 0.1, 0.4),
        "meridional_faces": jnp.clip(jnp.exp(math.log(0.4) - 1.3862944 * jax.random.uniform(key_of[4], (NSUB, NLAT, NLON), jnp.float32) ** steps_of(key_of[4], (NSUB, NLAT, NLON), ((0, 4), (2, 8)), -0.2, 0.2)), 0.1, 0.4),
        "coupling": scatter_about(key_of[5], (NSUB, F, F), 0.06, 0.375, ((0, 4),), jnp.float32),
    }


OMEGA = 0.4


def north(values):
    zero_edge = jnp.zeros_like(values[..., :1, :])
    return jnp.concatenate([values[..., 1:, :], zero_edge], axis=-2)


def south(values):
    zero_edge = jnp.zeros_like(values[..., :1, :])
    return jnp.concatenate([zero_edge, values[..., :-1, :]], axis=-2)


def operator_h(state_now, face_east, northern):
    face_west = jnp.roll(face_east, 1, axis=-1)
    east_side = jnp.roll(state_now, -1, axis=-1)
    west_side = jnp.roll(state_now, 1, axis=-1)
    return (state_now + face_east * (state_now - east_side) + face_west * (state_now - west_side)
            + northern * (state_now - north(state_now)) + south(northern) * (state_now - south(state_now)))


def smoother(source, face_east, northern):
    smoothed = OMEGA * source
    for sweep_index in range(SWEEPS):
        smoothed = smoothed + OMEGA * (source - operator_h(smoothed, face_east, northern))
    return smoothed


def transposed_explicit(smoothed, courant_x, courant_y, coupling_now):
    zonal_flux = courant_x * smoothed
    meridional_flux = courant_y * smoothed
    mixing = jnp.einsum("gf,gab->fab", coupling_now, smoothed, precision=lax.Precision.HIGHEST)
    zonal_term = 0.5 * (jnp.roll(zonal_flux, -1, axis=-1) - jnp.roll(zonal_flux, 1, axis=-1))
    meridional_term = 0.5 * (north(meridional_flux) - south(meridional_flux))
    return smoothed + mixing + zonal_term + meridional_term


def reference(forcing, zonal_courant, meridional_courant, zonal_faces, meridional_faces, coupling):
    row_index = lax.broadcasted_iota(jnp.int32, meridional_faces.shape, 1)
    northern_all = jnp.where(row_index < NLAT - 1, meridional_faces, jnp.zeros_like(meridional_faces))
    adjoint = jnp.zeros((F, NLAT, NLON), jnp.float32)
    starts = []
    for window in reversed(range(NSUB)):
        for step_index in reversed(range(STEPS)):
            smoothed = smoother(adjoint, zonal_faces[window], northern_all[window])
            adjoint = transposed_explicit(smoothed, zonal_courant[window], meridional_courant[window], coupling[window])
            adjoint = adjoint + forcing[window, step_index].astype(jnp.float32)
        starts.append(adjoint)
    return jnp.stack(starts[::-1], axis=0)
```

```python
import functools

import jax
import jax.numpy as jnp
from jax import lax
from jax.experimental import pallas as pl
from jax.experimental.pallas import tpu as pltpu
from jax.sharding import PartitionSpec as P

SWEEPS = 2
OMEGA = 0.4
SUB = 8
REACH = SWEEPS + 1
VMEM_BYTES = 48 * 2**20
F32 = jnp.float32
BF16 = jnp.bfloat16


class Sizes:
    def __init__(self, forcing_shape):
        _, self.steps, self.fields, self.rows, self.strip = forcing_shape
        self.lanes = self.rows // 2
        self.halo = 2 * REACH * self.steps
        self.main = self.strip // 2 + 2 * self.halo
        self.window = self.main + self.halo
        self.span = self.window // SUB
        self.shift = self.strip - self.main
        self.own = self.strip // 2
        self.groups = [-(-REACH * (self.steps + k) // SUB) for k in range(self.steps)]
        self.group_start = [self.fields * sum(self.groups[:k]) for k in range(self.steps)]
        self.coef_start = self.fields * sum(self.groups)
        self.coef_groups = self.halo // SUB
        self.payload = self.coef_start + 4 * self.coef_groups
        self.message = self.own + self.halo


def half_and_chip():
    tm = lax.axis_index("tm")
    return lax.rem(tm, 2), tm // 2


def prepare_kernel(z, fo, zc, mc, zf, mf, cp, keep_f, send_f, keep_c, send_c, pay_a, pay_b, buf):
    half, _ = half_and_chip()
    left = half == 0
    row = lax.broadcasted_iota(jnp.int32, (z.rows, z.strip), 0)

    def columns(values, slot):
        buf[slot] = values
        return [buf[slot, pl.ds(p, z.lanes, stride=2), :].T for p in range(2)]

    def split(both, groups, start, keep, send):
        for p in range(2):
            low, high = both[p][: z.main], both[p][z.shift :]
            keep[p] = jnp.where(left, low, high).astype(keep.dtype)
            send[p] = jnp.where(left, high, low).astype(send.dtype)
        for g in range(groups):
            lo, hi = SUB * g, z.strip - SUB * (groups - g)
            west = jnp.concatenate([both[p][lo : lo + SUB] for p in range(2)], axis=0)
            east = jnp.concatenate([both[p][hi : hi + SUB] for p in range(2)], axis=0)
            pay_a[start + g] = jnp.where(left, west, east).astype(BF16)
            pay_b[start + g] = jnp.where(left, east, west).astype(BF16)

    slots = buf.shape[0]
    count = 0
    for c, ref in enumerate((zf, mf, zc, mc)):
        values = ref[0]
        if c == 1:
            values = jnp.where(row < z.rows - 1, values, jnp.zeros_like(values))
        both = columns(values, count % slots)
        split(both, z.coef_groups, z.coef_start + c * z.coef_groups, keep_c.at[c], send_c.at[c])
        count += 1
    for ref in (keep_c, send_c):
        ref[4, 0, : z.fields, : z.fields] = cp[0]
    for k in range(z.steps):
        for f in range(z.fields):
            both = columns(fo[0, k, f].astype(F32), count % slots)
            split(both, z.groups[k], z.group_start[k] + f * z.groups[k], keep_f.at[k, f], send_f.at[k, f])
            count += 1


def fill_ghosts(ref, span, count):
    for n in range(count):
        for p in range(2):
            ref[0, n, p] = pltpu.roll(ref[span, n, p], 1, 0)
            ref[span + 1, n, p] = pltpu.roll(ref[1, n, p], SUB - 1, 0)


def chain_kernel(z, first, active, *refs):
    n_in = 6 if first else 10
    kf, rf, kc, rc, ra, rb = refs[:6]
    refs = refs[6:]
    if not first:
        msg_in, edge_in = refs[:2]
        refs = refs[4:]
    ko, so, msg, edge = refs[:4]
    (vf, vc, vp, seg, co, kk, r, u1, u2, pz, tmp, obuf, sems) = refs[4:]
    half, chip = half_and_chip()
    span, fields = z.span, z.fields
    lane = lax.broadcasted_iota(jnp.int32, (SUB, z.lanes), 1)
    zero = jnp.zeros((SUB, z.lanes), F32)

    def east_roll(v):
        return pltpu.roll(v, 1, 1)

    def west_roll(v):
        return pltpu.roll(v, z.lanes - 1, 1)

    def rows_at(offset, count):
        return pl.ds(pl.multiple_of(offset, SUB), count)

    def window_rows(t, main, groups):
        at = tmp.at[t]
        at[rows_at(z.main * half, z.halo), :] = jnp.zeros((z.halo, z.lanes), F32)
        at[rows_at(z.halo * (1 - half), z.main), :] = main
        for g, values in enumerate(groups):
            back = z.halo - SUB * (len(groups) - g)
            at[rows_at(jnp.where(half == 0, back, z.main + SUB * g), SUB), :] = values

    def segments(t):
        return [tmp[t, pl.ds(i, SUB, stride=span), :] for i in range(span)]

    def assemble(q):
        for k in range(z.steps):
            for f in range(fields):
                tiles = [vp[q, z.group_start[k] + f * z.groups[k] + g].astype(F32) for g in range(z.groups[k])]
                for p in range(2):
                    t = (2 * f + p) % tmp.shape[0]
                    window_rows(t, vf[q, k, f, p].astype(F32), [v[SUB * p : SUB * p + SUB] for v in tiles])
                    for i, v in enumerate(segments(t)):
                        seg[k, i, f, p] = v
        for c in range(4):
            start = z.coef_start + c * z.coef_groups
            tiles = [vp[q, start + g].astype(F32) for g in range(z.coef_groups)]
            for p in range(2):
                t = (2 * c + p) % tmp.shape[0]
                window_rows(t, vc[q, c, p], [v[SUB * p : SUB * p + SUB] for v in tiles])
                for i, v in enumerate(segments(t)):
                    u1[i + 1, c, p] = v
        fill_ghosts(u1, span, 1)
        for i in range(1, span + 1):
            be, bo = u1[i, 1, 0], u1[i, 1, 1]
            south = (east_roll(bo), be)
            for p in range(2):
                a, aw, b = u1[i, 0, p], u1[i - 1, 0, p], u1[i, 1, p]
                co[i, 0, p] = 1.0 - OMEGA * (1.0 + (a + aw) + (b + south[p]))
                co[i, 1, p] = OMEGA * a
                co[i, 2, p] = OMEGA * aw
                co[i, 3, p] = OMEGA * b
                co[i, 4, p] = OMEGA * south[p]
                co[i, 5, p] = (0.5 * OMEGA) * u1[i, 2, p]
                co[i, 6, p] = (0.5 * OMEGA) * u1[i, 3, p]
        for g in range(fields):
            for f in range(fields):
                value = vc[q, 4, 0, g : g + 1, f : f + 1]
                if f == g:
                    value = value + 1.0
                kk[g * fields + f] = jnp.broadcast_to(OMEGA * value, (SUB, z.lanes))

    def sweep(src, dst, i, source):
        ga = [co[i, c, 0] for c in range(5)]
        gb = [co[i, c, 1] for c in range(5)]
        for f in range(fields):
            a, b = src[i, f, 0], src[i, f, 1]
            va = ga[0] * a + ga[1] * src[i + 1, f, 0] + ga[2] * src[i - 1, f, 0] + ga[3] * b + ga[4] * east_roll(b)
            vb = gb[0] * b + gb[1] * src[i + 1, f, 1] + gb[2] * src[i - 1, f, 1] + gb[3] * west_roll(a) + gb[4] * a
            va = va + (a if source is None else source[i, f, 0])
            vb = vb + (b if source is None else source[i, f, 1])
            dst[i, f, 0] = va
            dst[i, f, 1] = vb
            if source is not None:
                pz[i, f, 0] = co[i, 5, 0] * va
                pz[i, f, 1] = co[i, 5, 1] * vb

    def step(k):
        fill_ghosts(r, span, fields)
        for i in range(1, span + 1):
            sweep(r, u1, i, None)
        fill_ghosts(u1, span, fields)
        for i in range(1, span + 1):
            sweep(u1, u2, i, r)
        fill_ghosts(pz, span, fields)
        for i in range(1, span + 1):
            us = [[u2[i, g, p] for p in range(2)] for g in range(fields)]
            for f in range(fields):
                qa, qb = co[i, 6, 0] * us[f][0], co[i, 6, 1] * us[f][1]
                qba = jnp.where(lane == 0, zero, east_roll(qb))
                qab = jnp.where(lane == z.lanes - 1, zero, west_roll(qa))
                oa = (pz[i + 1, f, 0] - pz[i - 1, f, 0]) + (qb - qba)
                ob = (pz[i + 1, f, 1] - pz[i - 1, f, 1]) + (qab - qa)
                for g in range(fields):
                    w = kk[g * fields + f]
                    oa = oa + w * us[g][0]
                    ob = ob + w * us[g][1]
                r[i, f, 0] = oa + seg[k, i - 1, f, 0]
                r[i, f, 1] = ob + seg[k, i - 1, f, 1]

    def to_rows(t, f, p):
        for i in range(span):
            tmp[t, pl.ds(i, SUB, stride=span), :] = r[i + 1, f, p]

    @pl.when(chip == active)
    def _():
        copies = [
            pltpu.make_async_copy(kf, vf.at[1 - half], sems.at[0]),
            pltpu.make_async_copy(rf, vf.at[half], sems.at[1]),
            pltpu.make_async_copy(kc, vc.at[1 - half], sems.at[2]),
            pltpu.make_async_copy(rc, vc.at[half], sems.at[3]),
            pltpu.make_async_copy(ra, vp.at[half], sems.at[4]),
            pltpu.make_async_copy(rb, vp.at[1 - half], sems.at[5]),
        ]
        for copy in copies:
            copy.start()
        if not first:
            offset = jnp.where(half == 0, 0, z.main)
            for f in range(fields):
                for p in range(2):
                    t = (2 * f + p) % tmp.shape[0]
                    tmp[t] = jnp.zeros((z.window, z.lanes), F32)
                    for g in range(z.message // SUB):
                        v = msg_in[f, g].astype(F32)[SUB * p : SUB * p + SUB]
                        tmp[t, z.halo + SUB * g : z.halo + SUB * (g + 1), :] = v
                    for g in range(z.halo // SUB):
                        v = edge_in[f, g].astype(F32)[SUB * p : SUB * p + SUB]
                        tmp[t, rows_at(offset + SUB * g, SUB), :] = v
                    for i, v in enumerate(segments(t)):
                        r[i + 1, f, p] = v
        for copy in copies:
            copy.wait()

        def sub_window(q, carry):
            assemble(q)
            begin = 0
            if first:
                begin = jnp.where(q == 0, 1, 0)

                @pl.when(q == 0)
                def _():
                    for i in range(span):
                        for f in range(fields):
                            for p in range(2):
                                r[i + 1, f, p] = seg[z.steps - 1, i, f, p]

            def one(n, c):
                step(z.steps - 1 - n)
                return c

            lax.fori_loop(begin, z.steps, one, 0)
            place = jnp.where(q == half, 1, 0)
            for f in range(fields):
                for p in range(2):
                    t = (2 * f + p) % tmp.shape[0]
                    to_rows(t, f, p)
                    obuf[place, f, p] = tmp[t, rows_at(z.halo * (1 + half), z.own), :]
            return carry

        lax.fori_loop(0, 2, sub_window, 0)
        outs = [
            pltpu.make_async_copy(obuf.at[0], ko, sems.at[0]),
            pltpu.make_async_copy(obuf.at[1], so, sems.at[1]),
        ]
        for copy in outs:
            copy.start()
        if first:
            offset = jnp.where(half == 0, z.halo, z.main - z.halo)
            for f in range(fields):
                for p in range(2):
                    to_rows(p, f, p)
                for g in range(z.message // SUB):
                    at = z.halo + SUB * g
                    msg[f, g] = jnp.concatenate([tmp[p, at : at + SUB, :] for p in range(2)], axis=0).astype(BF16)
                for g in range(z.halo // SUB):
                    tiles = [tmp[p, rows_at(offset + SUB * g, SUB), :] for p in range(2)]
                    edge[f, g] = jnp.concatenate(tiles, axis=0).astype(BF16)
        for copy in outs:
            copy.wait()


def finish_kernel(z, keep, got, out):
    half, _ = half_and_chip()
    for f in range(z.fields):
        for p in range(2):
            a, b = keep[f, p], got[f, p]
            west = jnp.where(half == 0, a, b)
            east = jnp.where(half == 0, b, a)
            out[0, f, pl.ds(p, z.lanes, stride=2), :] = jnp.concatenate([west, east], axis=0).T


def shape(dims, dtype):
    return jax.ShapeDtypeStruct(tuple(dims), dtype)


def in_vmem(count):
    return [pl.BlockSpec(memory_space=pltpu.VMEM)] * count


def anywhere(count):
    return [pl.BlockSpec(memory_space=pl.ANY)] * count


def per_device(forcing, zonal_courant, meridional_courant, zonal_faces, meridional_faces, coupling):
    z = Sizes(forcing.shape)
    assert z.window % SUB == 0 and z.main % 16 == 0 and z.shift % 16 == 0
    tm_count, strips = lax.axis_size("tm"), lax.axis_size("space")
    chips = tm_count // 2
    params = pltpu.CompilerParams(vmem_limit_bytes=VMEM_BYTES)
    f_shape = (z.steps, z.fields, 2, z.main, z.lanes)
    c_shape = (5, 2, z.main, z.lanes)
    pay_shape = (z.payload, 2 * SUB, z.lanes)
    keep_f, send_f, keep_c, send_c, pay_a, pay_b = pl.pallas_call(
        functools.partial(prepare_kernel, z),
        out_shape=[
            shape(f_shape, BF16),
            shape(f_shape, BF16),
            shape(c_shape, F32),
            shape(c_shape, F32),
            shape(pay_shape, BF16),
            shape(pay_shape, BF16),
        ],
        in_specs=in_vmem(6),
        out_specs=in_vmem(6),
        scratch_shapes=[pltpu.VMEM((4, z.rows, z.strip), F32)],
        compiler_params=params,
        name="prepare",
    )(forcing, zonal_courant, meridional_courant, zonal_faces, meridional_faces, coupling)

    def device(tm, space):
        return tm * strips + space % strips

    everyone = [(t, s) for t in range(tm_count) for s in range(strips)]
    partner = [(t, t ^ 1) for t in range(tm_count)]
    perm_a = [(device(t, s), device(t ^ 1, s + 1 if t % 2 else s - 1)) for t, s in everyone]
    perm_b = [(device(t, s), device(t, s - 1 if t % 2 else s + 1)) for t, s in everyone]
    got_a = lax.ppermute(pay_a, ("tm", "space"), perm_a)
    got_b = lax.ppermute(pay_b, ("tm", "space"), perm_b)
    got_f = lax.ppermute(send_f, "tm", partner)
    got_c = lax.ppermute(send_c, "tm", partner)
    half_shape = (z.fields, 2, z.own, z.lanes)
    msg_shape = (z.fields, z.message // SUB, 2 * SUB, z.lanes)
    edge_shape = (z.fields, z.halo // SUB, 2 * SUB, z.lanes)
    scratch = [
        pltpu.VMEM((2,) + f_shape, BF16),
        pltpu.VMEM((2,) + c_shape, F32),
        pltpu.VMEM((2,) + pay_shape, BF16),
        pltpu.VMEM((z.steps, z.span, z.fields, 2, SUB, z.lanes), F32),
        pltpu.VMEM((z.span + 2, 8, 2, SUB, z.lanes), F32),
        pltpu.VMEM((z.fields * z.fields, SUB, z.lanes), F32),
    ]
    scratch += [pltpu.VMEM((z.span + 2, z.fields, 2, SUB, z.lanes), F32)] * 4
    scratch += [
        pltpu.VMEM((4, z.window, z.lanes), F32),
        pltpu.VMEM((2,) + half_shape, F32),
        pltpu.SemaphoreType.DMA((6,)),
    ]
    carried = ()
    for turn in range(chips):
        first = turn == 0
        active = chips - 1 - turn
        kept, sent, msg, edge = pl.pallas_call(
            functools.partial(chain_kernel, z, first, active),
            out_shape=[
                shape(half_shape, F32),
                shape(half_shape, F32),
                shape(msg_shape, BF16),
                shape(edge_shape, BF16),
            ],
            in_specs=anywhere(6) + ([] if first else in_vmem(2) + anywhere(2)),
            out_specs=anywhere(2) + in_vmem(2),
            input_output_aliases={} if first else {8: 0, 9: 1},
            scratch_shapes=scratch,
            compiler_params=params,
            name="chain",
        )(keep_f, got_f, keep_c, got_c, got_a, got_b, *carried)
        if turn + 1 < chips:
            down = [(device(t, s), device((t - 2) % tm_count, s)) for t, s in everyone]
            across = [
                (device(t, s), device(((t ^ 1) - 2) % tm_count, s + 1 if t % 2 else s - 1)) for t, s in everyone
            ]
            msg = lax.ppermute(msg, ("tm", "space"), down)
            edge = lax.ppermute(edge, ("tm", "space"), across)
            carried = (msg, edge, kept, sent)
    got = lax.ppermute(sent, "tm", partner)
    return pl.pallas_call(
        functools.partial(finish_kernel, z),
        out_shape=shape((1, z.fields, z.rows, z.strip), F32),
        in_specs=in_vmem(2),
        out_specs=pl.BlockSpec(memory_space=pltpu.VMEM),
        compiler_params=params,
        name="finish",
    )(kept, got)


def solution(mesh):
    return jax.shard_map(
        per_device,
        mesh=mesh,
        in_specs=(
            P("tm", None, None, None, "space"),
            P("tm", None, "space"),
            P("tm", None, "space"),
            P("tm", None, "space"),
            P("tm", None, "space"),
            P("tm", None, None),
        ),
        out_specs=P("tm", None, None, "space"),
        check_vma=False,
    )
```

```python
import functools

import jax
import jax.numpy as jnp
from jax import lax
from jax.experimental import pallas as pl
from jax.experimental.pallas import tpu as pltpu
from jax.sharding import PartitionSpec as P

SWEEPS = 2
OMEGA = 0.4
SUB = 8
REACH = SWEEPS + 1
VMEM_BYTES = 20 * 2**20
F32 = jnp.float32
BF16 = jnp.bfloat16


class Sizes:
    def __init__(self, forcing_shape):
        _, self.steps, self.fields, self.rows, self.strip = forcing_shape
        self.lanes = self.rows // 2
        self.halo = 2 * REACH * self.steps
        self.main = self.strip // 2 + 2 * self.halo
        self.window = self.main + self.halo
        self.span = self.window // SUB
        self.shift = self.strip - self.main
        self.own = self.strip // 2
        self.groups = [-(-REACH * (self.steps + k) // SUB) for k in range(self.steps)]
        self.group_start = [self.fields * sum(self.groups[:k]) for k in range(self.steps)]
        self.coef_start = self.fields * sum(self.groups)
        self.coef_groups = self.halo // SUB
        self.payload = self.coef_start + 4 * self.coef_groups
        self.message = self.own + self.halo


def half_and_chip():
    tm = lax.axis_index("tm")
    return lax.rem(tm, 2), tm // 2


def prepare_kernel(z, fo_in, zc, mc, zf, mf, cp_in, keep_f, send_f, keep_c, send_c, pay_a, pay_b, fo, co, cp, buf, sems):
    half, _ = half_and_chip()
    left = half == 0
    row = lax.broadcasted_iota(jnp.int32, (z.rows, z.strip), 0)
    coef_copies = [
        pltpu.make_async_copy(ref.at[0], co.at[c], sems.at[c]) for c, ref in enumerate((zf, mf, zc, mc))
    ]
    forcing_copies = [pltpu.make_async_copy(fo_in.at[0, k], fo.at[k], sems.at[5 + k]) for k in range(z.steps)]
    mixing_copy = pltpu.make_async_copy(cp_in, cp, sems.at[4])
    for copy in coef_copies + [mixing_copy] + forcing_copies:
        copy.start()

    def columns(values, slot):
        buf[slot] = values
        return [buf[slot, pl.ds(p, z.lanes, stride=2), :].T for p in range(2)]

    def split(both, groups, start, keep, send):
        for p in range(2):
            low, high = both[p][: z.main], both[p][z.shift :]
            keep[p] = jnp.where(left, low, high).astype(keep.dtype)
            send[p] = jnp.where(left, high, low).astype(send.dtype)
        for g in range(groups):
            lo, hi = SUB * g, z.strip - SUB * (groups - g)
            west = jnp.concatenate([both[p][lo : lo + SUB] for p in range(2)], axis=0)
            east = jnp.concatenate([both[p][hi : hi + SUB] for p in range(2)], axis=0)
            pay_a[start + g] = jnp.where(left, west, east).astype(BF16)
            pay_b[start + g] = jnp.where(left, east, west).astype(BF16)

    slots = buf.shape[0]
    count = 0
    for c in range(4):
        coef_copies[c].wait()
        values = co[c]
        if c == 1:
            values = jnp.where(row < z.rows - 1, values, jnp.zeros_like(values))
        both = columns(values, count % slots)
        split(both, z.coef_groups, z.coef_start + c * z.coef_groups, keep_c.at[c], send_c.at[c])
        count += 1
    mixing_copy.wait()
    for ref in (keep_c, send_c):
        for g in range(z.fields):
            ref[4, 0, g : g + 1, : z.fields] = cp[g]
    for k in range(z.steps):
        forcing_copies[k].wait()
        for f in range(z.fields):
            both = columns(fo[k, f].astype(F32), count % slots)
            split(both, z.groups[k], z.group_start[k] + f * z.groups[k], keep_f.at[k, f], send_f.at[k, f])
            count += 1


def fill_ghosts(ref, span, count):
    for n in range(count):
        for p in range(2):
            ref[0, n, p] = pltpu.roll(ref[span, n, p], 1, 0)
            ref[span + 1, n, p] = pltpu.roll(ref[1, n, p], SUB - 1, 0)


class Band:
    def __init__(self, z, scratch):
        self.z = z
        self.r, self.u1, self.u2, self.pz, self.co, self.kk = scratch
        self.lane = lax.broadcasted_iota(jnp.int32, (SUB, z.lanes), 1)

    def east(self, v):
        return pltpu.roll(v, 1, 1)

    def west(self, v):
        return pltpu.roll(v, self.z.lanes - 1, 1)

    def set_operators(self, rows_c, q, offset, span):
        z, u1, co = self.z, self.u1, self.co
        for c in range(4):
            for p in range(2):
                for i in range(span):
                    u1[i + 1, c, p] = rows_c[q, c, p, pl.ds(offset + i, SUB, stride=span), :]
        fill_ghosts(u1, span, 1)
        for i in range(1, span + 1):
            be, bo = u1[i, 1, 0], u1[i, 1, 1]
            south = (self.east(bo), be)
            for p in range(2):
                a, aw, b = u1[i, 0, p], u1[i - 1, 0, p], u1[i, 1, p]
                co[i, 0, p] = 1.0 - OMEGA * (1.0 + (a + aw) + (b + south[p]))
                co[i, 1, p] = OMEGA * a
                co[i, 2, p] = OMEGA * aw
                co[i, 3, p] = OMEGA * b
                co[i, 4, p] = OMEGA * south[p]
                co[i, 5, p] = (0.5 * OMEGA) * u1[i, 2, p]
                co[i, 6, p] = (0.5 * OMEGA) * u1[i, 3, p]
        for g in range(z.fields):
            for f in range(z.fields):
                value = rows_c[q, 4, 0, g : g + 1, f : f + 1]
                if f == g:
                    value = value + 1.0
                self.kk[g * z.fields + f] = jnp.broadcast_to(OMEGA * value, (SUB, z.lanes))

    def load(self, at, offset, span):
        for i in range(span):
            for f in range(self.z.fields):
                for p in range(2):
                    self.r[i + 1, f, p] = at[f, p, pl.ds(offset + i, SUB, stride=span), :]

    def store(self, at, span):
        for i in range(span):
            for f in range(self.z.fields):
                for p in range(2):
                    at[f, p, pl.ds(i, SUB, stride=span), :] = self.r[i + 1, f, p]

    def sweep(self, src, dst, i, source):
        co = self.co
        ga = [co[i, c, 0] for c in range(5)]
        gb = [co[i, c, 1] for c in range(5)]
        for f in range(self.z.fields):
            a, b = src[i, f, 0], src[i, f, 1]
            va = ga[0] * a + ga[1] * src[i + 1, f, 0] + ga[2] * src[i - 1, f, 0] + ga[3] * b + ga[4] * self.east(b)
            vb = gb[0] * b + gb[1] * src[i + 1, f, 1] + gb[2] * src[i - 1, f, 1] + gb[3] * self.west(a) + gb[4] * a
            va = va + (a if source is None else source[i, f, 0])
            vb = vb + (b if source is None else source[i, f, 1])
            dst[i, f, 0] = va
            dst[i, f, 1] = vb
            if source is not None:
                self.pz[i, f, 0] = co[i, 5, 0] * va
                self.pz[i, f, 1] = co[i, 5, 1] * vb

    def step(self, forcing, offset, span):
        z, r, u1, u2, pz, co, kk = self.z, self.r, self.u1, self.u2, self.pz, self.co, self.kk
        zero = jnp.zeros((SUB, z.lanes), F32)
        fill_ghosts(r, span, z.fields)
        for i in range(1, span + 1):
            self.sweep(r, u1, i, None)
        fill_ghosts(u1, span, z.fields)
        for i in range(1, span + 1):
            self.sweep(u1, u2, i, r)
        fill_ghosts(pz, span, z.fields)
        for i in range(1, span + 1):
            us = [[u2[i, g, p] for p in range(2)] for g in range(z.fields)]
            for f in range(z.fields):
                qa, qb = co[i, 6, 0] * us[f][0], co[i, 6, 1] * us[f][1]
                qba = jnp.where(self.lane == 0, zero, self.east(qb))
                qab = jnp.where(self.lane == z.lanes - 1, zero, self.west(qa))
                oa = (pz[i + 1, f, 0] - pz[i - 1, f, 0]) + (qb - qba)
                ob = (pz[i + 1, f, 1] - pz[i - 1, f, 1]) + (qab - qa)
                for g in range(z.fields):
                    w = kk[g * z.fields + f]
                    oa = oa + w * us[g][0]
                    ob = ob + w * us[g][1]
                rows = pl.ds(offset + i - 1, SUB, stride=span)
                r[i, f, 0] = oa + forcing[f, 0, rows, :]
                r[i, f, 1] = ob + forcing[f, 1, rows, :]

    def steps(self, rows_f, q, begin, offset, span):
        last = self.z.steps - 1

        def one(n, carry):
            self.step(rows_f.at[q, last - n], offset, span)
            return carry

        lax.fori_loop(begin, last + 1, one, 0)


def aligned(offset, count):
    return pl.ds(pl.multiple_of(offset, SUB), count)


def inner_kernel(z, active, kf, rf, kc, rc, rows_f, rows_c, inner, *scratch):
    half, chip = half_and_chip()
    main_at = z.halo * (1 - half)
    blank = jnp.zeros((z.halo, z.lanes), F32)

    def put(ref, values):
        ref[aligned(main_at, z.main), :] = values.astype(F32)
        ref[aligned(z.main * half, z.halo), :] = blank

    for q, forcing, coefs in ((1 - half, kf, kc), (half, rf, rc)):
        for c in range(4):
            for p in range(2):
                put(rows_c.at[q, c, p], coefs[c, p])
        rows_c[q, 4, 0, :SUB, :] = coefs[4, 0, :SUB, :]
        for k in range(z.steps):
            for f in range(z.fields):
                for p in range(2):
                    put(rows_f.at[q, k, f, p], forcing[k, f, p])

    @pl.when(chip == active)
    def _():
        band = Band(z, scratch)
        span = z.main // SUB
        band.load(rows_f.at[0, z.steps - 1], main_at, span)

        def sub_window(q, carry):
            band.set_operators(rows_c, q, main_at, span)
            band.steps(rows_f, q, 1 - q, main_at, span)
            band.store(inner.at[q], span)
            return carry

        lax.fori_loop(0, 2, sub_window, 0)


def tile_of(ref, f, at):
    return jnp.concatenate([ref[f, p, at, :] for p in range(2)], axis=0).astype(BF16)


def rim_kernel(z, active, ra, rb, inner, rows_f_in, rows_c_in, rows_f, rows_c, ko, so, msg, edge, obuf, tmp, *scratch):
    half, chip = half_and_chip()
    for q, pay in ((half, ra), (1 - half, rb)):

        def put(ref, start, groups):
            for g in range(groups):
                tile = pay[start + g].astype(F32)
                at = jnp.where(half == 0, z.halo - SUB * (groups - g), z.main + SUB * g)
                for p in range(2):
                    ref[p, aligned(at, SUB), :] = tile[SUB * p : SUB * (p + 1)]

        for c in range(4):
            put(rows_c.at[q, c], z.coef_start + c * z.coef_groups, z.coef_groups)
        for k in range(z.steps):
            for f in range(z.fields):
                put(rows_f.at[q, k, f], z.group_start[k] + f * z.groups[k], z.groups[k])

    @pl.when(chip == active)
    def _():
        band = Band(z, scratch)
        span = 3 * z.halo // SUB
        offset = (z.window - 3 * z.halo) * half
        rim = slice(z.halo, 2 * z.halo)
        band.load(rows_f.at[0, z.steps - 1], offset, span)

        def sub_window(q, carry):
            band.set_operators(rows_c, q, offset, span)
            band.steps(rows_f, q, 1 - q, offset, span)
            band.store(tmp, span)
            place = jnp.where(q == half, 1, 0)
            for f in range(z.fields):
                for p in range(2):
                    obuf[place, f, p] = inner[q, f, p, aligned((z.main - z.own) * half, z.own), :]
                    obuf[place, f, p, aligned((z.own - z.halo) * half, z.halo), :] = tmp[f, p, rim, :]
            return carry

        lax.fori_loop(0, 2, sub_window, 0)
        ko[...] = obuf[0]
        so[...] = obuf[1]
        last = inner.at[1]
        for f in range(z.fields):
            for g in range(z.message // SUB):
                msg[f, g] = tile_of(last, f, aligned(z.halo * half + SUB * g, SUB))
            for g in range(z.halo // SUB):
                tile = tile_of(tmp, f, slice(z.halo + SUB * g, z.halo + SUB * (g + 1)))
                edge[f, g] = tile
                msg[f, (z.message - z.halo) // SUB * half + g] = tile


def late_kernel(z, active, msg, edge, rows_f, rows_c, ko_in, so_in, ko, so, obuf, tmp, *scratch):
    half, chip = half_and_chip()

    @pl.when(chip == active)
    def _():
        band = Band(z, scratch)
        wide, narrow = z.main // SUB, (z.main - z.halo) // SUB
        inset = z.halo // 2
        offset = z.halo * half

        def put(ref, f, g, at):
            tile = ref[f, g].astype(F32)
            for p in range(2):
                tmp[f, p, aligned(at, SUB), :] = tile[SUB * p : SUB * (p + 1)]

        for f in range(z.fields):
            for g in range(z.message // SUB):
                put(msg, f, g, z.halo * (1 - half) + SUB * g)
            for g in range(z.halo // SUB):
                put(edge, f, g, z.message * half + SUB * g)
        band.load(tmp, 0, wide)
        band.set_operators(rows_c, 0, offset, wide)
        band.steps(rows_f, 0, 0, offset, wide)
        band.store(tmp, wide)
        for f in range(z.fields):
            for p in range(2):
                obuf[1 - half, f, p] = tmp[f, p, z.halo : z.halo + z.own, :]
        band.load(tmp, inset, narrow)
        band.set_operators(rows_c, 1, offset + inset, narrow)
        band.steps(rows_f, 1, 0, offset + inset, narrow)
        band.store(tmp, narrow)
        for f in range(z.fields):
            for p in range(2):
                obuf[half, f, p] = tmp[f, p, inset : inset + z.own, :]
        ko[...] = obuf[0]
        so[...] = obuf[1]


def finish_kernel(z, keep, got, out):
    half, _ = half_and_chip()
    for f in range(z.fields):
        for p in range(2):
            a, b = keep[f, p], got[f, p]
            west = jnp.where(half == 0, a, b)
            east = jnp.where(half == 0, b, a)
            out[0, f, pl.ds(p, z.lanes, stride=2), :] = jnp.concatenate([west, east], axis=0).T


def shape(dims, dtype):
    return jax.ShapeDtypeStruct(tuple(dims), dtype)


def in_vmem(count):
    return [pl.BlockSpec(memory_space=pltpu.VMEM)] * count


def in_hbm(count):
    return [pl.BlockSpec(memory_space=pltpu.HBM)] * count


def per_device(forcing, zonal_courant, meridional_courant, zonal_faces, meridional_faces, coupling):
    z = Sizes(forcing.shape)
    tm_count, strips = lax.axis_size("tm"), lax.axis_size("space")
    assert tm_count == 4 and z.main % 16 == 0 and z.shift % 16 == 0
    params = pltpu.CompilerParams(vmem_limit_bytes=VMEM_BYTES)
    f_shape = (z.steps, z.fields, 2, z.main, z.lanes)
    c_shape = (5, 2, z.main, z.lanes)
    pay_shape = (z.payload, 2 * SUB, z.lanes)
    keep_f, send_f, keep_c, send_c, pay_a, pay_b = pl.pallas_call(
        functools.partial(prepare_kernel, z),
        out_shape=[
            shape(f_shape, BF16),
            shape(f_shape, BF16),
            shape(c_shape, F32),
            shape(c_shape, F32),
            shape(pay_shape, BF16),
            shape(pay_shape, BF16),
        ],
        in_specs=in_hbm(6),
        out_specs=in_vmem(6),
        scratch_shapes=[
            pltpu.VMEM(forcing.shape[1:], BF16),
            pltpu.VMEM((4, z.rows, z.strip), F32),
            pltpu.VMEM((z.fields, 1, z.fields), F32),
            pltpu.VMEM((4, z.rows, z.strip), F32),
            pltpu.SemaphoreType.DMA((5 + z.steps,)),
        ],
        compiler_params=params,
        name="prepare",
    )(
        *[
            pltpu.with_memory_space_constraint(array, pltpu.HBM)
            for array in (
                forcing,
                zonal_courant,
                meridional_courant,
                zonal_faces,
                meridional_faces,
                jnp.swapaxes(coupling, 0, 1),
            )
        ]
    )

    def device(tm, space):
        return tm * strips + space % strips

    everyone = [(t, s) for t in range(tm_count) for s in range(strips)]
    partner = [(t, t ^ 1) for t in range(tm_count)]
    perm_a = [(device(t, s), device(t ^ 1, s + 1 if t % 2 else s - 1)) for t, s in everyone]
    perm_b = [(device(t, s), device(t, s - 1 if t % 2 else s + 1)) for t, s in everyone]
    got_f = lax.ppermute(send_f, "tm", partner)
    got_c = lax.ppermute(send_c, "tm", partner)
    got_a = lax.ppermute(pay_a, ("tm", "space"), perm_a)
    got_b = lax.ppermute(pay_b, ("tm", "space"), perm_b)

    def band_scratch(span):
        state = pltpu.VMEM((span + 2, z.fields, 2, SUB, z.lanes), F32)
        return [state] * 4 + [
            pltpu.VMEM((span + 2, 7, 2, SUB, z.lanes), F32),
            pltpu.VMEM((z.fields * z.fields, SUB, z.lanes), F32),
        ]

    rows_f_shape = shape((2, z.steps, z.fields, 2, z.window, z.lanes), F32)
    rows_c_shape = shape((2, 5, 2, z.window, z.lanes), F32)
    half_dims = (z.fields, 2, z.own, z.lanes)
    rows_f, rows_c, inner = pl.pallas_call(
        functools.partial(inner_kernel, z, 1),
        out_shape=[rows_f_shape, rows_c_shape, shape((2, z.fields, 2, z.main, z.lanes), F32)],
        in_specs=in_vmem(4),
        out_specs=in_vmem(3),
        scratch_shapes=band_scratch(z.main // SUB),
        compiler_params=params,
        cost_estimate=pl.CostEstimate(flops=10**9, bytes_accessed=2 * 10**7, transcendentals=0),
        name="inner",
    )(keep_f, got_f, keep_c, got_c)
    rows_f, rows_c, kept, sent, msg, edge = pl.pallas_call(
        functools.partial(rim_kernel, z, 1),
        out_shape=[
            rows_f_shape,
            rows_c_shape,
            shape(half_dims, F32),
            shape(half_dims, F32),
            shape((z.fields, z.message // SUB, 2 * SUB, z.lanes), BF16),
            shape((z.fields, z.halo // SUB, 2 * SUB, z.lanes), BF16),
        ],
        in_specs=in_vmem(5),
        out_specs=in_vmem(6),
        input_output_aliases={3: 0, 4: 1},
        scratch_shapes=[
            pltpu.VMEM((2,) + half_dims, F32),
            pltpu.VMEM((z.fields, 2, 3 * z.halo, z.lanes), F32),
        ]
        + band_scratch(3 * z.halo // SUB),
        compiler_params=params,
        name="rim",
    )(got_a, got_b, inner, rows_f, rows_c)
    down = [(device(t, s), device((t - 2) % tm_count, s)) for t, s in everyone]
    across = [(device(t, s), device(((t ^ 1) - 2) % tm_count, s + 1 if t % 2 else s - 1)) for t, s in everyone]
    msg = lax.ppermute(msg, ("tm", "space"), down)
    edge = lax.ppermute(edge, ("tm", "space"), across)
    kept, sent = pl.pallas_call(
        functools.partial(late_kernel, z, 0),
        out_shape=[shape(half_dims, F32), shape(half_dims, F32)],
        in_specs=in_vmem(6),
        out_specs=in_vmem(2),
        input_output_aliases={4: 0, 5: 1},
        scratch_shapes=[
            pltpu.VMEM((2,) + half_dims, F32),
            pltpu.VMEM((z.fields, 2, z.main, z.lanes), F32),
        ]
        + band_scratch(z.main // SUB),
        compiler_params=params,
        name="late",
    )(msg, edge, rows_f, rows_c, kept, sent)
    got = lax.ppermute(sent, "tm", partner)
    return pl.pallas_call(
        functools.partial(finish_kernel, z),
        out_shape=shape((1, z.fields, z.rows, z.strip), F32),
        in_specs=in_vmem(2),
        out_specs=pl.BlockSpec(memory_space=pltpu.VMEM),
        compiler_params=params,
        name="finish",
    )(kept, got)


def solution(mesh):
    return jax.shard_map(
        per_device,
        mesh=mesh,
        in_specs=(
            P("tm", None, None, None, "space"),
            P("tm", None, "space"),
            P("tm", None, "space"),
            P("tm", None, "space"),
            P("tm", None, "space"),
            P("tm", None, None),
        ),
        out_specs=P("tm", None, None, "space"),
        check_vma=False,
    )
```

```python
import functools

import jax
import jax.numpy as jnp
from jax import lax
from jax.experimental import pallas as pl
from jax.experimental.pallas import tpu as pltpu
from jax.sharding import PartitionSpec as P

SWEEPS = 2
OMEGA = 0.4
SUB = 8
REACH = SWEEPS + 1
VMEM_BYTES = 20 * 2**20
F32 = jnp.float32
BF16 = jnp.bfloat16


class Sizes:
    def __init__(self, forcing_shape):
        _, self.steps, self.fields, self.rows, self.strip = forcing_shape
        self.lanes = self.rows // 2
        self.halo = 2 * REACH * self.steps
        self.main = self.strip // 2 + 2 * self.halo
        self.window = self.main + self.halo
        self.span = self.window // SUB
        self.shift = self.strip - self.main
        self.own = self.strip // 2
        self.groups = [-(-REACH * (self.steps + k) // SUB) for k in range(self.steps)]
        self.group_start = [self.fields * sum(self.groups[:k]) for k in range(self.steps)]
        self.coef_start = self.fields * sum(self.groups)
        self.coef_groups = self.halo // SUB
        self.payload = self.coef_start + 4 * self.coef_groups
        self.message = self.own + self.halo
        self.core = self.message - self.halo
        self.wide, self.narrow = self.main // SUB, (self.main - self.halo) // SUB
        self.inset = self.halo // 2


def half_and_chip():
    tm = lax.axis_index("tm")
    return lax.rem(tm, 2), tm // 2


def prepare_kernel(z, fo_in, zc, mc, zf, mf, cp_in, keep_f, send_f, keep_c, send_c, pay_a, pay_b, fo, co, cp, buf, sems):
    half, _ = half_and_chip()
    left = half == 0
    row = lax.broadcasted_iota(jnp.int32, (z.rows, z.strip), 0)
    coef_copies = [
        pltpu.make_async_copy(ref.at[0], co.at[c], sems.at[c]) for c, ref in enumerate((zf, mf, zc, mc))
    ]
    forcing_copies = [pltpu.make_async_copy(fo_in.at[0, k], fo.at[k], sems.at[5 + k]) for k in range(z.steps)]
    mixing_copy = pltpu.make_async_copy(cp_in, cp, sems.at[4])
    for copy in coef_copies + [mixing_copy] + forcing_copies:
        copy.start()

    def columns(values, slot):
        buf[slot] = values
        return [buf[slot, pl.ds(p, z.lanes, stride=2), :].T for p in range(2)]

    def split(both, groups, start, keep, send):
        for p in range(2):
            low, high = both[p][: z.main], both[p][z.shift :]
            keep[p] = jnp.where(left, low, high).astype(keep.dtype)
            send[p] = jnp.where(left, high, low).astype(send.dtype)
        for g in range(groups):
            lo, hi = SUB * g, z.strip - SUB * (groups - g)
            west = jnp.concatenate([both[p][lo : lo + SUB] for p in range(2)], axis=0)
            east = jnp.concatenate([both[p][hi : hi + SUB] for p in range(2)], axis=0)
            pay_a[start + g] = jnp.where(left, west, east).astype(BF16)
            pay_b[start + g] = jnp.where(left, east, west).astype(BF16)

    slots = buf.shape[0]
    count = 0
    for c in range(4):
        coef_copies[c].wait()
        values = co[c]
        if c == 1:
            values = jnp.where(row < z.rows - 1, values, jnp.zeros_like(values))
        both = columns(values, count % slots)
        split(both, z.coef_groups, z.coef_start + c * z.coef_groups, keep_c.at[c], send_c.at[c])
        count += 1
    mixing_copy.wait()
    for ref in (keep_c, send_c):
        for g in range(z.fields):
            ref[4, 0, g : g + 1, : z.fields] = cp[g]
    for k in range(z.steps):
        forcing_copies[k].wait()
        for f in range(z.fields):
            both = columns(fo[k, f].astype(F32), count % slots)
            split(both, z.groups[k], z.group_start[k] + f * z.groups[k], keep_f.at[k, f], send_f.at[k, f])
            count += 1


def fill_ghosts(ref, span, count):
    for n in range(count):
        for p in range(2):
            ref[0, n, p] = pltpu.roll(ref[span, n, p], 1, 0)
            ref[span + 1, n, p] = pltpu.roll(ref[1, n, p], SUB - 1, 0)


class Band:
    def __init__(self, z, scratch):
        self.z = z
        self.r, self.u1, self.u2, self.pz, self.co, self.kk = scratch
        self.lane = lax.broadcasted_iota(jnp.int32, (SUB, z.lanes), 1)

    def east(self, v):
        return pltpu.roll(v, 1, 1)

    def west(self, v):
        return pltpu.roll(v, self.z.lanes - 1, 1)

    def set_operators(self, rows_c, q, offset, span):
        z, u1, co = self.z, self.u1, self.co
        for c in range(4):
            for p in range(2):
                for i in range(span):
                    u1[i + 1, c, p] = rows_c[q, c, p, pl.ds(offset + i, SUB, stride=span), :]
        fill_ghosts(u1, span, 1)
        for i in range(1, span + 1):
            be, bo = u1[i, 1, 0], u1[i, 1, 1]
            south = (self.east(bo), be)
            for p in range(2):
                a, aw, b = u1[i, 0, p], u1[i - 1, 0, p], u1[i, 1, p]
                centre = 1.0 - OMEGA * (1.0 + (a + aw) + (b + south[p]))
                co[i, 0, p] = centre
                co[i, 7, p] = 1.0 + centre
                co[i, 1, p] = OMEGA * a
                co[i, 2, p] = OMEGA * aw
                co[i, 3, p] = OMEGA * b
                co[i, 4, p] = OMEGA * south[p]
                co[i, 5, p] = (0.5 * OMEGA) * u1[i, 2, p]
                co[i, 6, p] = (0.5 * OMEGA) * u1[i, 3, p]
        for g in range(z.fields):
            for f in range(z.fields):
                value = rows_c[q, 4, 0, g : g + 1, f : f + 1]
                if f == g:
                    value = value + 1.0
                self.kk[g * z.fields + f] = jnp.broadcast_to(OMEGA * value, (SUB, z.lanes))

    def load(self, at, offset, span):
        for i in range(span):
            for f in range(self.z.fields):
                for p in range(2):
                    self.r[i + 1, f, p] = at[f, p, pl.ds(offset + i, SUB, stride=span), :]

    def store(self, at, span):
        for i in range(span):
            for f in range(self.z.fields):
                for p in range(2):
                    at[f, p, pl.ds(i, SUB, stride=span), :] = self.r[i + 1, f, p]

    def sweep(self, src, dst, i, source):
        co = self.co
        first = 7 if source is None else 0
        ga = [co[i, c, 0] for c in (first, 1, 2, 3, 4)]
        gb = [co[i, c, 1] for c in (first, 1, 2, 3, 4)]
        for f in range(self.z.fields):
            a, b = src[i, f, 0], src[i, f, 1]
            va = ga[0] * a + ga[1] * src[i + 1, f, 0] + ga[2] * src[i - 1, f, 0] + ga[3] * b + ga[4] * self.east(b)
            vb = gb[0] * b + gb[1] * src[i + 1, f, 1] + gb[2] * src[i - 1, f, 1] + gb[3] * self.west(a) + gb[4] * a
            if source is not None:
                va = va + source[i, f, 0]
                vb = vb + source[i, f, 1]
                self.pz[i, f, 0] = co[i, 5, 0] * va
                self.pz[i, f, 1] = co[i, 5, 1] * vb
            dst[i, f, 0] = va
            dst[i, f, 1] = vb

    def step(self, forcing, offset, span):
        z, r, u1, u2, pz, co, kk = self.z, self.r, self.u1, self.u2, self.pz, self.co, self.kk
        zero = jnp.zeros((SUB, z.lanes), F32)
        fill_ghosts(r, span, z.fields)
        for i in range(1, span + 1):
            self.sweep(r, u1, i, None)
        fill_ghosts(u1, span, z.fields)
        for i in range(1, span + 1):
            self.sweep(u1, u2, i, r)
        fill_ghosts(pz, span, z.fields)
        for i in range(1, span + 1):
            us = [[u2[i, g, p] for p in range(2)] for g in range(z.fields)]
            for f in range(z.fields):
                qa, qb = co[i, 6, 0] * us[f][0], co[i, 6, 1] * us[f][1]
                qba = jnp.where(self.lane == 0, zero, self.east(qb))
                qab = jnp.where(self.lane == z.lanes - 1, zero, self.west(qa))
                oa = (pz[i + 1, f, 0] - pz[i - 1, f, 0]) + (qb - qba)
                ob = (pz[i + 1, f, 1] - pz[i - 1, f, 1]) + (qab - qa)
                for g in range(z.fields):
                    w = kk[g * z.fields + f]
                    oa = oa + w * us[g][0]
                    ob = ob + w * us[g][1]
                rows = pl.ds(offset + i - 1, SUB, stride=span)
                r[i, f, 0] = oa + forcing[f, 0, rows, :]
                r[i, f, 1] = ob + forcing[f, 1, rows, :]

    def steps(self, rows_f, q, begin, offset, span):
        last = self.z.steps - 1

        def one(n, carry):
            self.step(rows_f.at[q, last - n], offset, span)
            return carry

        lax.fori_loop(begin, last + 1, one, 0)


def aligned(offset, count):
    return pl.ds(pl.multiple_of(offset, SUB), count)


def tile_of(ref, f, at):
    return jnp.concatenate([ref[f, p, at, :] for p in range(2)], axis=0).astype(BF16)


def inner_kernel(z, active, kf, rf, kc, rc, rows_f, rows_c, inner, core, *scratch):
    half, chip = half_and_chip()
    main_at = z.halo * (1 - half)
    blank = jnp.zeros((z.halo, z.lanes), F32)

    def put(ref, values):
        ref[aligned(main_at, z.main), :] = values.astype(F32)
        ref[aligned(z.main * half, z.halo), :] = blank

    for q, forcing, coefs in ((1 - half, kf, kc), (half, rf, rc)):
        for c in range(4):
            for p in range(2):
                put(rows_c.at[q, c, p], coefs[c, p])
        rows_c[q, 4, 0, :SUB, :] = coefs[4, 0, :SUB, :]
        for k in range(z.steps):
            for f in range(z.fields):
                for p in range(2):
                    put(rows_f.at[q, k, f, p], forcing[k, f, p])

    @pl.when(chip == active)
    def _():
        band = Band(z, scratch)
        span = z.main // SUB
        band.load(rows_f.at[0, z.steps - 1], main_at, span)

        def sub_window(q, carry):
            band.set_operators(rows_c, q, main_at, span)
            band.steps(rows_f, q, 1 - q, main_at, span)
            band.store(inner.at[q], span)
            return carry

        lax.fori_loop(0, 2, sub_window, 0)
        for f in range(z.fields):
            for g in range(z.core // SUB):
                core[f, g] = tile_of(inner.at[1], f, slice(z.halo + SUB * g, z.halo + SUB * (g + 1)))


def rim_kernel(z, active, ra, rb, inner, rows_f_in, rows_c_in, rows_f, rows_c, ko, so, edge, *refs):
    late_operators, (obuf, tmp), scratch = refs[:4], refs[4:6], refs[6:]
    half, chip = half_and_chip()
    for q, pay in ((half, ra), (1 - half, rb)):

        def put(ref, start, groups):
            for g in range(groups):
                tile = pay[start + g].astype(F32)
                at = jnp.where(half == 0, z.halo - SUB * (groups - g), z.main + SUB * g)
                for p in range(2):
                    ref[p, aligned(at, SUB), :] = tile[SUB * p : SUB * (p + 1)]

        for c in range(4):
            put(rows_c.at[q, c], z.coef_start + c * z.coef_groups, z.coef_groups)
        for k in range(z.steps):
            for f in range(z.fields):
                put(rows_f.at[q, k, f], z.group_start[k] + f * z.groups[k], z.groups[k])

    @pl.when(chip != active)
    def _():
        for q, span, offset in ((0, z.wide, z.halo * half), (1, z.narrow, z.halo * half + z.inset)):
            band = Band(z, scratch[:4] + late_operators[2 * q : 2 * q + 2])
            band.set_operators(rows_c, q, offset, span)

    @pl.when(chip == active)
    def _():
        band = Band(z, scratch)
        span = 3 * z.halo // SUB
        offset = (z.window - 3 * z.halo) * half
        rim = slice(z.halo, 2 * z.halo)
        band.load(rows_f.at[0, z.steps - 1], offset, span)

        def sub_window(q, carry):
            band.set_operators(rows_c, q, offset, span)
            band.steps(rows_f, q, 1 - q, offset, span)
            band.store(tmp, span)

            @pl.when(q == 1)
            def _():
                for f in range(z.fields):
                    for g in range(z.halo // SUB):
                        edge[f, g] = tile_of(tmp, f, slice(z.halo + SUB * g, z.halo + SUB * (g + 1)))

            place = jnp.where(q == half, 1, 0)
            for f in range(z.fields):
                for p in range(2):
                    obuf[place, f, p] = inner[q, f, p, aligned((z.main - z.own) * half, z.own), :]
                    obuf[place, f, p, aligned((z.own - z.halo) * half, z.halo), :] = tmp[f, p, rim, :]
            return carry

        lax.fori_loop(0, 2, sub_window, 0)
        ko[...] = obuf[0]
        so[...] = obuf[1]


def late_kernel(z, active, core, near, far, rows_f, ko_in, so_in, co0, kk0, co1, kk1, ko, so, obuf, tmp, *scratch):
    half, chip = half_and_chip()

    @pl.when(chip == active)
    def _():
        offset = z.halo * half

        def put(ref, at):
            for f in range(z.fields):
                for g in range(ref.shape[1]):
                    tile = ref[f, g].astype(F32)
                    for p in range(2):
                        tmp[f, p, aligned(at + SUB * g, SUB), :] = tile[SUB * p : SUB * (p + 1)]

        put(core, 2 * z.halo * (1 - half))
        put(near, z.halo + (z.core - z.halo) * half)
        put(far, z.message * half)
        band = Band(z, scratch + (co0, kk0))
        band.load(tmp, 0, z.wide)
        band.steps(rows_f, 0, 0, offset, z.wide)
        band.store(tmp, z.wide)
        for f in range(z.fields):
            for p in range(2):
                obuf[1 - half, f, p] = tmp[f, p, z.halo : z.halo + z.own, :]
        band = Band(z, scratch + (co1, kk1))
        band.load(tmp, z.inset, z.narrow)
        band.steps(rows_f, 1, 0, offset + z.inset, z.narrow)
        band.store(tmp, z.narrow)
        for f in range(z.fields):
            for p in range(2):
                obuf[half, f, p] = tmp[f, p, z.inset : z.inset + z.own, :]
        ko[...] = obuf[0]
        so[...] = obuf[1]


def finish_kernel(z, keep, got, out):
    half, _ = half_and_chip()
    for f in range(z.fields):
        for p in range(2):
            a, b = keep[f, p], got[f, p]
            west = jnp.where(half == 0, a, b)
            east = jnp.where(half == 0, b, a)
            out[0, f, pl.ds(p, z.lanes, stride=2), :] = jnp.concatenate([west, east], axis=0).T


def shape(dims, dtype):
    return jax.ShapeDtypeStruct(tuple(dims), dtype)


def in_vmem(count):
    return [pl.BlockSpec(memory_space=pltpu.VMEM)] * count


def in_hbm(count):
    return [pl.BlockSpec(memory_space=pltpu.HBM)] * count


def per_device(forcing, zonal_courant, meridional_courant, zonal_faces, meridional_faces, coupling):
    z = Sizes(forcing.shape)
    tm_count, strips = lax.axis_size("tm"), lax.axis_size("space")
    assert tm_count == 4 and z.main % 16 == 0 and z.shift % 16 == 0
    params = pltpu.CompilerParams(vmem_limit_bytes=VMEM_BYTES)
    f_shape = (z.steps, z.fields, 2, z.main, z.lanes)
    c_shape = (5, 2, z.main, z.lanes)
    pay_shape = (z.payload, 2 * SUB, z.lanes)
    keep_f, send_f, keep_c, send_c, pay_a, pay_b = pl.pallas_call(
        functools.partial(prepare_kernel, z),
        out_shape=[
            shape(f_shape, BF16),
            shape(f_shape, BF16),
            shape(c_shape, F32),
            shape(c_shape, F32),
            shape(pay_shape, BF16),
            shape(pay_shape, BF16),
        ],
        in_specs=in_hbm(6),
        out_specs=in_vmem(6),
        scratch_shapes=[
            pltpu.VMEM(forcing.shape[1:], BF16),
            pltpu.VMEM((4, z.rows, z.strip), F32),
            pltpu.VMEM((z.fields, 1, z.fields), F32),
            pltpu.VMEM((4, z.rows, z.strip), F32),
            pltpu.SemaphoreType.DMA((5 + z.steps,)),
        ],
        compiler_params=params,
        name="prepare",
    )(
        *[
            pltpu.with_memory_space_constraint(array, pltpu.HBM)
            for array in (
                forcing,
                zonal_courant,
                meridional_courant,
                zonal_faces,
                meridional_faces,
                jnp.swapaxes(coupling, 0, 1),
            )
        ]
    )

    def device(tm, space):
        return tm * strips + space % strips

    everyone = [(t, s) for t in range(tm_count) for s in range(strips)]
    partner = [(t, t ^ 1) for t in range(tm_count)]
    perm_a = [(device(t, s), device(t ^ 1, s + 1 if t % 2 else s - 1)) for t, s in everyone]
    perm_b = [(device(t, s), device(t, s - 1 if t % 2 else s + 1)) for t, s in everyone]
    got_f = lax.ppermute(send_f, "tm", partner)
    got_c = lax.ppermute(send_c, "tm", partner)
    got_a = lax.ppermute(pay_a, ("tm", "space"), perm_a)
    got_b = lax.ppermute(pay_b, ("tm", "space"), perm_b)

    def band_scratch(span):
        state = pltpu.VMEM((span + 2, z.fields, 2, SUB, z.lanes), F32)
        return [state] * 4

    def operators(span):
        return [shape(dims, F32) for dims in ((span + 2, 8, 2, SUB, z.lanes), (z.fields**2, SUB, z.lanes))]

    def operator_scratch(span):
        return [pltpu.VMEM(spec.shape, spec.dtype) for spec in operators(span)]

    rows_f_shape = shape((2, z.steps, z.fields, 2, z.window, z.lanes), F32)
    rows_c_shape = shape((2, 5, 2, z.window, z.lanes), F32)
    half_dims = (z.fields, 2, z.own, z.lanes)
    def tiles(columns):
        return shape((z.fields, columns // SUB, 2 * SUB, z.lanes), BF16)

    rows_f, rows_c, inner, core = pl.pallas_call(
        functools.partial(inner_kernel, z, 1),
        out_shape=[rows_f_shape, rows_c_shape, shape((2, z.fields, 2, z.main, z.lanes), F32), tiles(z.core)],
        in_specs=in_vmem(4),
        out_specs=in_vmem(4),
        scratch_shapes=band_scratch(z.wide) + operator_scratch(z.wide),
        compiler_params=params,
        cost_estimate=pl.CostEstimate(flops=10**9, bytes_accessed=2 * 10**7, transcendentals=0),
        name="inner",
    )(keep_f, got_f, keep_c, got_c)
    down = [(device(t, s), device(t - 2, s)) for t, s in everyone if t >= 2]
    across = [(device(t, s), device((t ^ 1) - 2, s + 1 if t % 2 else s - 1)) for t, s in everyone if t >= 2]
    core = lax.ppermute(core, ("tm", "space"), down)
    rows_f, rows_c, kept, sent, edge, *late_operators = pl.pallas_call(
        functools.partial(rim_kernel, z, 1),
        out_shape=[
            rows_f_shape,
            rows_c_shape,
            shape(half_dims, F32),
            shape(half_dims, F32),
            tiles(z.halo),
        ]
        + operators(z.wide)
        + operators(z.narrow),
        in_specs=in_vmem(5),
        out_specs=in_vmem(9),
        input_output_aliases={3: 0, 4: 1},
        scratch_shapes=[
            pltpu.VMEM((2,) + half_dims, F32),
            pltpu.VMEM((z.fields, 2, 3 * z.halo, z.lanes), F32),
        ]
        + band_scratch(z.wide)
        + operator_scratch(3 * z.halo // SUB),
        compiler_params=params,
        cost_estimate=pl.CostEstimate(flops=10**9, bytes_accessed=2 * 10**7, transcendentals=0),
        name="rim",
    )(got_a, got_b, inner, rows_f, rows_c)
    far = lax.ppermute(edge, ("tm", "space"), across)
    near = lax.ppermute(edge, ("tm", "space"), down)
    kept, sent = pl.pallas_call(
        functools.partial(late_kernel, z, 0),
        out_shape=[shape(half_dims, F32), shape(half_dims, F32)],
        in_specs=in_vmem(10),
        out_specs=in_vmem(2),
        input_output_aliases={4: 0, 5: 1},
        scratch_shapes=[
            pltpu.VMEM((2,) + half_dims, F32),
            pltpu.VMEM((z.fields, 2, z.main, z.lanes), F32),
        ]
        + band_scratch(z.wide),
        compiler_params=params,
        name="late",
    )(core, near, far, rows_f, kept, sent, *late_operators)
    got = lax.ppermute(sent, "tm", partner)
    return pl.pallas_call(
        functools.partial(finish_kernel, z),
        out_shape=shape((1, z.fields, z.rows, z.strip), F32),
        in_specs=in_vmem(2),
        out_specs=pl.BlockSpec(memory_space=pltpu.VMEM),
        compiler_params=params,
        name="finish",
    )(kept, got)


def solution(mesh):
    return jax.shard_map(
        per_device,
        mesh=mesh,
        in_specs=(
            P("tm", None, None, None, "space"),
            P("tm", None, "space"),
            P("tm", None, "space"),
            P("tm", None, "space"),
            P("tm", None, "space"),
            P("tm", None, None),
        ),
        out_specs=P("tm", None, None, "space"),
        check_vma=False,
    )
```

```python
import functools

import jax
import jax.numpy as jnp
from jax import lax
from jax.experimental import pallas as pl
from jax.experimental.pallas import tpu as pltpu
from jax.sharding import PartitionSpec as P

SWEEPS = 2
OMEGA = 0.4
SUB = 8
REACH = SWEEPS + 1
VMEM_BYTES = 20 * 2**20
F32 = jnp.float32
BF16 = jnp.bfloat16


class Sizes:
    def __init__(self, forcing_shape):
        _, self.steps, self.fields, self.rows, self.strip = forcing_shape
        self.lanes = self.rows // 2
        self.halo = 2 * REACH * self.steps
        self.main = self.strip // 2 + 2 * self.halo
        self.window = self.main + self.halo
        self.span = self.window // SUB
        self.shift = self.strip - self.main
        self.own = self.strip // 2
        self.groups = [-(-REACH * (self.steps + k) // SUB) for k in range(self.steps)]
        self.group_start = [self.fields * sum(self.groups[:k]) for k in range(self.steps)]
        self.coef_start = self.fields * sum(self.groups)
        self.coef_groups = self.halo // SUB
        self.payload = self.coef_start + 4 * self.coef_groups
        self.message = self.own + self.halo
        self.core = self.message - self.halo
        self.wide, self.narrow = self.main // SUB, (self.main - self.halo) // SUB
        self.inset = self.halo // 2
        self.rim = 3 * self.halo
        self.base = -self.inset % SUB


def half_and_chip():
    tm = lax.axis_index("tm")
    return lax.rem(tm, 2), tm // 2


def prepare_kernel(z, fo_in, zc, mc, zf, mf, cp_in, keep_f, send_f, keep_c, send_c, pay_a, pay_b, fo, co, cp, buf, sems):
    half, _ = half_and_chip()
    left = half == 0
    row = lax.broadcasted_iota(jnp.int32, (z.rows, z.strip), 0)
    coef_copies = [
        pltpu.make_async_copy(ref.at[0], co.at[c], sems.at[c]) for c, ref in enumerate((zf, mf, zc, mc))
    ]
    forcing_copies = [pltpu.make_async_copy(fo_in.at[0, k], fo.at[k], sems.at[5 + k]) for k in range(z.steps)]
    mixing_copy = pltpu.make_async_copy(cp_in, cp, sems.at[4])
    for copy in coef_copies + [mixing_copy] + forcing_copies:
        copy.start()

    def columns(values, slot):
        buf[slot] = values
        return [buf[slot, pl.ds(p, z.lanes, stride=2), :].T for p in range(2)]

    def split(both, groups, start, keep, send):
        for p in range(2):
            low, high = both[p][: z.main], both[p][z.shift :]
            keep[p] = jnp.where(left, low, high).astype(keep.dtype)
            send[p] = jnp.where(left, high, low).astype(send.dtype)
        for g in range(groups):
            lo, hi = SUB * g, z.strip - SUB * (groups - g)
            west = jnp.concatenate([both[p][lo : lo + SUB] for p in range(2)], axis=0)
            east = jnp.concatenate([both[p][hi : hi + SUB] for p in range(2)], axis=0)
            pay_a[start + g] = jnp.where(left, west, east).astype(BF16)
            pay_b[start + g] = jnp.where(left, east, west).astype(BF16)

    slots = buf.shape[0]
    count = 0
    for c in range(4):
        coef_copies[c].wait()
        values = co[c]
        if c == 1:
            values = jnp.where(row < z.rows - 1, values, jnp.zeros_like(values))
        both = columns(values, count % slots)
        split(both, z.coef_groups, z.coef_start + c * z.coef_groups, keep_c.at[c], send_c.at[c])
        count += 1
    mixing_copy.wait()
    for ref in (keep_c, send_c):
        for g in range(z.fields):
            ref[4, 0, g : g + 1, : z.fields] = cp[g]
    for k in range(z.steps):
        forcing_copies[k].wait()
        for f in range(z.fields):
            both = columns(fo[k, f].astype(F32), count % slots)
            split(both, z.groups[k], z.group_start[k] + f * z.groups[k], keep_f.at[k, f], send_f.at[k, f])
            count += 1


def fill_ghosts(ref, span, count):
    for n in range(count):
        for p in range(2):
            ref[0, n, p] = pltpu.roll(ref[span, n, p], 1, 0)
            ref[span + 1, n, p] = pltpu.roll(ref[1, n, p], SUB - 1, 0)


class Band:
    def __init__(self, z, scratch):
        self.z = z
        self.r, self.u1, self.u2, self.pz, self.co, self.kk = scratch
        self.lane = lax.broadcasted_iota(jnp.int32, (SUB, z.lanes), 1)

    def east(self, v):
        return pltpu.roll(v, 1, 1)

    def west(self, v):
        return pltpu.roll(v, self.z.lanes - 1, 1)

    def set_operators(self, rows_c, q, offset, span):
        z, u1, co = self.z, self.u1, self.co
        for c in range(4):
            for p in range(2):
                for i in range(span):
                    u1[i + 1, c, p] = rows_c[q, c, p, pl.ds(offset + i, SUB, stride=span), :]
        fill_ghosts(u1, span, 1)
        for i in range(1, span + 1):
            be, bo = u1[i, 1, 0], u1[i, 1, 1]
            south = (self.east(bo), be)
            for p in range(2):
                a, aw, b = u1[i, 0, p], u1[i - 1, 0, p], u1[i, 1, p]
                centre = 1.0 - OMEGA * (1.0 + (a + aw) + (b + south[p]))
                co[i, 0, p] = centre
                co[i, 7, p] = 1.0 + centre
                co[i, 1, p] = OMEGA * a
                co[i, 2, p] = OMEGA * aw
                co[i, 3, p] = OMEGA * b
                co[i, 4, p] = OMEGA * south[p]
                co[i, 5, p] = (0.5 * OMEGA) * u1[i, 2, p]
                co[i, 6, p] = (0.5 * OMEGA) * u1[i, 3, p]
        for g in range(z.fields):
            for f in range(z.fields):
                value = rows_c[q, 4, 0, g : g + 1, f : f + 1]
                if f == g:
                    value = value + 1.0
                self.kk[g * z.fields + f] = jnp.broadcast_to(OMEGA * value, (SUB, z.lanes))

    def load(self, at, offset, span):
        for i in range(span):
            for f in range(self.z.fields):
                for p in range(2):
                    self.r[i + 1, f, p] = at[f, p, pl.ds(offset + i, SUB, stride=span), :]

    def store(self, at, span, base=0):
        for i in range(span):
            for f in range(self.z.fields):
                for p in range(2):
                    at[f, p, pl.ds(base + i, SUB, stride=span), :] = self.r[i + 1, f, p]

    def sweep(self, src, dst, i, source):
        co = self.co
        first = 7 if source is None else 0
        ga = [co[i, c, 0] for c in (first, 1, 2, 3, 4)]
        gb = [co[i, c, 1] for c in (first, 1, 2, 3, 4)]
        for f in range(self.z.fields):
            a, b = src[i, f, 0], src[i, f, 1]
            va = ga[0] * a + ga[1] * src[i + 1, f, 0] + ga[2] * src[i - 1, f, 0] + ga[3] * b + ga[4] * self.east(b)
            vb = gb[0] * b + gb[1] * src[i + 1, f, 1] + gb[2] * src[i - 1, f, 1] + gb[3] * self.west(a) + gb[4] * a
            if source is not None:
                va = va + source[i, f, 0]
                vb = vb + source[i, f, 1]
                self.pz[i, f, 0] = co[i, 5, 0] * va
                self.pz[i, f, 1] = co[i, 5, 1] * vb
            dst[i, f, 0] = va
            dst[i, f, 1] = vb

    def step(self, forcing, offset, span):
        z, r, u1, u2, pz, co, kk = self.z, self.r, self.u1, self.u2, self.pz, self.co, self.kk
        zero = jnp.zeros((SUB, z.lanes), F32)
        fill_ghosts(r, span, z.fields)
        for i in range(1, span + 1):
            self.sweep(r, u1, i, None)
        fill_ghosts(u1, span, z.fields)
        for i in range(1, span + 1):
            self.sweep(u1, u2, i, r)
        fill_ghosts(pz, span, z.fields)
        for i in range(1, span + 1):
            us = [[u2[i, g, p] for p in range(2)] for g in range(z.fields)]
            for f in range(z.fields):
                qa, qb = co[i, 6, 0] * us[f][0], co[i, 6, 1] * us[f][1]
                qba = jnp.where(self.lane == 0, zero, self.east(qb))
                qab = jnp.where(self.lane == z.lanes - 1, zero, self.west(qa))
                oa = (pz[i + 1, f, 0] - pz[i - 1, f, 0]) + (qb - qba)
                ob = (pz[i + 1, f, 1] - pz[i - 1, f, 1]) + (qab - qa)
                for g in range(z.fields):
                    w = kk[g * z.fields + f]
                    oa = oa + w * us[g][0]
                    ob = ob + w * us[g][1]
                rows = pl.ds(offset + i - 1, SUB, stride=span)
                r[i, f, 0] = oa + forcing[f, 0, rows, :]
                r[i, f, 1] = ob + forcing[f, 1, rows, :]

    def steps(self, rows_f, q, begin, offset, span):
        last = self.z.steps - 1

        def one(n, carry):
            self.step(rows_f.at[q, last - n], offset, span)
            return carry

        lax.fori_loop(begin, last + 1, one, 0)


def aligned(offset, count):
    return pl.ds(pl.multiple_of(offset, SUB), count)


def tile_of(ref, f, at):
    return jnp.concatenate([ref[f, p, at, :] for p in range(2)], axis=0).astype(BF16)


def inner_kernel(z, active, kf, rf, kc, rc, rows_f, rows_c, inner, core, *scratch):
    half, chip = half_and_chip()
    main_at = z.halo * (1 - half)
    blank = jnp.zeros((z.halo, z.lanes), F32)

    def put(ref, values):
        ref[aligned(main_at, z.main), :] = values.astype(F32)
        ref[aligned(z.main * half, z.halo), :] = blank

    for q, forcing, coefs in ((1 - half, kf, kc), (half, rf, rc)):
        for c in range(4):
            for p in range(2):
                put(rows_c.at[q, c, p], coefs[c, p])
        rows_c[q, 4, 0, :SUB, :] = coefs[4, 0, :SUB, :]
        for k in range(z.steps):
            for f in range(z.fields):
                for p in range(2):
                    put(rows_f.at[q, k, f, p], forcing[k, f, p])

    @pl.when(chip == active)
    def _():
        band = Band(z, scratch)
        span = z.main // SUB
        band.load(rows_f.at[0, z.steps - 1], main_at, span)

        def sub_window(q, carry):
            band.set_operators(rows_c, q, main_at, span)
            band.steps(rows_f, q, 1 - q, main_at, span)
            band.store(inner.at[q], span)
            return carry

        lax.fori_loop(0, 2, sub_window, 0)
        for f in range(z.fields):
            for g in range(z.core // SUB):
                core[f, g] = tile_of(inner.at[1], f, slice(z.halo + SUB * g, z.halo + SUB * (g + 1)))


def rim_kernel(z, active, ra, rb, inner, rows_f_in, rows_c_in, rows_f, rows_c, ko, so, edge, *refs):
    late_operators, (obuf, tmp), scratch = refs[:5], refs[5:7], refs[7:]
    half, chip = half_and_chip()
    for q, pay in ((half, ra), (1 - half, rb)):

        def put(ref, start, groups):
            for g in range(groups):
                tile = pay[start + g].astype(F32)
                at = jnp.where(half == 0, z.halo - SUB * (groups - g), z.main + SUB * g)
                for p in range(2):
                    ref[p, aligned(at, SUB), :] = tile[SUB * p : SUB * (p + 1)]

        for c in range(4):
            put(rows_c.at[q, c], z.coef_start + c * z.coef_groups, z.coef_groups)
        for k in range(z.steps):
            for f in range(z.fields):
                put(rows_f.at[q, k, f], z.group_start[k] + f * z.groups[k], z.groups[k])

    @pl.when(chip != active)
    def _():
        co_core, co_rim, co_late, mix_first, mix_last = late_operators
        for q, co, mix, columns, offset in (
            (0, co_core, mix_first, z.core, z.halo * (2 - half)),
            (0, co_rim, mix_first, z.rim, (z.window - z.rim) * half),
            (1, co_late, mix_last, z.main - z.halo, z.halo * half + z.inset),
        ):
            Band(z, scratch[:4] + (co, mix)).set_operators(rows_c, q, offset, columns // SUB)

    @pl.when(chip == active)
    def _():
        band = Band(z, scratch)
        span = z.rim // SUB
        offset = (z.window - z.rim) * half
        rim = slice(z.halo, 2 * z.halo)
        band.load(rows_f.at[0, z.steps - 1], offset, span)

        def sub_window(q, carry):
            band.set_operators(rows_c, q, offset, span)
            band.steps(rows_f, q, 1 - q, offset, span)
            band.store(tmp, span)

            @pl.when(q == 1)
            def _():
                for f in range(z.fields):
                    for g in range(z.halo // SUB):
                        edge[f, g] = tile_of(tmp, f, slice(z.halo + SUB * g, z.halo + SUB * (g + 1)))

            place = jnp.where(q == half, 1, 0)
            for f in range(z.fields):
                for p in range(2):
                    obuf[place, f, p] = inner[q, f, p, aligned((z.main - z.own) * half, z.own), :]
                    obuf[place, f, p, aligned((z.own - z.halo) * half, z.halo), :] = tmp[f, p, rim, :]
            return carry

        lax.fori_loop(0, 2, sub_window, 0)
        ko[...] = obuf[0]
        so[...] = obuf[1]


def put_tiles(z, tmp, tiles, at):
    for f in range(z.fields):
        for n, tile in enumerate(tiles(f)):
            for p in range(2):
                tmp[f, p, aligned(at + SUB * n, SUB), :] = tile.astype(F32)[SUB * p : SUB * (p + 1)]


def early_kernel(z, active, core, rows_f, co, mix, state, tmp, *scratch):
    half, chip = half_and_chip()

    @pl.when(chip == active)
    def _():
        band = Band(z, scratch + (co, mix))
        span = z.core // SUB
        put_tiles(z, tmp, lambda f: [core[f, g] for g in range(z.core // SUB)], 0)
        band.load(tmp, 0, span)
        band.steps(rows_f, 0, 0, z.halo * (2 - half), span)
        band.store(state, span, z.base)


def late_kernel(
    z, active, core, near, far, state, rows_f, co_rim, mix_first, co_late, mix_last, ko_in, so_in, ko, so, obuf, tmp, *scratch
):
    half, chip = half_and_chip()

    @pl.when(chip == active)
    def _():
        groups = z.halo // SUB
        span = z.rim // SUB
        put_tiles(z, tmp, lambda f: [far[f, g] for g in range(groups)], 2 * z.halo * half)
        put_tiles(z, tmp, lambda f: [near[f, g] for g in range(groups)], z.halo)
        first = (z.core // SUB - groups) * half
        put_tiles(z, tmp, lambda f: [core[f, first + g] for g in range(groups)], 2 * z.halo * (1 - half))
        band = Band(z, scratch + (co_rim, mix_first))
        band.load(tmp, 0, span)
        band.steps(rows_f, 0, 0, (z.window - z.rim) * half, span)
        band.store(tmp, span, z.base)
        outer, inner = 2 * z.halo, z.core - z.halo
        start = z.inset + z.base
        for f in range(z.fields):
            for p in range(2):
                rim = tmp[f, p, start : start + outer, :]
                tmp[f, p, aligned(inner * half, outer), :] = rim
                tmp[f, p, aligned(outer * (1 - half), inner), :] = state[f, p, start : start + inner, :]
                obuf[1 - half, f, p] = tmp[f, p, z.inset : z.inset + z.own, :]
        band = Band(z, scratch + (co_late, mix_last))
        band.load(tmp, 0, z.narrow)
        band.steps(rows_f, 1, 0, z.halo * half + z.inset, z.narrow)
        band.store(tmp, z.narrow)
        for f in range(z.fields):
            for p in range(2):
                obuf[half, f, p] = tmp[f, p, z.inset : z.inset + z.own, :]
        ko[...] = obuf[0]
        so[...] = obuf[1]


def finish_kernel(z, keep, got, out):
    half, _ = half_and_chip()
    for f in range(z.fields):
        for p in range(2):
            a, b = keep[f, p], got[f, p]
            west = jnp.where(half == 0, a, b)
            east = jnp.where(half == 0, b, a)
            out[0, f, pl.ds(p, z.lanes, stride=2), :] = jnp.concatenate([west, east], axis=0).T


def shape(dims, dtype):
    return jax.ShapeDtypeStruct(tuple(dims), dtype)


def in_vmem(count):
    return [pl.BlockSpec(memory_space=pltpu.VMEM)] * count


def in_hbm(count):
    return [pl.BlockSpec(memory_space=pltpu.HBM)] * count


def per_device(forcing, zonal_courant, meridional_courant, zonal_faces, meridional_faces, coupling):
    z = Sizes(forcing.shape)
    tm_count, strips = lax.axis_size("tm"), lax.axis_size("space")
    assert tm_count == 4 and z.main % 16 == 0 and z.shift % 16 == 0
    params = pltpu.CompilerParams(vmem_limit_bytes=VMEM_BYTES)
    f_shape = (z.steps, z.fields, 2, z.main, z.lanes)
    c_shape = (5, 2, z.main, z.lanes)
    pay_shape = (z.payload, 2 * SUB, z.lanes)
    keep_f, send_f, keep_c, send_c, pay_a, pay_b = pl.pallas_call(
        functools.partial(prepare_kernel, z),
        out_shape=[
            shape(f_shape, BF16),
            shape(f_shape, BF16),
            shape(c_shape, F32),
            shape(c_shape, F32),
            shape(pay_shape, BF16),
            shape(pay_shape, BF16),
        ],
        in_specs=in_hbm(6),
        out_specs=in_vmem(6),
        scratch_shapes=[
            pltpu.VMEM(forcing.shape[1:], BF16),
            pltpu.VMEM((4, z.rows, z.strip), F32),
            pltpu.VMEM((z.fields, 1, z.fields), F32),
            pltpu.VMEM((4, z.rows, z.strip), F32),
            pltpu.SemaphoreType.DMA((5 + z.steps,)),
        ],
        compiler_params=params,
        name="prepare",
    )(
        *[
            pltpu.with_memory_space_constraint(array, pltpu.HBM)
            for array in (
                forcing,
                zonal_courant,
                meridional_courant,
                zonal_faces,
                meridional_faces,
                jnp.swapaxes(coupling, 0, 1),
            )
        ]
    )

    def device(tm, space):
        return tm * strips + space % strips

    everyone = [(t, s) for t in range(tm_count) for s in range(strips)]
    partner = [(t, t ^ 1) for t in range(tm_count)]
    perm_a = [(device(t, s), device(t ^ 1, s + 1 if t % 2 else s - 1)) for t, s in everyone]
    perm_b = [(device(t, s), device(t, s - 1 if t % 2 else s + 1)) for t, s in everyone]
    got_f = lax.ppermute(send_f, "tm", partner)
    got_c = lax.ppermute(send_c, "tm", partner)
    got_a = lax.ppermute(pay_a, ("tm", "space"), perm_a)
    got_b = lax.ppermute(pay_b, ("tm", "space"), perm_b)

    def band_scratch(span):
        state = pltpu.VMEM((span + 2, z.fields, 2, SUB, z.lanes), F32)
        return [state] * 4

    def stencil(columns):
        return shape((columns // SUB + 2, 8, 2, SUB, z.lanes), F32)

    mixing = shape((z.fields**2, SUB, z.lanes), F32)

    def operator_scratch(columns):
        return [pltpu.VMEM(spec.shape, spec.dtype) for spec in (stencil(columns), mixing)]

    rows_f_shape = shape((2, z.steps, z.fields, 2, z.window, z.lanes), F32)
    rows_c_shape = shape((2, 5, 2, z.window, z.lanes), F32)
    half_dims = (z.fields, 2, z.own, z.lanes)
    def tiles(columns):
        return shape((z.fields, columns // SUB, 2 * SUB, z.lanes), BF16)

    rows_f, rows_c, inner, core = pl.pallas_call(
        functools.partial(inner_kernel, z, 1),
        out_shape=[rows_f_shape, rows_c_shape, shape((2, z.fields, 2, z.main, z.lanes), F32), tiles(z.core)],
        in_specs=in_vmem(4),
        out_specs=in_vmem(4),
        scratch_shapes=band_scratch(z.wide) + operator_scratch(z.main),
        compiler_params=params,
        cost_estimate=pl.CostEstimate(flops=10**9, bytes_accessed=2 * 10**7, transcendentals=0),
        name="inner",
    )(keep_f, got_f, keep_c, got_c)
    down = [(device(t, s), device(t ^ 2, s)) for t, s in everyone]
    across = [(device(t, s), device((t ^ 1) - 2, s + 1 if t % 2 else s - 1)) for t, s in everyone if t >= 2]
    core = lax.ppermute(core, ("tm", "space"), down)
    rows_f, rows_c, kept, sent, edge, co_core, co_rim, co_late, mix_first, mix_last = pl.pallas_call(
        functools.partial(rim_kernel, z, 1),
        out_shape=[
            rows_f_shape,
            rows_c_shape,
            shape(half_dims, F32),
            shape(half_dims, F32),
            tiles(z.halo),
            stencil(z.core),
            stencil(z.rim),
            stencil(z.main - z.halo),
            mixing,
            mixing,
        ],
        in_specs=in_vmem(5),
        out_specs=in_vmem(10),
        input_output_aliases={3: 0, 4: 1},
        scratch_shapes=[
            pltpu.VMEM((2,) + half_dims, F32),
            pltpu.VMEM((z.fields, 2, z.rim, z.lanes), F32),
        ]
        + band_scratch(z.wide)
        + operator_scratch(z.rim),
        compiler_params=params,
        cost_estimate=pl.CostEstimate(flops=10**9, bytes_accessed=2 * 10**7, transcendentals=0),
        name="rim",
    )(got_a, got_b, inner, rows_f, rows_c)
    state = pl.pallas_call(
        functools.partial(early_kernel, z, 0),
        out_shape=shape((z.fields, 2, z.core + SUB, z.lanes), F32),
        in_specs=in_vmem(4),
        out_specs=pl.BlockSpec(memory_space=pltpu.VMEM),
        scratch_shapes=[pltpu.VMEM((z.fields, 2, z.core, z.lanes), F32)] + band_scratch(z.core // SUB),
        compiler_params=params,
        name="early",
    )(core, rows_f, co_core, mix_first)
    far = lax.ppermute(edge, ("tm", "space"), across)
    near = lax.ppermute(edge, ("tm", "space"), [(i, j) for i, j in down if i > j])
    kept, sent = pl.pallas_call(
        functools.partial(late_kernel, z, 0),
        out_shape=[shape(half_dims, F32), shape(half_dims, F32)],
        in_specs=in_vmem(11),
        out_specs=in_vmem(2),
        input_output_aliases={9: 0, 10: 1},
        scratch_shapes=[
            pltpu.VMEM((2,) + half_dims, F32),
            pltpu.VMEM((z.fields, 2, z.main, z.lanes), F32),
        ]
        + band_scratch(z.narrow),
        compiler_params=params,
        name="late",
    )(core, near, far, state, rows_f, co_rim, mix_first, co_late, mix_last, kept, sent)
    got = lax.ppermute(sent, "tm", partner)
    return pl.pallas_call(
        functools.partial(finish_kernel, z),
        out_shape=shape((1, z.fields, z.rows, z.strip), F32),
        in_specs=in_vmem(2),
        out_specs=pl.BlockSpec(memory_space=pltpu.VMEM),
        compiler_params=params,
        name="finish",
    )(kept, got)


def solution(mesh):
    return jax.shard_map(
        per_device,
        mesh=mesh,
        in_specs=(
            P("tm", None, None, None, "space"),
            P("tm", None, "space"),
            P("tm", None, "space"),
            P("tm", None, "space"),
            P("tm", None, "space"),
            P("tm", None, None),
        ),
        out_specs=P("tm", None, None, "space"),
        check_vma=False,
    )
```

```python
import functools

import jax
import jax.numpy as jnp
from jax import lax
from jax.experimental import pallas as pl
from jax.experimental.pallas import tpu as pltpu
from jax.sharding import PartitionSpec as P

SWEEPS = 2
OMEGA = 0.4
SUB = 8
REACH = SWEEPS + 1
VMEM_BYTES = 20 * 2**20
F32 = jnp.float32
BF16 = jnp.bfloat16


class Sizes:
    def __init__(self, forcing_shape):
        _, self.steps, self.fields, self.rows, self.strip = forcing_shape
        self.lanes = self.rows // 2
        self.halo = 2 * REACH * self.steps
        self.main = self.strip // 2 + 2 * self.halo
        self.window = self.main + self.halo
        self.span = self.window // SUB
        self.shift = self.strip - self.main
        self.own = self.strip // 2
        self.groups = [-(-REACH * (self.steps + k) // SUB) for k in range(self.steps)]
        self.group_start = [self.fields * sum(self.groups[:k]) for k in range(self.steps)]
        self.coef_start = self.fields * sum(self.groups)
        self.coef_groups = self.halo // SUB
        self.payload = self.coef_start + 4 * self.coef_groups
        self.message = self.own + self.halo
        self.core = self.message - self.halo
        self.wide, self.narrow = self.main // SUB, (self.main - self.halo) // SUB
        self.inset = self.halo // 2
        self.rim = 3 * self.halo
        self.base = -self.inset % SUB


def half_and_chip():
    tm = lax.axis_index("tm")
    return lax.rem(tm, 2), tm // 2


def prepare_kernel(z, fo_in, zc, mc, zf, mf, cp_in, keep_f, send_f, keep_c, send_c, pay_a, pay_b, fo, co, cp, buf, sems):
    half, _ = half_and_chip()
    left = half == 0
    row = lax.broadcasted_iota(jnp.int32, (z.rows, z.strip), 0)
    coef_copies = [
        pltpu.make_async_copy(ref.at[0], co.at[c], sems.at[c]) for c, ref in enumerate((zf, mf, zc, mc))
    ]
    forcing_copies = [pltpu.make_async_copy(fo_in.at[0, k], fo.at[k], sems.at[5 + k]) for k in range(z.steps)]
    mixing_copy = pltpu.make_async_copy(cp_in, cp, sems.at[4])
    for copy in coef_copies + [mixing_copy] + forcing_copies:
        copy.start()

    def columns(values, slot):
        buf[slot] = values
        return [buf[slot, pl.ds(p, z.lanes, stride=2), :].T for p in range(2)]

    def split(both, groups, start, keep, send):
        for p in range(2):
            low, high = both[p][: z.main], both[p][z.shift :]
            keep[p] = jnp.where(left, low, high).astype(keep.dtype)
            send[p] = jnp.where(left, high, low).astype(send.dtype)
        for g in range(groups):
            lo, hi = SUB * g, z.strip - SUB * (groups - g)
            west = jnp.concatenate([both[p][lo : lo + SUB] for p in range(2)], axis=0)
            east = jnp.concatenate([both[p][hi : hi + SUB] for p in range(2)], axis=0)
            pay_a[start + g] = jnp.where(left, west, east).astype(BF16)
            pay_b[start + g] = jnp.where(left, east, west).astype(BF16)

    slots = buf.shape[0]
    count = 0
    for c in range(4):
        coef_copies[c].wait()
        values = co[c]
        if c == 1:
            values = jnp.where(row < z.rows - 1, values, jnp.zeros_like(values))
        both = columns(values, count % slots)
        split(both, z.coef_groups, z.coef_start + c * z.coef_groups, keep_c.at[c], send_c.at[c])
        count += 1
    mixing_copy.wait()
    for ref in (keep_c, send_c):
        for g in range(z.fields):
            ref[4, 0, g : g + 1, : z.fields] = cp[g]
    for k in range(z.steps):
        forcing_copies[k].wait()
        for f in range(z.fields):
            both = columns(fo[k, f].astype(F32), count % slots)
            split(both, z.groups[k], z.group_start[k] + f * z.groups[k], keep_f.at[k, f], send_f.at[k, f])
            count += 1


def fill_ghosts(ref, span, count):
    for n in range(count):
        for p in range(2):
            ref[0, n, p] = pltpu.roll(ref[span, n, p], 1, 0)
            ref[span + 1, n, p] = pltpu.roll(ref[1, n, p], SUB - 1, 0)


class Band:
    def __init__(self, z, scratch):
        self.z = z
        self.r, self.u1, self.u2, self.pz, self.co, self.kk = scratch
        self.lane = lax.broadcasted_iota(jnp.int32, (SUB, z.lanes), 1)

    def east(self, v):
        return pltpu.roll(v, 1, 1)

    def west(self, v):
        return pltpu.roll(v, self.z.lanes - 1, 1)

    def set_operators(self, rows_c, q, offset, span):
        z, u1, co = self.z, self.u1, self.co
        for c in range(4):
            for p in range(2):
                for i in range(span):
                    u1[i + 1, c, p] = rows_c[q, c, p, pl.ds(offset + i, SUB, stride=span), :]
        fill_ghosts(u1, span, 1)
        for i in range(1, span + 1):
            be, bo = u1[i, 1, 0], u1[i, 1, 1]
            south = (self.east(bo), be)
            for p in range(2):
                a, aw, b = u1[i, 0, p], u1[i - 1, 0, p], u1[i, 1, p]
                centre = 1.0 - OMEGA * (1.0 + (a + aw) + (b + south[p]))
                co[i, 0, p] = centre
                co[i, 7, p] = 1.0 + centre
                co[i, 1, p] = OMEGA * a
                co[i, 2, p] = OMEGA * aw
                co[i, 3, p] = OMEGA * b
                co[i, 4, p] = OMEGA * south[p]
                co[i, 5, p] = (0.5 * OMEGA) * u1[i, 2, p]
                co[i, 6, p] = (0.5 * OMEGA) * u1[i, 3, p]
        for g in range(z.fields):
            for f in range(z.fields):
                value = rows_c[q, 4, 0, g : g + 1, f : f + 1]
                if f == g:
                    value = value + 1.0
                self.kk[g * z.fields + f] = jnp.broadcast_to(OMEGA * value, (SUB, z.lanes))

    def load(self, at, offset, span):
        for i in range(span):
            for f in range(self.z.fields):
                for p in range(2):
                    self.r[i + 1, f, p] = at[f, p, pl.ds(offset + i, SUB, stride=span), :]

    def store(self, at, span, base=0):
        for i in range(span):
            for f in range(self.z.fields):
                for p in range(2):
                    at[f, p, pl.ds(base + i, SUB, stride=span), :] = self.r[i + 1, f, p]

    def sweep(self, src, dst, i, source):
        co = self.co
        first = 7 if source is None else 0
        ga = [co[i, c, 0] for c in (first, 1, 2, 3, 4)]
        gb = [co[i, c, 1] for c in (first, 1, 2, 3, 4)]
        for f in range(self.z.fields):
            a, b = src[i, f, 0], src[i, f, 1]
            va = ga[0] * a + ga[1] * src[i + 1, f, 0] + ga[2] * src[i - 1, f, 0] + ga[3] * b + ga[4] * self.east(b)
            vb = gb[0] * b + gb[1] * src[i + 1, f, 1] + gb[2] * src[i - 1, f, 1] + gb[3] * self.west(a) + gb[4] * a
            if source is not None:
                va = va + source[i, f, 0]
                vb = vb + source[i, f, 1]
                self.pz[i, f, 0] = co[i, 5, 0] * va
                self.pz[i, f, 1] = co[i, 5, 1] * vb
            dst[i, f, 0] = va
            dst[i, f, 1] = vb

    def step(self, forcing, offset, span):
        z, r, u1, u2, pz, co, kk = self.z, self.r, self.u1, self.u2, self.pz, self.co, self.kk
        zero = jnp.zeros((SUB, z.lanes), F32)
        fill_ghosts(r, span, z.fields)
        for i in range(1, span + 1):
            self.sweep(r, u1, i, None)
        fill_ghosts(u1, span, z.fields)
        for i in range(1, span + 1):
            self.sweep(u1, u2, i, r)
        fill_ghosts(pz, span, z.fields)
        for i in range(1, span + 1):
            us = [[u2[i, g, p] for p in range(2)] for g in range(z.fields)]
            for f in range(z.fields):
                qa, qb = co[i, 6, 0] * us[f][0], co[i, 6, 1] * us[f][1]
                qba = jnp.where(self.lane == 0, zero, self.east(qb))
                qab = jnp.where(self.lane == z.lanes - 1, zero, self.west(qa))
                oa = (pz[i + 1, f, 0] - pz[i - 1, f, 0]) + (qb - qba)
                ob = (pz[i + 1, f, 1] - pz[i - 1, f, 1]) + (qab - qa)
                for g in range(z.fields):
                    w = kk[g * z.fields + f]
                    oa = oa + w * us[g][0]
                    ob = ob + w * us[g][1]
                rows = pl.ds(offset + i - 1, SUB, stride=span)
                r[i, f, 0] = oa + forcing[f, 0, rows, :]
                r[i, f, 1] = ob + forcing[f, 1, rows, :]

    def steps(self, rows_f, q, begin, offset, span):
        last = self.z.steps - 1

        def one(n, carry):
            self.step(rows_f.at[q, last - n], offset, span)
            return carry

        lax.fori_loop(begin, last + 1, one, 0)


def aligned(offset, count):
    return pl.ds(pl.multiple_of(offset, SUB), count)


def tile_of(ref, f, at):
    return jnp.concatenate([ref[f, p, at, :] for p in range(2)], axis=0).astype(BF16)


def inner_kernel(z, active, kf, rf, kc, rc, rows_f, rows_c, inner, core, *scratch):
    half, chip = half_and_chip()
    main_at = z.halo * (1 - half)
    blank = jnp.zeros((z.halo, z.lanes), F32)

    def put(ref, values):
        ref[aligned(main_at, z.main), :] = values.astype(F32)
        ref[aligned(z.main * half, z.halo), :] = blank

    for q, forcing, coefs in ((1 - half, kf, kc), (half, rf, rc)):
        for c in range(4):
            for p in range(2):
                put(rows_c.at[q, c, p], coefs[c, p])
        rows_c[q, 4, 0, :SUB, :] = coefs[4, 0, :SUB, :]
        for k in range(z.steps):
            for f in range(z.fields):
                for p in range(2):
                    put(rows_f.at[q, k, f, p], forcing[k, f, p])

    @pl.when(chip == active)
    def _():
        band = Band(z, scratch)
        span = z.main // SUB
        band.load(rows_f.at[0, z.steps - 1], main_at, span)

        def sub_window(q, carry):
            band.set_operators(rows_c, q, main_at, span)
            band.steps(rows_f, q, 1 - q, main_at, span)
            band.store(inner.at[q], span)
            return carry

        lax.fori_loop(0, 2, sub_window, 0)
        for f in range(z.fields):
            for g in range(z.core // SUB):
                core[f, g] = tile_of(inner.at[1], f, slice(z.halo + SUB * g, z.halo + SUB * (g + 1)))


def rim_kernel(z, active, ra, rb, inner, rows_f_in, rows_c_in, rows_f, rows_c, ko, so, edge, *refs):
    late_operators, (obuf, tmp), scratch = refs[:5], refs[5:7], refs[7:]
    half, chip = half_and_chip()
    for q, pay in ((half, ra), (1 - half, rb)):

        def put(ref, start, groups):
            for g in range(groups):
                tile = pay[start + g].astype(F32)
                at = jnp.where(half == 0, z.halo - SUB * (groups - g), z.main + SUB * g)
                for p in range(2):
                    ref[p, aligned(at, SUB), :] = tile[SUB * p : SUB * (p + 1)]

        for c in range(4):
            put(rows_c.at[q, c], z.coef_start + c * z.coef_groups, z.coef_groups)
        for k in range(z.steps):
            for f in range(z.fields):
                put(rows_f.at[q, k, f], z.group_start[k] + f * z.groups[k], z.groups[k])

    @pl.when(chip != active)
    def _():
        co_core, co_rim, co_late, mix_first, mix_last = late_operators
        for q, co, mix, columns, offset in (
            (0, co_core, mix_first, z.core, z.halo * (2 - half)),
            (0, co_rim, mix_first, z.rim, (z.window - z.rim) * half),
            (1, co_late, mix_last, z.main - z.halo, z.halo * half + z.inset),
        ):
            Band(z, scratch[:4] + (co, mix)).set_operators(rows_c, q, offset, columns // SUB)

    @pl.when(chip == active)
    def _():
        band = Band(z, scratch)
        span = z.rim // SUB
        offset = (z.window - z.rim) * half
        rim = slice(z.halo, 2 * z.halo)
        band.load(rows_f.at[0, z.steps - 1], offset, span)

        def sub_window(q, carry):
            band.set_operators(rows_c, q, offset, span)
            band.steps(rows_f, q, 1 - q, offset, span)
            band.store(tmp, span)

            @pl.when(q == 1)
            def _():
                for f in range(z.fields):
                    for g in range(z.halo // SUB):
                        edge[f, g] = tile_of(tmp, f, slice(z.halo + SUB * g, z.halo + SUB * (g + 1)))

            place = jnp.where(q == half, 1, 0)
            for f in range(z.fields):
                for p in range(2):
                    obuf[place, f, p] = inner[q, f, p, aligned((z.main - z.own) * half, z.own), :]
                    obuf[place, f, p, aligned((z.own - z.halo) * half, z.halo), :] = tmp[f, p, rim, :]
            return carry

        lax.fori_loop(0, 2, sub_window, 0)
        ko[...] = obuf[0]
        so[...] = obuf[1]


def put_tiles(z, tmp, tiles, at):
    for f in range(z.fields):
        for n, tile in enumerate(tiles(f)):
            for p in range(2):
                tmp[f, p, aligned(at + SUB * n, SUB), :] = tile.astype(F32)[SUB * p : SUB * (p + 1)]


def early_kernel(z, active, core, rows_f, co, mix, state, tmp, *scratch):
    half, chip = half_and_chip()

    @pl.when(chip == active)
    def _():
        band = Band(z, scratch + (co, mix))
        span = z.core // SUB
        put_tiles(z, tmp, lambda f: [core[f, g] for g in range(z.core // SUB)], 0)
        band.load(tmp, 0, span)
        band.steps(rows_f, 0, 0, z.halo * (2 - half), span)
        band.store(state, span, z.base)


def late_kernel(
    z, active, core, near, far, state, rows_f, co_rim, mix_first, co_late, mix_last, ko_in, so_in, ko, so, obuf, tmp, *scratch
):
    half, chip = half_and_chip()

    @pl.when(chip == active)
    def _():
        groups = z.halo // SUB
        span = z.rim // SUB
        put_tiles(z, tmp, lambda f: [far[f, g] for g in range(groups)], 2 * z.halo * half)
        put_tiles(z, tmp, lambda f: [near[f, g] for g in range(groups)], z.halo)
        first = (z.core // SUB - groups) * half
        put_tiles(z, tmp, lambda f: [core[f, first + g] for g in range(groups)], 2 * z.halo * (1 - half))
        band = Band(z, scratch + (co_rim, mix_first))
        band.load(tmp, 0, span)
        band.steps(rows_f, 0, 0, (z.window - z.rim) * half, span)
        band.store(tmp, span, z.base)
        outer, inner = 2 * z.halo, z.core - z.halo
        start = z.inset + z.base
        for f in range(z.fields):
            for p in range(2):
                rim = tmp[f, p, start : start + outer, :]
                tmp[f, p, aligned(inner * half, outer), :] = rim
                tmp[f, p, aligned(outer * (1 - half), inner), :] = state[f, p, start : start + inner, :]
                obuf[1 - half, f, p] = tmp[f, p, z.inset : z.inset + z.own, :]
        band = Band(z, scratch + (co_late, mix_last))
        band.load(tmp, 0, z.narrow)
        band.steps(rows_f, 1, 0, z.halo * half + z.inset, z.narrow)
        band.store(tmp, z.narrow)
        for f in range(z.fields):
            for p in range(2):
                obuf[half, f, p] = tmp[f, p, z.inset : z.inset + z.own, :]
        ko[...] = obuf[0]
        so[...] = obuf[1]


def finish_kernel(z, keep, got, out):
    half, _ = half_and_chip()
    for f in range(z.fields):
        for p in range(2):
            a, b = keep[f, p], got[f, p]
            west = jnp.where(half == 0, a, b)
            east = jnp.where(half == 0, b, a)
            out[0, f, pl.ds(p, z.lanes, stride=2), :] = jnp.concatenate([west, east], axis=0).T


def shape(dims, dtype):
    return jax.ShapeDtypeStruct(tuple(dims), dtype)


def in_vmem(count):
    return [pl.BlockSpec(memory_space=pltpu.VMEM)] * count


def in_hbm(count):
    return [pl.BlockSpec(memory_space=pltpu.HBM)] * count


def per_device(forcing, zonal_courant, meridional_courant, zonal_faces, meridional_faces, coupling):
    z = Sizes(forcing.shape)
    tm_count, strips = lax.axis_size("tm"), lax.axis_size("space")
    assert tm_count == 4 and z.main % 16 == 0 and z.shift % 16 == 0
    params = pltpu.CompilerParams(vmem_limit_bytes=VMEM_BYTES)
    f_shape = (z.steps, z.fields, 2, z.main, z.lanes)
    c_shape = (5, 2, z.main, z.lanes)
    pay_shape = (z.payload, 2 * SUB, z.lanes)
    keep_f, send_f, keep_c, send_c, pay_a, pay_b = pl.pallas_call(
        functools.partial(prepare_kernel, z),
        out_shape=[
            shape(f_shape, BF16),
            shape(f_shape, BF16),
            shape(c_shape, F32),
            shape(c_shape, F32),
            shape(pay_shape, BF16),
            shape(pay_shape, BF16),
        ],
        in_specs=in_hbm(6),
        out_specs=in_vmem(6),
        scratch_shapes=[
            pltpu.VMEM(forcing.shape[1:], BF16),
            pltpu.VMEM((4, z.rows, z.strip), F32),
            pltpu.VMEM((z.fields, 1, z.fields), F32),
            pltpu.VMEM((4, z.rows, z.strip), F32),
            pltpu.SemaphoreType.DMA((5 + z.steps,)),
        ],
        compiler_params=params,
        name="prepare",
    )(
        *[
            pltpu.with_memory_space_constraint(array, pltpu.HBM)
            for array in (
                forcing,
                zonal_courant,
                meridional_courant,
                zonal_faces,
                meridional_faces,
                jnp.swapaxes(coupling, 0, 1),
            )
        ]
    )

    def device(tm, space):
        return tm * strips + space % strips

    everyone = [(t, s) for t in range(tm_count) for s in range(strips)]
    partner = [(t, t ^ 1) for t in range(tm_count)]
    perm_a = [(device(t, s), device(t ^ 1, s + 1 if t % 2 else s - 1)) for t, s in everyone]
    perm_b = [(device(t, s), device(t, s - 1 if t % 2 else s + 1)) for t, s in everyone]
    got_f = lax.ppermute(send_f, "tm", partner)
    got_c = lax.ppermute(send_c, "tm", partner)
    got_a = lax.ppermute(pay_a, ("tm", "space"), perm_a)
    got_b = lax.ppermute(pay_b, ("tm", "space"), perm_b)

    def band_scratch(span):
        state = pltpu.VMEM((span + 2, z.fields, 2, SUB, z.lanes), F32)
        return [state] * 4

    def stencil(columns):
        return shape((columns // SUB + 2, 8, 2, SUB, z.lanes), F32)

    mixing = shape((z.fields**2, SUB, z.lanes), F32)

    def operator_scratch(columns):
        return [pltpu.VMEM(spec.shape, spec.dtype) for spec in (stencil(columns), mixing)]

    rows_f_shape = shape((2, z.steps, z.fields, 2, z.window, z.lanes), F32)
    rows_c_shape = shape((2, 5, 2, z.window, z.lanes), F32)
    half_dims = (z.fields, 2, z.own, z.lanes)
    def tiles(columns):
        return shape((z.fields, columns // SUB, 2 * SUB, z.lanes), BF16)

    rows_f, rows_c, inner, core = pl.pallas_call(
        functools.partial(inner_kernel, z, 1),
        out_shape=[rows_f_shape, rows_c_shape, shape((2, z.fields, 2, z.main, z.lanes), F32), tiles(z.core)],
        in_specs=in_vmem(4),
        out_specs=in_vmem(4),
        scratch_shapes=band_scratch(z.wide) + operator_scratch(z.main),
        compiler_params=params,
        cost_estimate=pl.CostEstimate(flops=10**9, bytes_accessed=2 * 10**7, transcendentals=0),
        name="inner",
    )(keep_f, got_f, keep_c, got_c)
    down = [(device(t, s), device(t ^ 2, s)) for t, s in everyone]
    across = [(device(t, s), device((t ^ 1) - 2, s + 1 if t % 2 else s - 1) if t >= 2 else device(t + 2, s)) for t, s in everyone]
    core = lax.ppermute(core, ("tm", "space"), down)
    rows_f, rows_c, kept, sent, edge, co_core, co_rim, co_late, mix_first, mix_last = pl.pallas_call(
        functools.partial(rim_kernel, z, 1),
        out_shape=[
            rows_f_shape,
            rows_c_shape,
            shape(half_dims, F32),
            shape(half_dims, F32),
            tiles(z.halo),
            stencil(z.core),
            stencil(z.rim),
            stencil(z.main - z.halo),
            mixing,
            mixing,
        ],
        in_specs=in_vmem(5),
        out_specs=in_vmem(10),
        input_output_aliases={3: 0, 4: 1},
        scratch_shapes=[
            pltpu.VMEM((2,) + half_dims, F32),
            pltpu.VMEM((z.fields, 2, z.rim, z.lanes), F32),
        ]
        + band_scratch(z.wide)
        + operator_scratch(z.rim),
        compiler_params=params,
        cost_estimate=pl.CostEstimate(flops=10**9, bytes_accessed=2 * 10**7, transcendentals=0),
        name="rim",
    )(got_a, got_b, inner, rows_f, rows_c)
    state = pl.pallas_call(
        functools.partial(early_kernel, z, 0),
        out_shape=shape((z.fields, 2, z.core + SUB, z.lanes), F32),
        in_specs=in_vmem(4),
        out_specs=pl.BlockSpec(memory_space=pltpu.VMEM),
        scratch_shapes=[pltpu.VMEM((z.fields, 2, z.core, z.lanes), F32)] + band_scratch(z.core // SUB),
        compiler_params=params,
        name="early",
    )(core, rows_f, co_core, mix_first)
    far = lax.ppermute(edge, ("tm", "space"), across)
    near = lax.ppermute(edge, ("tm", "space"), down)
    kept, sent = pl.pallas_call(
        functools.partial(late_kernel, z, 0),
        out_shape=[shape(half_dims, F32), shape(half_dims, F32)],
        in_specs=in_vmem(11),
        out_specs=in_vmem(2),
        input_output_aliases={9: 0, 10: 1},
        scratch_shapes=[
            pltpu.VMEM((2,) + half_dims, F32),
            pltpu.VMEM((z.fields, 2, z.main, z.lanes), F32),
        ]
        + band_scratch(z.narrow),
        compiler_params=params,
        name="late",
    )(core, near, far, state, rows_f, co_rim, mix_first, co_late, mix_last, kept, sent)
    got = lax.ppermute(sent, "tm", partner)
    return pl.pallas_call(
        functools.partial(finish_kernel, z),
        out_shape=shape((1, z.fields, z.rows, z.strip), F32),
        in_specs=in_vmem(2),
        out_specs=pl.BlockSpec(memory_space=pltpu.VMEM),
        compiler_params=params,
        name="finish",
    )(kept, got)


def solution(mesh):
    return jax.shard_map(
        per_device,
        mesh=mesh,
        in_specs=(
            P("tm", None, None, None, "space"),
            P("tm", None, "space"),
            P("tm", None, "space"),
            P("tm", None, "space"),
            P("tm", None, "space"),
            P("tm", None, None),
        ),
        out_specs=P("tm", None, None, "space"),
        check_vma=False,
    )
```

```python
import functools

import jax
import jax.numpy as jnp
from jax import lax
from jax.experimental import pallas as pl
from jax.experimental.pallas import tpu as pltpu
from jax.sharding import PartitionSpec as P

SWEEPS = 2
OMEGA = 0.4
SUB = 8
REACH = SWEEPS + 1
VMEM_BYTES = 20 * 2**20
F32 = jnp.float32
BF16 = jnp.bfloat16


class Sizes:
    def __init__(self, forcing_shape):
        _, self.steps, self.fields, self.rows, self.strip = forcing_shape
        self.lanes = self.rows // 2
        self.halo = 2 * REACH * self.steps
        self.main = self.strip // 2 + 2 * self.halo
        self.window = self.main + self.halo
        self.span = self.window // SUB
        self.shift = self.strip - self.main
        self.own = self.strip // 2
        self.depths = [REACH * (self.steps + k) for k in range(self.steps)]
        self.depth = self.depths[-1]
        self.starts = [self.fields * sum(self.depths[:k]) for k in range(self.steps)]
        self.coef_start = self.fields * sum(self.depths)
        self.payload = -(-(self.coef_start + 4 * self.depth) // SUB)
        self.message = self.own + self.halo
        self.core = self.message - self.halo
        self.wide, self.narrow = self.main // SUB, (self.main - self.halo) // SUB
        self.inset = self.halo // 2
        self.outer = 3 * self.halo
        self.rim = -(-3 * self.depth // SUB) * SUB
        self.rim_own = self.rim - 2 * self.depth
        self.base = -self.inset % SUB


def half_and_chip():
    tm = lax.axis_index("tm")
    return lax.rem(tm, 2), tm // 2


def prepare_kernel(z, fo_in, zc, mc, zf, mf, cp_in, keep_f, send_f, keep_c, send_c, pay_a, pay_b, fo, co, cp, buf, edges, sems):
    half, _ = half_and_chip()
    left = half == 0
    row = lax.broadcasted_iota(jnp.int32, (z.rows, z.strip), 0)
    coef_copies = [
        pltpu.make_async_copy(ref.at[0], co.at[c], sems.at[c]) for c, ref in enumerate((zf, mf, zc, mc))
    ]
    forcing_copies = [pltpu.make_async_copy(fo_in.at[0, k], fo.at[k], sems.at[5 + k]) for k in range(z.steps)]
    mixing_copy = pltpu.make_async_copy(cp_in, cp, sems.at[4])
    for copy in coef_copies + [mixing_copy] + forcing_copies:
        copy.start()

    def columns(values, slot):
        buf[slot] = values
        return [buf[slot, pl.ds(p, z.lanes, stride=2), :].T for p in range(2)]

    def split(both, depth, start, keep, send):
        for p in range(2):
            low, high = both[p][: z.main], both[p][z.shift :]
            keep[p] = jnp.where(left, low, high).astype(keep.dtype)
            send[p] = jnp.where(left, high, low).astype(send.dtype)
            edges[0, p, start : start + depth, :] = both[p][:depth]
            edges[1, p, start : start + depth, :] = both[p][z.strip - depth :]

    slots = buf.shape[0]
    count = 0
    for c in range(4):
        coef_copies[c].wait()
        values = co[c]
        if c == 1:
            values = jnp.where(row < z.rows - 1, values, jnp.zeros_like(values))
        both = columns(values, count % slots)
        split(both, z.depth, z.coef_start + c * z.depth, keep_c.at[c], send_c.at[c])
        count += 1
    mixing_copy.wait()
    for ref in (keep_c, send_c):
        for g in range(z.fields):
            ref[4, 0, g : g + 1, : z.fields] = cp[g]
    for k in range(z.steps):
        forcing_copies[k].wait()
        for f in range(z.fields):
            both = columns(fo[k, f].astype(F32), count % slots)
            split(both, z.depths[k], z.starts[k] + f * z.depths[k], keep_f.at[k, f], send_f.at[k, f])
            count += 1
    for g in range(z.payload):
        at = slice(SUB * g, SUB * (g + 1))
        west, east = (jnp.concatenate([edges[n, p, at, :] for p in range(2)], axis=0) for n in range(2))
        pay_a[g] = jnp.where(left, west, east).astype(BF16)
        pay_b[g] = jnp.where(left, east, west).astype(BF16)


def fill_ghosts(ref, span, count):
    for n in range(count):
        for p in range(2):
            ref[0, n, p] = pltpu.roll(ref[span, n, p], 1, 0)
            ref[span + 1, n, p] = pltpu.roll(ref[1, n, p], SUB - 1, 0)


class Band:
    def __init__(self, z, scratch):
        self.z = z
        self.r, self.u1, self.u2, self.pz, self.co, self.kk = scratch
        self.lane = lax.broadcasted_iota(jnp.int32, (SUB, z.lanes), 1)

    def east(self, v):
        return pltpu.roll(v, 1, 1)

    def west(self, v):
        return pltpu.roll(v, self.z.lanes - 1, 1)

    def set_operators(self, rows_c, q, offset, span):
        z, u1, co = self.z, self.u1, self.co
        for c in range(4):
            for p in range(2):
                for i in range(span):
                    u1[i + 1, c, p] = rows_c[q, c, p, pl.ds(offset + i, SUB, stride=span), :]
        fill_ghosts(u1, span, 1)
        for i in range(1, span + 1):
            be, bo = u1[i, 1, 0], u1[i, 1, 1]
            south = (self.east(bo), be)
            for p in range(2):
                a, aw, b = u1[i, 0, p], u1[i - 1, 0, p], u1[i, 1, p]
                centre = 1.0 - OMEGA * (1.0 + (a + aw) + (b + south[p]))
                co[i, 0, p] = centre
                co[i, 7, p] = 1.0 + centre
                co[i, 1, p] = OMEGA * a
                co[i, 2, p] = OMEGA * aw
                co[i, 3, p] = OMEGA * b
                co[i, 4, p] = OMEGA * south[p]
                co[i, 5, p] = (0.5 * OMEGA) * u1[i, 2, p]
                co[i, 6, p] = (0.5 * OMEGA) * u1[i, 3, p]
        for g in range(z.fields):
            for f in range(z.fields):
                value = rows_c[q, 4, 0, g : g + 1, f : f + 1]
                if f == g:
                    value = value + 1.0
                self.kk[g * z.fields + f] = jnp.broadcast_to(OMEGA * value, (SUB, z.lanes))

    def load(self, at, offset, span):
        for i in range(span):
            for f in range(self.z.fields):
                for p in range(2):
                    self.r[i + 1, f, p] = at[f, p, pl.ds(offset + i, SUB, stride=span), :]

    def store(self, at, span, base=0):
        for i in range(span):
            for f in range(self.z.fields):
                for p in range(2):
                    at[f, p, pl.ds(base + i, SUB, stride=span), :] = self.r[i + 1, f, p]

    def sweep(self, src, dst, i, source):
        co = self.co
        first = 7 if source is None else 0
        ga = [co[i, c, 0] for c in (first, 1, 2, 3, 4)]
        gb = [co[i, c, 1] for c in (first, 1, 2, 3, 4)]
        for f in range(self.z.fields):
            a, b = src[i, f, 0], src[i, f, 1]
            va = ga[0] * a + ga[1] * src[i + 1, f, 0] + ga[2] * src[i - 1, f, 0] + ga[3] * b + ga[4] * self.east(b)
            vb = gb[0] * b + gb[1] * src[i + 1, f, 1] + gb[2] * src[i - 1, f, 1] + gb[3] * self.west(a) + gb[4] * a
            if source is not None:
                va = va + source[i, f, 0]
                vb = vb + source[i, f, 1]
                self.pz[i, f, 0] = co[i, 5, 0] * va
                self.pz[i, f, 1] = co[i, 5, 1] * vb
            dst[i, f, 0] = va
            dst[i, f, 1] = vb

    def step(self, forcing, offset, span):
        z, r, u1, u2, pz, co, kk = self.z, self.r, self.u1, self.u2, self.pz, self.co, self.kk
        zero = jnp.zeros((SUB, z.lanes), F32)
        fill_ghosts(r, span, z.fields)
        for i in range(1, span + 1):
            self.sweep(r, u1, i, None)
        fill_ghosts(u1, span, z.fields)
        for i in range(1, span + 1):
            self.sweep(u1, u2, i, r)
        fill_ghosts(pz, span, z.fields)
        for i in range(1, span + 1):
            us = [[u2[i, g, p] for p in range(2)] for g in range(z.fields)]
            for f in range(z.fields):
                qa, qb = co[i, 6, 0] * us[f][0], co[i, 6, 1] * us[f][1]
                qba = jnp.where(self.lane == 0, zero, self.east(qb))
                qab = jnp.where(self.lane == z.lanes - 1, zero, self.west(qa))
                oa = (pz[i + 1, f, 0] - pz[i - 1, f, 0]) + (qb - qba)
                ob = (pz[i + 1, f, 1] - pz[i - 1, f, 1]) + (qab - qa)
                for g in range(z.fields):
                    w = kk[g * z.fields + f]
                    oa = oa + w * us[g][0]
                    ob = ob + w * us[g][1]
                rows = pl.ds(offset + i - 1, SUB, stride=span)
                r[i, f, 0] = oa + forcing[f, 0, rows, :]
                r[i, f, 1] = ob + forcing[f, 1, rows, :]

    def steps(self, rows_f, q, begin, offset, span):
        last = self.z.steps - 1

        def one(n, carry):
            self.step(rows_f.at[q, last - n], offset, span)
            return carry

        lax.fori_loop(begin, last + 1, one, 0)


def aligned(offset, count):
    return pl.ds(pl.multiple_of(offset, SUB), count)


def tile_of(ref, f, at):
    return jnp.concatenate([ref[f, p, at, :] for p in range(2)], axis=0).astype(BF16)


def inner_kernel(z, active, kf, rf, kc, rc, rows_f, rows_c, inner, core, *scratch):
    half, chip = half_and_chip()
    main_at = z.halo * (1 - half)
    blank = jnp.zeros((z.halo, z.lanes), F32)

    def put(ref, values):
        ref[aligned(main_at, z.main), :] = values.astype(F32)
        ref[aligned(z.main * half, z.halo), :] = blank

    for q, forcing, coefs in ((1 - half, kf, kc), (half, rf, rc)):
        for c in range(4):
            for p in range(2):
                put(rows_c.at[q, c, p], coefs[c, p])
        rows_c[q, 4, 0, :SUB, :] = coefs[4, 0, :SUB, :]
        for k in range(z.steps):
            for f in range(z.fields):
                for p in range(2):
                    put(rows_f.at[q, k, f, p], forcing[k, f, p])

    @pl.when(chip == active)
    def _():
        band = Band(z, scratch)
        span = z.main // SUB
        band.load(rows_f.at[0, z.steps - 1], main_at, span)
        band.set_operators(rows_c, 0, main_at, span)
        band.steps(rows_f, 0, 1, main_at, span)
        band.store(inner.at[0], span)
        cut = REACH * (z.steps - 1) // SUB * SUB
        span -= 2 * cut // SUB
        band.load(inner.at[0], cut, span)
        band.set_operators(rows_c, 1, main_at + cut, span)
        band.steps(rows_f, 1, 0, main_at + cut, span)
        band.store(inner.at[1], span, cut)
        for f in range(z.fields):
            for g in range(z.core // SUB):
                core[f, g] = tile_of(inner.at[1], f, slice(z.halo + SUB * g, z.halo + SUB * (g + 1)))


def rim_kernel(z, active, ra, rb, inner, rows_f_in, rows_c_in, rows_f, rows_c, ko, so, edge, *refs):
    late_operators, (obuf, tmp, edges), scratch = refs[:5], refs[5:8], refs[8:]
    half, chip = half_and_chip()
    for n, pay in enumerate((ra, rb)):
        for g in range(z.payload):
            tile = pay[g].astype(F32)
            for p in range(2):
                edges[n, p, SUB * g : SUB * (g + 1), :] = tile[SUB * p : SUB * (p + 1)]

    def place_edges(side):
        for n, q in ((0, side), (1, 1 - side)):
            blocks = [(rows_c.at[q, c], z.coef_start + c * z.depth, z.depth) for c in range(4)]
            for k in range(z.steps):
                for f in range(z.fields):
                    blocks.append((rows_f.at[q, k, f], z.starts[k] + f * z.depths[k], z.depths[k]))
            for ref, start, depth in blocks:
                at = z.main if side else z.halo - depth
                for p in range(2):
                    ref[p, at : at + depth, :] = edges[n, p, start : start + depth, :]

    for side in range(2):
        pl.when(half == side)(functools.partial(place_edges, side))

    @pl.when(chip != active)
    def _():
        co_core, co_rim, co_late, mix_first, mix_last = late_operators
        for q, co, mix, columns, offset in (
            (0, co_core, mix_first, z.core, z.halo * (2 - half)),
            (0, co_rim, mix_first, z.outer, (z.window - z.outer) * half),
            (1, co_late, mix_last, z.main - z.halo, z.halo * half + z.inset),
        ):
            Band(z, scratch[:4] + (co, mix)).set_operators(rows_c, q, offset, columns // SUB)

    @pl.when(chip == active)
    def _():
        band = Band(z, scratch)
        start = z.halo - z.depth
        offset = start + (z.main + z.depth - z.rim - start) * half
        base = start + (2 * z.halo + z.depth - z.rim - start) * half
        sublane = lax.broadcasted_iota(jnp.int32, (SUB, z.lanes), 0)
        mine = []
        for g in range(z.halo // SUB):
            at = sublane + SUB * g
            mine.append(jnp.where(half == 0, at, z.halo - 1 - at) < z.rim_own)

        def keep(q):
            place = jnp.where(half == q, 1, 0)
            for f in range(z.fields):
                merged = []
                for p in range(2):
                    obuf[place, f, p] = inner[q, f, p, aligned((z.main - z.own) * half, z.own), :]
                    for g in range(z.halo // SUB):
                        rim = tmp[f, p, z.halo + SUB * g : z.halo + SUB * (g + 1), :]
                        own = inner[q, f, p, aligned((z.main - z.halo) * half + SUB * g, SUB), :]
                        merged.append(jnp.where(mine[g], rim, own))
                        obuf[place, f, p, aligned((z.own - z.halo) * half + SUB * g, SUB), :] = merged[-1]
                if q == 1:
                    for g in range(z.halo // SUB):
                        edge[f, g] = jnp.concatenate([merged[g], merged[g + z.halo // SUB]], axis=0).astype(BF16)

        band.load(rows_f.at[0, z.steps - 1], offset, z.rim // SUB)
        band.set_operators(rows_c, 0, offset, z.rim // SUB)
        band.steps(rows_f, 0, 1, offset, z.rim // SUB)
        band.store(tmp, z.rim // SUB, base)
        keep(0)
        offset = z.inset + (z.main - 2 * z.halo) * half
        band.load(tmp, z.inset, 2 * z.halo // SUB)
        band.set_operators(rows_c, 1, offset, 2 * z.halo // SUB)
        band.steps(rows_f, 1, 0, offset, 2 * z.halo // SUB)
        band.store(tmp, 2 * z.halo // SUB, z.inset)
        keep(1)
        ko[...] = obuf[0]
        so[...] = obuf[1]


def put_tiles(z, tmp, tiles, at):
    for f in range(z.fields):
        for n, tile in enumerate(tiles(f)):
            for p in range(2):
                tmp[f, p, aligned(at + SUB * n, SUB), :] = tile.astype(F32)[SUB * p : SUB * (p + 1)]


def early_kernel(z, active, core, rows_f, co, mix, state, tmp, *scratch):
    half, chip = half_and_chip()

    @pl.when(chip == active)
    def _():
        band = Band(z, scratch + (co, mix))
        span = z.core // SUB
        put_tiles(z, tmp, lambda f: [core[f, g] for g in range(z.core // SUB)], 0)
        band.load(tmp, 0, span)
        band.steps(rows_f, 0, 0, z.halo * (2 - half), span)
        band.store(state, span, z.base)


def late_kernel(
    z, active, core, near, far, state, rows_f, co_rim, mix_first, co_late, mix_last, ko_in, so_in, ko, so, obuf, tmp, *scratch
):
    half, chip = half_and_chip()

    @pl.when(chip == active)
    def _():
        groups = z.halo // SUB
        span = z.outer // SUB
        put_tiles(z, tmp, lambda f: [far[f, g] for g in range(groups)], 2 * z.halo * half)
        put_tiles(z, tmp, lambda f: [near[f, g] for g in range(groups)], z.halo)
        first = (z.core // SUB - groups) * half
        put_tiles(z, tmp, lambda f: [core[f, first + g] for g in range(groups)], 2 * z.halo * (1 - half))
        band = Band(z, scratch + (co_rim, mix_first))
        band.load(tmp, 0, span)
        band.steps(rows_f, 0, 0, (z.window - z.outer) * half, span)
        band.store(tmp, span, z.base)
        outer, inner = 2 * z.halo, z.core - z.halo
        start = z.inset + z.base
        for f in range(z.fields):
            for p in range(2):
                rim = tmp[f, p, start : start + outer, :]
                tmp[f, p, aligned(inner * half, outer), :] = rim
                tmp[f, p, aligned(outer * (1 - half), inner), :] = state[f, p, start : start + inner, :]
                obuf[1 - half, f, p] = tmp[f, p, z.inset : z.inset + z.own, :]
        band = Band(z, scratch + (co_late, mix_last))
        band.load(tmp, 0, z.narrow)
        band.steps(rows_f, 1, 0, z.halo * half + z.inset, z.narrow)
        band.store(tmp, z.narrow)
        for f in range(z.fields):
            for p in range(2):
                obuf[half, f, p] = tmp[f, p, z.inset : z.inset + z.own, :]
        ko[...] = obuf[0]
        so[...] = obuf[1]


def finish_kernel(z, keep, got, out):
    half, _ = half_and_chip()
    for f in range(z.fields):
        for p in range(2):
            a, b = keep[f, p], got[f, p]
            west = jnp.where(half == 0, a, b)
            east = jnp.where(half == 0, b, a)
            out[0, f, pl.ds(p, z.lanes, stride=2), :] = jnp.concatenate([west, east], axis=0).T


def shape(dims, dtype):
    return jax.ShapeDtypeStruct(tuple(dims), dtype)


def in_vmem(count):
    return [pl.BlockSpec(memory_space=pltpu.VMEM)] * count


def in_hbm(count):
    return [pl.BlockSpec(memory_space=pltpu.HBM)] * count


def per_device(forcing, zonal_courant, meridional_courant, zonal_faces, meridional_faces, coupling):
    z = Sizes(forcing.shape)
    tm_count, strips = lax.axis_size("tm"), lax.axis_size("space")
    assert tm_count == 4 and z.main % 16 == 0 and z.shift % 16 == 0
    params = pltpu.CompilerParams(vmem_limit_bytes=VMEM_BYTES)
    f_shape = (z.steps, z.fields, 2, z.main, z.lanes)
    c_shape = (5, 2, z.main, z.lanes)
    pay_shape = (z.payload, 2 * SUB, z.lanes)
    keep_f, send_f, keep_c, send_c, pay_a, pay_b = pl.pallas_call(
        functools.partial(prepare_kernel, z),
        out_shape=[
            shape(f_shape, BF16),
            shape(f_shape, BF16),
            shape(c_shape, F32),
            shape(c_shape, F32),
            shape(pay_shape, BF16),
            shape(pay_shape, BF16),
        ],
        in_specs=in_hbm(6),
        out_specs=in_vmem(6),
        scratch_shapes=[
            pltpu.VMEM(forcing.shape[1:], BF16),
            pltpu.VMEM((4, z.rows, z.strip), F32),
            pltpu.VMEM((z.fields, 1, z.fields), F32),
            pltpu.VMEM((4, z.rows, z.strip), F32),
            pltpu.VMEM((2, 2, SUB * z.payload, z.lanes), F32),
            pltpu.SemaphoreType.DMA((5 + z.steps,)),
        ],
        compiler_params=params,
        name="prepare",
    )(
        *[
            pltpu.with_memory_space_constraint(array, pltpu.HBM)
            for array in (
                forcing,
                zonal_courant,
                meridional_courant,
                zonal_faces,
                meridional_faces,
                jnp.swapaxes(coupling, 0, 1),
            )
        ]
    )

    def device(tm, space):
        return tm * strips + space % strips

    everyone = [(t, s) for t in range(tm_count) for s in range(strips)]
    partner = [(t, t ^ 1) for t in range(tm_count)]
    perm_a = [(device(t, s), device(t ^ 1, s + 1 if t % 2 else s - 1)) for t, s in everyone]
    perm_b = [(device(t, s), device(t, s - 1 if t % 2 else s + 1)) for t, s in everyone]
    got_f = lax.ppermute(send_f, "tm", partner)
    got_c = lax.ppermute(send_c, "tm", partner)
    got_a = lax.ppermute(pay_a, ("tm", "space"), perm_a)
    got_b = lax.ppermute(pay_b, ("tm", "space"), perm_b)

    def band_scratch(span):
        state = pltpu.VMEM((span + 2, z.fields, 2, SUB, z.lanes), F32)
        return [state] * 4

    def stencil(columns):
        return shape((columns // SUB + 2, 8, 2, SUB, z.lanes), F32)

    mixing = shape((z.fields**2, SUB, z.lanes), F32)

    def operator_scratch(columns):
        return [pltpu.VMEM(spec.shape, spec.dtype) for spec in (stencil(columns), mixing)]

    rows_f_shape = shape((2, z.steps, z.fields, 2, z.window, z.lanes), F32)
    rows_c_shape = shape((2, 5, 2, z.window, z.lanes), F32)
    half_dims = (z.fields, 2, z.own, z.lanes)
    def tiles(columns):
        return shape((z.fields, columns // SUB, 2 * SUB, z.lanes), BF16)

    rows_f, rows_c, inner, core = pl.pallas_call(
        functools.partial(inner_kernel, z, 1),
        out_shape=[rows_f_shape, rows_c_shape, shape((2, z.fields, 2, z.main, z.lanes), F32), tiles(z.core)],
        in_specs=in_vmem(4),
        out_specs=in_vmem(4),
        scratch_shapes=band_scratch(z.wide) + operator_scratch(z.main),
        compiler_params=params,
        cost_estimate=pl.CostEstimate(flops=10**9, bytes_accessed=2 * 10**7, transcendentals=0),
        name="inner",
    )(keep_f, got_f, keep_c, got_c)
    down = [(device(t, s), device(t ^ 2, s)) for t, s in everyone]
    across = [(device(t, s), device((t ^ 1) - 2, s + 1 if t % 2 else s - 1) if t >= 2 else device(t + 2, s)) for t, s in everyone]
    core = lax.ppermute(core, ("tm", "space"), down)
    rows_f, rows_c, kept, sent, edge, co_core, co_rim, co_late, mix_first, mix_last = pl.pallas_call(
        functools.partial(rim_kernel, z, 1),
        out_shape=[
            rows_f_shape,
            rows_c_shape,
            shape(half_dims, F32),
            shape(half_dims, F32),
            tiles(z.halo),
            stencil(z.core),
            stencil(z.outer),
            stencil(z.main - z.halo),
            mixing,
            mixing,
        ],
        in_specs=in_vmem(5),
        out_specs=in_vmem(10),
        input_output_aliases={3: 0, 4: 1},
        scratch_shapes=[
            pltpu.VMEM((2,) + half_dims, F32),
            pltpu.VMEM((z.fields, 2, z.rim + SUB, z.lanes), F32),
            pltpu.VMEM((2, 2, SUB * z.payload, z.lanes), F32),
        ]
        + band_scratch(z.wide)
        + operator_scratch(z.rim),
        compiler_params=params,
        cost_estimate=pl.CostEstimate(flops=10**9, bytes_accessed=2 * 10**7, transcendentals=0),
        name="rim",
    )(got_a, got_b, inner, rows_f, rows_c)
    state = pl.pallas_call(
        functools.partial(early_kernel, z, 0),
        out_shape=shape((z.fields, 2, z.core + SUB, z.lanes), F32),
        in_specs=in_vmem(4),
        out_specs=pl.BlockSpec(memory_space=pltpu.VMEM),
        scratch_shapes=[pltpu.VMEM((z.fields, 2, z.core, z.lanes), F32)] + band_scratch(z.core // SUB),
        compiler_params=params,
        name="early",
    )(core, rows_f, co_core, mix_first)
    far = lax.ppermute(edge, ("tm", "space"), across)
    near = lax.ppermute(edge, ("tm", "space"), down)
    kept, sent = pl.pallas_call(
        functools.partial(late_kernel, z, 0),
        out_shape=[shape(half_dims, F32), shape(half_dims, F32)],
        in_specs=in_vmem(11),
        out_specs=in_vmem(2),
        input_output_aliases={9: 0, 10: 1},
        scratch_shapes=[
            pltpu.VMEM((2,) + half_dims, F32),
            pltpu.VMEM((z.fields, 2, z.main, z.lanes), F32),
        ]
        + band_scratch(z.narrow),
        compiler_params=params,
        name="late",
    )(core, near, far, state, rows_f, co_rim, mix_first, co_late, mix_last, kept, sent)
    got = lax.ppermute(sent, "tm", partner)
    return pl.pallas_call(
        functools.partial(finish_kernel, z),
        out_shape=shape((1, z.fields, z.rows, z.strip), F32),
        in_specs=in_vmem(2),
        out_specs=pl.BlockSpec(memory_space=pltpu.VMEM),
        compiler_params=params,
        name="finish",
    )(kept, got)


def solution(mesh):
    return jax.shard_map(
        per_device,
        mesh=mesh,
        in_specs=(
            P("tm", None, None, None, "space"),
            P("tm", None, "space"),
            P("tm", None, "space"),
            P("tm", None, "space"),
            P("tm", None, "space"),
            P("tm", None, None),
        ),
        out_specs=P("tm", None, None, "space"),
        check_vma=False,
    )
```

```python
import functools

import jax
import jax.numpy as jnp
from jax import lax
from jax.experimental import pallas as pl
from jax.experimental.pallas import tpu as pltpu
from jax.sharding import PartitionSpec as P

SWEEPS = 2
OMEGA = 0.4
SUB = 8
REACH = SWEEPS + 1
VMEM_BYTES = 20 * 2**20
F32 = jnp.float32
BF16 = jnp.bfloat16


class Sizes:
    def __init__(self, forcing_shape):
        _, self.steps, self.fields, self.rows, self.strip = forcing_shape
        self.lanes = self.rows // 2
        self.halo = 2 * REACH * self.steps
        self.main = self.strip // 2 + 2 * self.halo
        self.window = self.main + self.halo
        self.span = self.window // SUB
        self.shift = self.strip - self.main
        self.own = self.strip // 2
        self.depths = [REACH * (self.steps + k) for k in range(self.steps)]
        self.depth = self.depths[-1]
        self.starts = [self.fields * sum(self.depths[:k]) for k in range(self.steps)]
        self.coef_start = self.fields * sum(self.depths)
        self.coef_depths = [self.halo - c for c in range(4)]
        self.coef_starts = [self.coef_start + sum(self.coef_depths[:c]) for c in range(4)]
        self.payload = -(-(self.coef_start + sum(self.coef_depths)) // SUB)
        self.message = self.own + self.halo
        self.core = self.message - self.halo
        self.wide, self.narrow = self.main // SUB, (self.main - self.halo) // SUB
        self.inset = self.halo // 2
        self.outer = 3 * self.halo
        self.rim = -(-3 * self.depth // SUB) * SUB
        self.rim_own = self.rim - 2 * self.depth
        self.base = -self.inset % SUB


def half_and_chip():
    tm = lax.axis_index("tm")
    return lax.rem(tm, 2), tm // 2


def prepare_kernel(z, fo_in, zc, mc, zf, mf, cp_in, keep_f, send_f, keep_c, send_c, pay_a, pay_b, fo, co, cp, buf, edges, sems):
    half, _ = half_and_chip()
    left = half == 0
    row = lax.broadcasted_iota(jnp.int32, (z.rows, z.strip), 0)
    coef_copies = [
        pltpu.make_async_copy(ref.at[0], co.at[c], sems.at[c]) for c, ref in enumerate((zf, mf, zc, mc))
    ]
    part = z.fields // 2
    forcing_copies = []
    for n in range(2 * z.steps):
        block = (n // 2, pl.ds(n % 2 * part, part))
        forcing_copies.append(pltpu.make_async_copy(fo_in.at[(0, *block)], fo.at[block], sems.at[5 + n]))
    mixing_copy = pltpu.make_async_copy(cp_in, cp, sems.at[4])
    for copy in coef_copies + [mixing_copy] + forcing_copies:
        copy.start()

    def columns(values, slot):
        buf[slot] = values
        return [buf[slot, pl.ds(p, z.lanes, stride=2), :].T for p in range(2)]

    def split(both, depth, start, keep, send):
        for p in range(2):
            low, high = both[p][: z.main], both[p][z.shift :]
            keep[p] = jnp.where(left, low, high).astype(keep.dtype)
            send[p] = jnp.where(left, high, low).astype(send.dtype)
            edges[0, p, start : start + depth, :] = both[p][:depth]
            edges[1, p, start : start + depth, :] = both[p][z.strip - depth :]

    slots = buf.shape[0]
    count = 0
    for c in range(4):
        coef_copies[c].wait()
        values = co[c]
        if c == 1:
            values = jnp.where(row < z.rows - 1, values, jnp.zeros_like(values))
        both = columns(values, count % slots)
        split(both, z.coef_depths[c], z.coef_starts[c], keep_c.at[c], send_c.at[c])
        count += 1
    mixing_copy.wait()
    for ref in (keep_c, send_c):
        for g in range(z.fields):
            ref[4, 0, g : g + 1, : z.fields] = cp[g]
    for k in range(z.steps):
        for f in range(z.fields):
            if f % part == 0:
                forcing_copies[2 * k + f // part].wait()
            both = columns(fo[k, f].astype(F32), count % slots)
            split(both, z.depths[k], z.starts[k] + f * z.depths[k], keep_f.at[k, f], send_f.at[k, f])
            count += 1
    for g in range(z.payload):
        at = slice(SUB * g, SUB * (g + 1))
        west, east = (jnp.concatenate([edges[n, p, at, :] for p in range(2)], axis=0) for n in range(2))
        pay_a[g] = jnp.where(left, west, east).astype(BF16)
        pay_b[g] = jnp.where(left, east, west).astype(BF16)


def fill_ghosts(ref, span, count):
    for n in range(count):
        for p in range(2):
            ref[0, n, p] = pltpu.roll(ref[span, n, p], 1, 0)
            ref[span + 1, n, p] = pltpu.roll(ref[1, n, p], SUB - 1, 0)


class Band:
    def __init__(self, z, scratch):
        self.z = z
        self.r, self.u1, self.u2, self.pz, self.co, self.kk = scratch
        self.lane = lax.broadcasted_iota(jnp.int32, (SUB, z.lanes), 1)

    def east(self, v):
        return pltpu.roll(v, 1, 1)

    def west(self, v):
        return pltpu.roll(v, self.z.lanes - 1, 1)

    def set_operators(self, rows_c, q, offset, span):
        z, u1, co = self.z, self.u1, self.co
        for c in range(4):
            for p in range(2):
                for i in range(span):
                    u1[i + 1, c, p] = rows_c[q, c, p, pl.ds(offset + i, SUB, stride=span), :]
        fill_ghosts(u1, span, 1)
        for i in range(1, span + 1):
            be, bo = u1[i, 1, 0], u1[i, 1, 1]
            south = (self.east(bo), be)
            for p in range(2):
                a, aw, b = u1[i, 0, p], u1[i - 1, 0, p], u1[i, 1, p]
                centre = 1.0 - OMEGA * (1.0 + (a + aw) + (b + south[p]))
                co[i, 0, p] = centre
                co[i, 7, p] = 1.0 + centre
                co[i, 1, p] = OMEGA * a
                co[i, 2, p] = OMEGA * aw
                co[i, 3, p] = OMEGA * b
                co[i, 4, p] = OMEGA * south[p]
                co[i, 5, p] = (0.5 * OMEGA) * u1[i, 2, p]
                co[i, 6, p] = (0.5 * OMEGA) * u1[i, 3, p]

    def load(self, at, offset, span):
        for i in range(span):
            for f in range(self.z.fields):
                for p in range(2):
                    self.r[i + 1, f, p] = at[f, p, pl.ds(offset + i, SUB, stride=span), :]

    def store(self, at, span, base=0):
        for i in range(span):
            for f in range(self.z.fields):
                for p in range(2):
                    at[f, p, pl.ds(base + i, SUB, stride=span), :] = self.r[i + 1, f, p]

    def sweep(self, src, dst, i, source):
        co = self.co
        first = 7 if source is None else 0
        ga = [co[i, c, 0] for c in (first, 1, 2, 3, 4)]
        gb = [co[i, c, 1] for c in (first, 1, 2, 3, 4)]
        for f in range(self.z.fields):
            a, b = src[i, f, 0], src[i, f, 1]
            va = ga[0] * a + ga[1] * src[i + 1, f, 0] + ga[2] * src[i - 1, f, 0] + ga[3] * b + ga[4] * self.east(b)
            vb = gb[0] * b + gb[1] * src[i + 1, f, 1] + gb[2] * src[i - 1, f, 1] + gb[3] * self.west(a) + gb[4] * a
            if source is not None:
                va = va + source[i, f, 0]
                vb = vb + source[i, f, 1]
                self.pz[i, f, 0] = co[i, 5, 0] * va
                self.pz[i, f, 1] = co[i, 5, 1] * vb
            dst[i, f, 0] = va
            dst[i, f, 1] = vb

    def step(self, forcing, offset, span):
        z, r, u1, u2, pz, co, kk = self.z, self.r, self.u1, self.u2, self.pz, self.co, self.kk
        zero = jnp.zeros((SUB, z.lanes), F32)
        fill_ghosts(r, span, z.fields)
        for i in range(1, span + 1):
            self.sweep(r, u1, i, None)
        fill_ghosts(u1, span, z.fields)
        for i in range(1, span + 1):
            self.sweep(u1, u2, i, r)
        fill_ghosts(pz, span, z.fields)
        for i in range(1, span + 1):
            us = [[u2[i, g, p] for p in range(2)] for g in range(z.fields)]
            for f in range(z.fields):
                qa, qb = co[i, 6, 0] * us[f][0], co[i, 6, 1] * us[f][1]
                qba = jnp.where(self.lane == 0, zero, self.east(qb))
                qab = jnp.where(self.lane == z.lanes - 1, zero, self.west(qa))
                oa = (pz[i + 1, f, 0] - pz[i - 1, f, 0]) + (qb - qba)
                ob = (pz[i + 1, f, 1] - pz[i - 1, f, 1]) + (qab - qa)
                for g in range(z.fields):
                    w = kk[g * z.fields + f]
                    oa = oa + w * us[g][0]
                    ob = ob + w * us[g][1]
                rows = pl.ds(offset + i - 1, SUB, stride=span)
                r[i, f, 0] = oa + forcing[f, 0, rows, :]
                r[i, f, 1] = ob + forcing[f, 1, rows, :]

    def steps(self, rows_f, q, begin, offset, span):
        last = self.z.steps - 1

        def one(n, carry):
            self.step(rows_f.at[q, last - n], offset, span)
            return carry

        lax.fori_loop(begin, last + 1, one, 0)


def set_mixing(z, mix, table):
    for g in range(z.fields):
        for f in range(z.fields):
            value = table[g : g + 1, f : f + 1]
            if f == g:
                value = value + 1.0
            mix[g * z.fields + f] = jnp.broadcast_to(OMEGA * value, (SUB, z.lanes))


def aligned(offset, count):
    return pl.ds(pl.multiple_of(offset, SUB), count)


def tile_of(ref, f, at):
    return jnp.concatenate([ref[f, p, at, :] for p in range(2)], axis=0).astype(BF16)


def inner_kernel(z, active, kf, rf, kc, rc, rows_f, rows_c, inner, core, mix_first, mix_last, *scratch):
    half, chip = half_and_chip()
    *scratch, tables = scratch
    main_at = z.halo * (1 - half)
    blank = jnp.zeros((z.halo, z.lanes), F32)

    def put(ref, values):
        ref[aligned(main_at, z.main), :] = values.astype(F32)
        ref[aligned(z.main * half, z.halo), :] = blank

    for q, forcing, coefs in ((1 - half, kf, kc), (half, rf, rc)):
        for c in range(4):
            for p in range(2):
                put(rows_c.at[q, c, p], coefs[c, p])
        tables[q, :, :] = coefs[4, 0, :SUB, :]
        for k in range(z.steps):
            for f in range(z.fields):
                for p in range(2):
                    put(rows_f.at[q, k, f, p], forcing[k, f, p])

    set_mixing(z, mix_first, tables.at[0])
    set_mixing(z, mix_last, tables.at[1])

    @pl.when(chip == active)
    def _():
        band = Band(z, (*scratch, mix_first))
        span = z.main // SUB
        band.load(rows_f.at[0, z.steps - 1], main_at, span)
        band.set_operators(rows_c, 0, main_at, span)
        band.steps(rows_f, 0, 1, main_at, span)
        band.store(inner.at[0], span)
        cut = REACH * (z.steps - 1) // SUB * SUB
        span -= 2 * cut // SUB
        band = Band(z, (*scratch, mix_last))
        band.load(inner.at[0], cut, span)
        band.set_operators(rows_c, 1, main_at + cut, span)
        band.steps(rows_f, 1, 0, main_at + cut, span)
        band.store(inner.at[1], span, cut)
        for f in range(z.fields):
            for g in range(z.core // SUB):
                core[f, g] = tile_of(inner.at[1], f, slice(z.halo + SUB * g, z.halo + SUB * (g + 1)))


def rim_kernel(z, active, ra, rb, inner, mix_first, mix_last, rows_f_in, rows_c_in, rows_f, rows_c, ko, so, edge, *refs):
    (co_core, co_rim, co_late), (obuf, tmp, edges), scratch = refs[:3], refs[3:6], refs[6:]
    half, chip = half_and_chip()
    for n, pay in enumerate((ra, rb)):
        for g in range(z.payload):
            tile = pay[g].astype(F32)
            for p in range(2):
                edges[n, p, SUB * g : SUB * (g + 1), :] = tile[SUB * p : SUB * (p + 1)]

    def place_edges(side):
        for n, q in ((0, side), (1, 1 - side)):
            blocks = [(rows_c.at[q, c], z.coef_starts[c], z.coef_depths[c]) for c in range(4)]
            for k in range(z.steps):
                for f in range(z.fields):
                    blocks.append((rows_f.at[q, k, f], z.starts[k] + f * z.depths[k], z.depths[k]))
            for ref, start, depth in blocks:
                at = z.main if side else z.halo - depth
                for p in range(2):
                    ref[p, at : at + depth, :] = edges[n, p, start : start + depth, :]

    for side in range(2):
        pl.when(half == side)(functools.partial(place_edges, side))

    @pl.when(chip != active)
    def _():
        for q, co, mix, columns, offset in (
            (0, co_core, mix_first, z.core, z.halo * (2 - half)),
            (0, co_rim, mix_first, z.outer, (z.window - z.outer) * half),
            (1, co_late, mix_last, z.main - z.halo, z.halo * half + z.inset),
        ):
            Band(z, (*scratch[:4], co, mix)).set_operators(rows_c, q, offset, columns // SUB)

    @pl.when(chip == active)
    def _():
        band = Band(z, (*scratch, mix_first))
        start = z.halo - z.depth
        offset = start + (z.main + z.depth - z.rim - start) * half
        base = start + (2 * z.halo + z.depth - z.rim - start) * half
        sublane = lax.broadcasted_iota(jnp.int32, (SUB, z.lanes), 0)
        mine = []
        for g in range(z.halo // SUB):
            at = sublane + SUB * g
            mine.append(jnp.where(half == 0, at, z.halo - 1 - at) < z.rim_own)

        def keep(q):
            place = jnp.where(half == q, 1, 0)
            for f in range(z.fields):
                merged = []
                for p in range(2):
                    obuf[place, f, p] = inner[q, f, p, aligned((z.main - z.own) * half, z.own), :]
                    for g in range(z.halo // SUB):
                        rim = tmp[f, p, z.halo + SUB * g : z.halo + SUB * (g + 1), :]
                        own = inner[q, f, p, aligned((z.main - z.halo) * half + SUB * g, SUB), :]
                        merged.append(jnp.where(mine[g], rim, own))
                        obuf[place, f, p, aligned((z.own - z.halo) * half + SUB * g, SUB), :] = merged[-1]
                if q == 1:
                    for g in range(z.halo // SUB):
                        edge[f, g] = jnp.concatenate([merged[g], merged[g + z.halo // SUB]], axis=0).astype(BF16)

        band.load(rows_f.at[0, z.steps - 1], offset, z.rim // SUB)
        band.set_operators(rows_c, 0, offset, z.rim // SUB)
        band.steps(rows_f, 0, 1, offset, z.rim // SUB)
        band.store(tmp, z.rim // SUB, base)
        keep(0)
        band = Band(z, (*scratch, mix_last))
        offset = z.inset + (z.main - 2 * z.halo) * half
        band.load(tmp, z.inset, 2 * z.halo // SUB)
        band.set_operators(rows_c, 1, offset, 2 * z.halo // SUB)
        band.steps(rows_f, 1, 0, offset, 2 * z.halo // SUB)
        band.store(tmp, 2 * z.halo // SUB, z.inset)
        keep(1)
        ko[...] = obuf[0]
        so[...] = obuf[1]


def put_tiles(z, tmp, tiles, at):
    for f in range(z.fields):
        for n, tile in enumerate(tiles(f)):
            for p in range(2):
                tmp[f, p, aligned(at + SUB * n, SUB), :] = tile.astype(F32)[SUB * p : SUB * (p + 1)]


def early_kernel(z, active, core, rows_f, co, mix, state, tmp, *scratch):
    half, chip = half_and_chip()

    @pl.when(chip == active)
    def _():
        band = Band(z, scratch + (co, mix))
        span = z.core // SUB
        put_tiles(z, tmp, lambda f: [core[f, g] for g in range(z.core // SUB)], 0)
        band.load(tmp, 0, span)
        band.steps(rows_f, 0, 0, z.halo * (2 - half), span)
        band.store(state, span, z.base)


def late_kernel(
    z, active, core, near, far, state, rows_f, co_rim, mix_first, co_late, mix_last, ko_in, so_in, ko, so, obuf, tmp, *scratch
):
    half, chip = half_and_chip()

    @pl.when(chip == active)
    def _():
        groups = z.halo // SUB
        span = z.outer // SUB
        put_tiles(z, tmp, lambda f: [far[f, g] for g in range(groups)], 2 * z.halo * half)
        put_tiles(z, tmp, lambda f: [near[f, g] for g in range(groups)], z.halo)
        first = (z.core // SUB - groups) * half
        put_tiles(z, tmp, lambda f: [core[f, first + g] for g in range(groups)], 2 * z.halo * (1 - half))
        band = Band(z, scratch + (co_rim, mix_first))
        band.load(tmp, 0, span)
        band.steps(rows_f, 0, 0, (z.window - z.outer) * half, span)
        band.store(tmp, span, z.base)
        outer, inner = 2 * z.halo, z.core - z.halo
        start = z.inset + z.base
        for f in range(z.fields):
            for p in range(2):
                rim = tmp[f, p, start : start + outer, :]
                tmp[f, p, aligned(inner * half, outer), :] = rim
                tmp[f, p, aligned(outer * (1 - half), inner), :] = state[f, p, start : start + inner, :]
                obuf[1 - half, f, p] = tmp[f, p, z.inset : z.inset + z.own, :]
        band = Band(z, scratch + (co_late, mix_last))
        band.load(tmp, 0, z.narrow)
        band.steps(rows_f, 1, 0, z.halo * half + z.inset, z.narrow)
        band.store(tmp, z.narrow)
        for f in range(z.fields):
            for p in range(2):
                obuf[half, f, p] = tmp[f, p, z.inset : z.inset + z.own, :]
        ko[...] = obuf[0]
        so[...] = obuf[1]


def finish_kernel(z, keep, got, out, rows, sems):
    half, _ = half_and_chip()
    copies = []
    for f in range(z.fields):
        for p in range(2):
            a, b = keep[f, p], got[f, p]
            west = jnp.where(half == 0, a, b)
            east = jnp.where(half == 0, b, a)
            rows[f, pl.ds(p, z.lanes, stride=2), :] = jnp.concatenate([west, east], axis=0).T
        copies.append(pltpu.make_async_copy(rows.at[f], out.at[0, f], sems.at[f]))
        copies[-1].start()
    for copy in copies:
        copy.wait()


def shape(dims, dtype):
    return jax.ShapeDtypeStruct(tuple(dims), dtype)


def in_vmem(count):
    return [pl.BlockSpec(memory_space=pltpu.VMEM)] * count


def in_hbm(count):
    return [pl.BlockSpec(memory_space=pltpu.HBM)] * count


def per_device(forcing, zonal_courant, meridional_courant, zonal_faces, meridional_faces, coupling):
    z = Sizes(forcing.shape)
    tm_count, strips = lax.axis_size("tm"), lax.axis_size("space")
    assert tm_count == 4 and z.main % 16 == 0 and z.shift % 16 == 0
    params = pltpu.CompilerParams(vmem_limit_bytes=VMEM_BYTES)
    f_shape = (z.steps, z.fields, 2, z.main, z.lanes)
    c_shape = (5, 2, z.main, z.lanes)
    pay_shape = (z.payload, 2 * SUB, z.lanes)
    keep_f, send_f, keep_c, send_c, pay_a, pay_b = pl.pallas_call(
        functools.partial(prepare_kernel, z),
        out_shape=[
            shape(f_shape, BF16),
            shape(f_shape, BF16),
            shape(c_shape, F32),
            shape(c_shape, F32),
            shape(pay_shape, BF16),
            shape(pay_shape, BF16),
        ],
        in_specs=in_hbm(6),
        out_specs=in_vmem(6),
        scratch_shapes=[
            pltpu.VMEM(forcing.shape[1:], BF16),
            pltpu.VMEM((4, z.rows, z.strip), F32),
            pltpu.VMEM((z.fields, 1, z.fields), F32),
            pltpu.VMEM((4, z.rows, z.strip), F32),
            pltpu.VMEM((2, 2, SUB * z.payload, z.lanes), F32),
            pltpu.SemaphoreType.DMA((5 + 2 * z.steps,)),
        ],
        compiler_params=params,
        name="prepare",
    )(
        *[
            pltpu.with_memory_space_constraint(array, pltpu.HBM)
            for array in (
                forcing,
                zonal_courant,
                meridional_courant,
                zonal_faces,
                meridional_faces,
                jnp.swapaxes(coupling, 0, 1),
            )
        ]
    )

    def device(tm, space):
        return tm * strips + space % strips

    everyone = [(t, s) for t in range(tm_count) for s in range(strips)]
    partner = [(t, t ^ 1) for t in range(tm_count)]
    perm_a = [(device(t, s), device(t ^ 1, s + 1 if t % 2 else s - 1)) for t, s in everyone]
    perm_b = [(device(t, s), device(t, s - 1 if t % 2 else s + 1)) for t, s in everyone]
    got_f = lax.ppermute(send_f, "tm", partner)
    got_c = lax.ppermute(send_c, "tm", partner)
    got_a = lax.ppermute(pay_a, ("tm", "space"), perm_a)
    got_b = lax.ppermute(pay_b, ("tm", "space"), perm_b)

    def band_scratch(span):
        state = pltpu.VMEM((span + 2, z.fields, 2, SUB, z.lanes), F32)
        return [state] * 4

    def stencil(columns):
        return shape((columns // SUB + 2, 8, 2, SUB, z.lanes), F32)

    mixing = shape((z.fields**2, SUB, z.lanes), F32)

    def stencil_scratch(columns):
        return [pltpu.VMEM(stencil(columns).shape, F32)]

    rows_f_shape = shape((2, z.steps, z.fields, 2, z.window, z.lanes), F32)
    rows_c_shape = shape((2, 4, 2, z.window, z.lanes), F32)
    half_dims = (z.fields, 2, z.own, z.lanes)
    def tiles(columns):
        return shape((z.fields, columns // SUB, 2 * SUB, z.lanes), BF16)

    rows_f, rows_c, inner, core, mix_first, mix_last = pl.pallas_call(
        functools.partial(inner_kernel, z, 1),
        out_shape=[
            rows_f_shape,
            rows_c_shape,
            shape((2, z.fields, 2, z.main, z.lanes), F32),
            tiles(z.core),
            mixing,
            mixing,
        ],
        in_specs=in_vmem(4),
        out_specs=in_vmem(6),
        scratch_shapes=band_scratch(z.wide) + stencil_scratch(z.main) + [pltpu.VMEM((2, SUB, z.lanes), F32)],
        compiler_params=params,
        cost_estimate=pl.CostEstimate(flops=10**9, bytes_accessed=2 * 10**7, transcendentals=0),
        name="inner",
    )(keep_f, got_f, keep_c, got_c)
    down = [(device(t, s), device(t ^ 2, s)) for t, s in everyone]
    across = [(device(t, s), device((t ^ 1) - 2, s + 1 if t % 2 else s - 1) if t >= 2 else device(t + 2, s)) for t, s in everyone]
    core = lax.ppermute(core, ("tm", "space"), down)
    rows_f, rows_c, kept, sent, edge, co_core, co_rim, co_late = pl.pallas_call(
        functools.partial(rim_kernel, z, 1),
        out_shape=[
            rows_f_shape,
            rows_c_shape,
            shape(half_dims, F32),
            shape(half_dims, F32),
            tiles(z.halo),
            stencil(z.core),
            stencil(z.outer),
            stencil(z.main - z.halo),
        ],
        in_specs=in_vmem(7),
        out_specs=in_vmem(8),
        input_output_aliases={5: 0, 6: 1},
        scratch_shapes=[
            pltpu.VMEM((2,) + half_dims, F32),
            pltpu.VMEM((z.fields, 2, z.rim + SUB, z.lanes), F32),
            pltpu.VMEM((2, 2, SUB * z.payload, z.lanes), F32),
        ]
        + band_scratch(z.wide)
        + stencil_scratch(z.rim),
        compiler_params=params,
        cost_estimate=pl.CostEstimate(flops=10**9, bytes_accessed=2 * 10**7, transcendentals=0),
        name="rim",
    )(got_a, got_b, inner, mix_first, mix_last, rows_f, rows_c)
    state = pl.pallas_call(
        functools.partial(early_kernel, z, 0),
        out_shape=shape((z.fields, 2, z.core + SUB, z.lanes), F32),
        in_specs=in_vmem(4),
        out_specs=pl.BlockSpec(memory_space=pltpu.VMEM),
        scratch_shapes=[pltpu.VMEM((z.fields, 2, z.core, z.lanes), F32)] + band_scratch(z.core // SUB),
        compiler_params=params,
        name="early",
    )(core, rows_f, co_core, mix_first)
    far = lax.ppermute(edge, ("tm", "space"), across)
    near = lax.ppermute(edge, ("tm", "space"), down)
    kept, sent = pl.pallas_call(
        functools.partial(late_kernel, z, 0),
        out_shape=[shape(half_dims, F32), shape(half_dims, F32)],
        in_specs=in_vmem(11),
        out_specs=in_vmem(2),
        input_output_aliases={9: 0, 10: 1},
        scratch_shapes=[
            pltpu.VMEM((2,) + half_dims, F32),
            pltpu.VMEM((z.fields, 2, z.main, z.lanes), F32),
        ]
        + band_scratch(z.narrow),
        compiler_params=params,
        name="late",
    )(core, near, far, state, rows_f, co_rim, mix_first, co_late, mix_last, kept, sent)
    got = lax.ppermute(sent, "tm", partner)
    return pl.pallas_call(
        functools.partial(finish_kernel, z),
        out_shape=shape((1, z.fields, z.rows, z.strip), F32),
        in_specs=in_vmem(2),
        out_specs=pl.BlockSpec(memory_space=pltpu.HBM),
        scratch_shapes=[
            pltpu.VMEM((z.fields, z.rows, z.strip), F32),
            pltpu.SemaphoreType.DMA((z.fields,)),
        ],
        compiler_params=params,
        name="finish",
    )(kept, got)


def solution(mesh):
    return jax.shard_map(
        per_device,
        mesh=mesh,
        in_specs=(
            P("tm", None, None, None, "space"),
            P("tm", None, "space"),
            P("tm", None, "space"),
            P("tm", None, "space"),
            P("tm", None, "space"),
            P("tm", None, None),
        ),
        out_specs=P("tm", None, None, "space"),
        check_vma=False,
    )
```

```python
import functools

import jax
import jax.numpy as jnp
from jax import lax
from jax.experimental import pallas as pl
from jax.experimental.pallas import tpu as pltpu
from jax.sharding import PartitionSpec as P

SWEEPS = 2
OMEGA = 0.4
SUB = 8
REACH = SWEEPS + 1
VMEM_BYTES = 20 * 2**20
F32 = jnp.float32
BF16 = jnp.bfloat16


class Sizes:
    def __init__(self, forcing_shape):
        _, self.steps, self.fields, self.rows, self.strip = forcing_shape
        self.lanes = self.rows // 2
        self.halo = 2 * REACH * self.steps
        self.main = self.strip // 2 + 2 * self.halo
        self.window = self.main + self.halo
        self.span = self.window // SUB
        self.shift = self.strip - self.main
        self.own = self.strip // 2
        self.depths = [REACH * (self.steps + k) for k in range(self.steps)]
        self.depth = self.depths[-1]
        self.starts = [self.fields * sum(self.depths[:k]) for k in range(self.steps)]
        self.coef_start = self.fields * sum(self.depths)
        self.coef_depths = [self.halo - c for c in range(4)]
        self.coef_starts = [self.coef_start + sum(self.coef_depths[:c]) for c in range(4)]
        self.payload = -(-(self.coef_start + sum(self.coef_depths)) // SUB)
        self.message = self.own + self.halo
        self.core = self.message - self.halo
        self.wide, self.narrow = self.main // SUB, (self.main - self.halo) // SUB
        self.inset = self.halo // 2
        self.outer = 3 * self.halo
        self.rim = -(-3 * self.depth // SUB) * SUB
        self.rim_own = self.rim - 2 * self.depth
        self.base = -self.inset % SUB


def half_and_chip():
    tm = lax.axis_index("tm")
    return lax.rem(tm, 2), tm // 2


def prepare_kernel(z, fo_in, zc, mc, zf, mf, cp_in, keep_f, send_f, keep_c, send_c, pay_a, pay_b, fo, co, cp, buf, edges, sems):
    half, _ = half_and_chip()
    left = half == 0
    row = lax.broadcasted_iota(jnp.int32, (z.rows, z.strip), 0)
    coef_copies = [
        pltpu.make_async_copy(ref.at[0], co.at[c], sems.at[c]) for c, ref in enumerate((zf, mf, zc, mc))
    ]
    part = z.steps // 4
    forcing_copies = []
    for n in range(4):
        block = pl.ds(n * part, part)
        forcing_copies.append(pltpu.make_async_copy(fo_in.at[0, block], fo.at[block], sems.at[5 + n]))
    mixing_copy = pltpu.make_async_copy(cp_in, cp, sems.at[4])
    for copy in coef_copies + [mixing_copy] + forcing_copies:
        copy.start()

    def columns(values, slot):
        buf[slot] = values
        return [buf[slot, pl.ds(p, z.lanes, stride=2), :].T for p in range(2)]

    def split(both, depth, start, keep, send):
        for p in range(2):
            low, high = both[p][: z.main], both[p][z.shift :]
            keep[p] = jnp.where(left, low, high).astype(keep.dtype)
            send[p] = jnp.where(left, high, low).astype(send.dtype)
            edges[0, p, start : start + depth, :] = both[p][:depth]
            edges[1, p, start : start + depth, :] = both[p][z.strip - depth :]

    slots = buf.shape[0]
    count = 0
    for c in range(4):
        coef_copies[c].wait()
        values = co[c]
        if c == 1:
            values = jnp.where(row < z.rows - 1, values, jnp.zeros_like(values))
        both = columns(values, count % slots)
        split(both, z.coef_depths[c], z.coef_starts[c], keep_c.at[c], send_c.at[c])
        count += 1
    mixing_copy.wait()
    for ref in (keep_c, send_c):
        for g in range(z.fields):
            ref[4, 0, g : g + 1, : z.fields] = cp[g]
    for k in range(z.steps):
        if k % part == 0:
            forcing_copies[k // part].wait()
        for f in range(z.fields):
            both = columns(fo[k, f].astype(F32), count % slots)
            split(both, z.depths[k], z.starts[k] + f * z.depths[k], keep_f.at[k, f], send_f.at[k, f])
            count += 1
    for g in range(z.payload):
        at = slice(SUB * g, SUB * (g + 1))
        west, east = (jnp.concatenate([edges[n, p, at, :] for p in range(2)], axis=0) for n in range(2))
        pay_a[g] = jnp.where(left, west, east).astype(BF16)
        pay_b[g] = jnp.where(left, east, west).astype(BF16)


def fill_ghosts(ref, span, count):
    for n in range(count):
        for p in range(2):
            ref[0, n, p] = pltpu.roll(ref[span, n, p], 1, 0)
            ref[span + 1, n, p] = pltpu.roll(ref[1, n, p], SUB - 1, 0)


class Band:
    def __init__(self, z, scratch):
        self.z = z
        self.r, self.u1, self.u2, self.pz, self.co, self.kk = scratch
        self.lane = lax.broadcasted_iota(jnp.int32, (SUB, z.lanes), 1)

    def east(self, v):
        return pltpu.roll(v, 1, 1)

    def west(self, v):
        return pltpu.roll(v, self.z.lanes - 1, 1)

    def set_operators(self, rows_c, q, offset, span):
        z, u1, co = self.z, self.u1, self.co
        for c in range(4):
            for p in range(2):
                for i in range(span):
                    u1[i + 1, c, p] = rows_c[q, c, p, pl.ds(offset + i, SUB, stride=span), :]
        fill_ghosts(u1, span, 1)
        for i in range(1, span + 1):
            be, bo = u1[i, 1, 0], u1[i, 1, 1]
            south = (self.east(bo), be)
            for p in range(2):
                a, aw, b = u1[i, 0, p], u1[i - 1, 0, p], u1[i, 1, p]
                centre = 1.0 - OMEGA * (1.0 + (a + aw) + (b + south[p]))
                co[i, 0, p] = centre
                co[i, 7, p] = 1.0 + centre
                co[i, 1, p] = OMEGA * a
                co[i, 2, p] = OMEGA * aw
                co[i, 3, p] = OMEGA * b
                co[i, 4, p] = OMEGA * south[p]
                co[i, 5, p] = (0.5 * OMEGA) * u1[i, 2, p]
                co[i, 6, p] = (0.5 * OMEGA) * u1[i, 3, p]

    def load(self, at, offset, span):
        for i in range(span):
            for f in range(self.z.fields):
                for p in range(2):
                    self.r[i + 1, f, p] = at[f, p, pl.ds(offset + i, SUB, stride=span), :]

    def store(self, at, span, base=0):
        for i in range(span):
            for f in range(self.z.fields):
                for p in range(2):
                    at[f, p, pl.ds(base + i, SUB, stride=span), :] = self.r[i + 1, f, p]

    def sweep(self, src, dst, i, source):
        co = self.co
        first = 7 if source is None else 0
        ga = [co[i, c, 0] for c in (first, 1, 2, 3, 4)]
        gb = [co[i, c, 1] for c in (first, 1, 2, 3, 4)]
        for f in range(self.z.fields):
            a, b = src[i, f, 0], src[i, f, 1]
            va = ga[0] * a + ga[1] * src[i + 1, f, 0] + ga[2] * src[i - 1, f, 0] + ga[3] * b + ga[4] * self.east(b)
            vb = gb[0] * b + gb[1] * src[i + 1, f, 1] + gb[2] * src[i - 1, f, 1] + gb[3] * self.west(a) + gb[4] * a
            if source is not None:
                va = va + source[i, f, 0]
                vb = vb + source[i, f, 1]
                self.pz[i, f, 0] = co[i, 5, 0] * va
                self.pz[i, f, 1] = co[i, 5, 1] * vb
            dst[i, f, 0] = va
            dst[i, f, 1] = vb

    def step(self, forcing, offset, span):
        z, r, u1, u2, pz, co, kk = self.z, self.r, self.u1, self.u2, self.pz, self.co, self.kk
        zero = jnp.zeros((SUB, z.lanes), F32)
        fill_ghosts(r, span, z.fields)
        for i in range(1, span + 1):
            self.sweep(r, u1, i, None)
        fill_ghosts(u1, span, z.fields)
        for i in range(1, span + 1):
            self.sweep(u1, u2, i, r)
        fill_ghosts(pz, span, z.fields)
        for i in range(1, span + 1):
            us = [[u2[i, g, p] for p in range(2)] for g in range(z.fields)]
            for f in range(z.fields):
                qa, qb = co[i, 6, 0] * us[f][0], co[i, 6, 1] * us[f][1]
                qba = jnp.where(self.lane == 0, zero, self.east(qb))
                qab = jnp.where(self.lane == z.lanes - 1, zero, self.west(qa))
                oa = (pz[i + 1, f, 0] - pz[i - 1, f, 0]) + (qb - qba)
                ob = (pz[i + 1, f, 1] - pz[i - 1, f, 1]) + (qab - qa)
                for g in range(z.fields):
                    w = kk[g * z.fields + f]
                    oa = oa + w * us[g][0]
                    ob = ob + w * us[g][1]
                rows = pl.ds(offset + i - 1, SUB, stride=span)
                r[i, f, 0] = oa + forcing[f, 0, rows, :]
                r[i, f, 1] = ob + forcing[f, 1, rows, :]

    def steps(self, rows_f, q, begin, offset, span):
        last = self.z.steps - 1

        def one(n, carry):
            self.step(rows_f.at[q, last - n], offset, span)
            return carry

        lax.fori_loop(begin, last + 1, one, 0)


def set_mixing(z, mix, table):
    for g in range(z.fields):
        for f in range(z.fields):
            value = table[g : g + 1, f : f + 1]
            if f == g:
                value = value + 1.0
            mix[g * z.fields + f] = jnp.broadcast_to(OMEGA * value, (SUB, z.lanes))


def aligned(offset, count):
    return pl.ds(pl.multiple_of(offset, SUB), count)


def tile_of(ref, f, at):
    return jnp.concatenate([ref[f, p, at, :] for p in range(2)], axis=0).astype(BF16)


def inner_kernel(z, active, kf, rf, kc, rc, rows_f, rows_c, inner, core, mix_first, mix_last, *scratch):
    half, chip = half_and_chip()
    *scratch, tables = scratch
    main_at = z.halo * (1 - half)
    blank = jnp.zeros((z.halo, z.lanes), F32)

    def put(ref, values):
        ref[aligned(main_at, z.main), :] = values.astype(F32)
        ref[aligned(z.main * half, z.halo), :] = blank

    for q, forcing, coefs in ((1 - half, kf, kc), (half, rf, rc)):
        for c in range(4):
            for p in range(2):
                put(rows_c.at[q, c, p], coefs[c, p])
        tables[q, :, :] = coefs[4, 0, :SUB, :]
        for k in range(z.steps):
            for f in range(z.fields):
                for p in range(2):
                    put(rows_f.at[q, k, f, p], forcing[k, f, p])

    set_mixing(z, mix_first, tables.at[0])
    set_mixing(z, mix_last, tables.at[1])

    @pl.when(chip == active)
    def _():
        band = Band(z, (*scratch, mix_first))
        span = z.main // SUB
        band.load(rows_f.at[0, z.steps - 1], main_at, span)
        band.set_operators(rows_c, 0, main_at, span)
        band.steps(rows_f, 0, 1, main_at, span)
        band.store(inner.at[0], span)
        cut = REACH * (z.steps - 1) // SUB * SUB
        span -= 2 * cut // SUB
        band = Band(z, (*scratch, mix_last))
        band.load(inner.at[0], cut, span)
        band.set_operators(rows_c, 1, main_at + cut, span)
        band.steps(rows_f, 1, 0, main_at + cut, span)
        band.store(inner.at[1], span, cut)
        for f in range(z.fields):
            for g in range(z.core // SUB):
                core[f, g] = tile_of(inner.at[1], f, slice(z.halo + SUB * g, z.halo + SUB * (g + 1)))


def rim_kernel(z, active, ra, rb, inner, mix_first, mix_last, rows_f_in, rows_c_in, rows_f, rows_c, ko, so, edge, *refs):
    (co_core, co_rim, co_late), (obuf, tmp, edges), scratch = refs[:3], refs[3:6], refs[6:]
    half, chip = half_and_chip()
    for n, pay in enumerate((ra, rb)):
        for g in range(z.payload):
            tile = pay[g].astype(F32)
            for p in range(2):
                edges[n, p, SUB * g : SUB * (g + 1), :] = tile[SUB * p : SUB * (p + 1)]

    def place_edges(side):
        for n, q in ((0, side), (1, 1 - side)):
            blocks = [(rows_c.at[q, c], z.coef_starts[c], z.coef_depths[c]) for c in range(4)]
            for k in range(z.steps):
                for f in range(z.fields):
                    blocks.append((rows_f.at[q, k, f], z.starts[k] + f * z.depths[k], z.depths[k]))
            for ref, start, depth in blocks:
                at = z.main if side else z.halo - depth
                for p in range(2):
                    ref[p, at : at + depth, :] = edges[n, p, start : start + depth, :]

    for side in range(2):
        pl.when(half == side)(functools.partial(place_edges, side))

    @pl.when(chip != active)
    def _():
        for q, co, mix, columns, offset in (
            (0, co_core, mix_first, z.core, z.halo * (2 - half)),
            (0, co_rim, mix_first, z.outer, (z.window - z.outer) * half),
            (1, co_late, mix_last, z.main - z.halo, z.halo * half + z.inset),
        ):
            Band(z, (*scratch[:4], co, mix)).set_operators(rows_c, q, offset, columns // SUB)

    @pl.when(chip == active)
    def _():
        band = Band(z, (*scratch, mix_first))
        start = z.halo - z.depth
        offset = start + (z.main + z.depth - z.rim - start) * half
        base = start + (2 * z.halo + z.depth - z.rim - start) * half
        sublane = lax.broadcasted_iota(jnp.int32, (SUB, z.lanes), 0)
        mine = []
        for g in range(z.halo // SUB):
            at = sublane + SUB * g
            mine.append(jnp.where(half == 0, at, z.halo - 1 - at) < z.rim_own)

        def keep(q):
            place = jnp.where(half == q, 1, 0)
            for f in range(z.fields):
                merged = []
                for p in range(2):
                    obuf[place, f, p] = inner[q, f, p, aligned((z.main - z.own) * half, z.own), :]
                    for g in range(z.halo // SUB):
                        rim = tmp[f, p, z.halo + SUB * g : z.halo + SUB * (g + 1), :]
                        own = inner[q, f, p, aligned((z.main - z.halo) * half + SUB * g, SUB), :]
                        merged.append(jnp.where(mine[g], rim, own))
                        obuf[place, f, p, aligned((z.own - z.halo) * half + SUB * g, SUB), :] = merged[-1]
                if q == 1:
                    for g in range(z.halo // SUB):
                        edge[f, g] = jnp.concatenate([merged[g], merged[g + z.halo // SUB]], axis=0).astype(BF16)

        band.load(rows_f.at[0, z.steps - 1], offset, z.rim // SUB)
        band.set_operators(rows_c, 0, offset, z.rim // SUB)
        band.steps(rows_f, 0, 1, offset, z.rim // SUB)
        band.store(tmp, z.rim // SUB, base)
        keep(0)
        band = Band(z, (*scratch, mix_last))
        offset = z.inset + (z.main - 2 * z.halo) * half
        band.load(tmp, z.inset, 2 * z.halo // SUB)
        band.set_operators(rows_c, 1, offset, 2 * z.halo // SUB)
        band.steps(rows_f, 1, 0, offset, 2 * z.halo // SUB)
        band.store(tmp, 2 * z.halo // SUB, z.inset)
        keep(1)
        ko[...] = obuf[0]
        so[...] = obuf[1]


def put_tiles(z, tmp, tiles, at):
    for f in range(z.fields):
        for n, tile in enumerate(tiles(f)):
            for p in range(2):
                tmp[f, p, aligned(at + SUB * n, SUB), :] = tile.astype(F32)[SUB * p : SUB * (p + 1)]


def early_kernel(z, active, core, rows_f, co, mix, state, tmp, *scratch):
    half, chip = half_and_chip()

    @pl.when(chip == active)
    def _():
        band = Band(z, scratch + (co, mix))
        span = z.core // SUB
        put_tiles(z, tmp, lambda f: [core[f, g] for g in range(z.core // SUB)], 0)
        band.load(tmp, 0, span)
        band.steps(rows_f, 0, 0, z.halo * (2 - half), span)
        band.store(state, span, z.base)


def late_kernel(
    z, active, core, near, far, state, rows_f, co_rim, mix_first, co_late, mix_last, ko_in, so_in, ko, so, obuf, tmp, *scratch
):
    half, chip = half_and_chip()

    @pl.when(chip == active)
    def _():
        groups = z.halo // SUB
        span = z.outer // SUB
        put_tiles(z, tmp, lambda f: [far[f, g] for g in range(groups)], 2 * z.halo * half)
        put_tiles(z, tmp, lambda f: [near[f, g] for g in range(groups)], z.halo)
        first = (z.core // SUB - groups) * half
        put_tiles(z, tmp, lambda f: [core[f, first + g] for g in range(groups)], 2 * z.halo * (1 - half))
        band = Band(z, scratch + (co_rim, mix_first))
        band.load(tmp, 0, span)
        band.steps(rows_f, 0, 0, (z.window - z.outer) * half, span)
        band.store(tmp, span, z.base)
        outer, inner = 2 * z.halo, z.core - z.halo
        start = z.inset + z.base
        for f in range(z.fields):
            for p in range(2):
                rim = tmp[f, p, start : start + outer, :]
                tmp[f, p, aligned(inner * half, outer), :] = rim
                tmp[f, p, aligned(outer * (1 - half), inner), :] = state[f, p, start : start + inner, :]
                obuf[1 - half, f, p] = tmp[f, p, z.inset : z.inset + z.own, :]
        band = Band(z, scratch + (co_late, mix_last))
        band.load(tmp, 0, z.narrow)
        band.steps(rows_f, 1, 0, z.halo * half + z.inset, z.narrow)
        band.store(tmp, z.narrow)
        for f in range(z.fields):
            for p in range(2):
                obuf[half, f, p] = tmp[f, p, z.inset : z.inset + z.own, :]
        ko[...] = obuf[0]
        so[...] = obuf[1]


def finish_kernel(z, keep, got, out, rows, sems):
    half, _ = half_and_chip()
    copies = []
    for f in range(z.fields):
        for p in range(2):
            a, b = keep[f, p], got[f, p]
            west = jnp.where(half == 0, a, b)
            east = jnp.where(half == 0, b, a)
            rows[f, pl.ds(p, z.lanes, stride=2), :] = jnp.concatenate([west, east], axis=0).T
        copies.append(pltpu.make_async_copy(rows.at[f], out.at[0, f], sems.at[f]))
        copies[-1].start()
    for copy in copies:
        copy.wait()


def shape(dims, dtype):
    return jax.ShapeDtypeStruct(tuple(dims), dtype)


def in_vmem(count):
    return [pl.BlockSpec(memory_space=pltpu.VMEM)] * count


def in_hbm(count):
    return [pl.BlockSpec(memory_space=pltpu.HBM)] * count


def per_device(forcing, zonal_courant, meridional_courant, zonal_faces, meridional_faces, coupling):
    z = Sizes(forcing.shape)
    tm_count, strips = lax.axis_size("tm"), lax.axis_size("space")
    assert tm_count == 4 and z.main % 16 == 0 and z.shift % 16 == 0
    params = pltpu.CompilerParams(vmem_limit_bytes=VMEM_BYTES)
    f_shape = (z.steps, z.fields, 2, z.main, z.lanes)
    c_shape = (5, 2, z.main, z.lanes)
    pay_shape = (z.payload, 2 * SUB, z.lanes)
    keep_f, send_f, keep_c, send_c, pay_a, pay_b = pl.pallas_call(
        functools.partial(prepare_kernel, z),
        out_shape=[
            shape(f_shape, BF16),
            shape(f_shape, BF16),
            shape(c_shape, F32),
            shape(c_shape, F32),
            shape(pay_shape, BF16),
            shape(pay_shape, BF16),
        ],
        in_specs=in_hbm(6),
        out_specs=in_vmem(6),
        scratch_shapes=[
            pltpu.VMEM(forcing.shape[1:], BF16),
            pltpu.VMEM((4, z.rows, z.strip), F32),
            pltpu.VMEM((z.fields, 1, z.fields), F32),
            pltpu.VMEM((4, z.rows, z.strip), F32),
            pltpu.VMEM((2, 2, SUB * z.payload, z.lanes), F32),
            pltpu.SemaphoreType.DMA((5 + 2 * z.steps,)),
        ],
        compiler_params=params,
        name="prepare",
    )(
        *[
            pltpu.with_memory_space_constraint(array, pltpu.HBM)
            for array in (
                forcing,
                zonal_courant,
                meridional_courant,
                zonal_faces,
                meridional_faces,
                jnp.swapaxes(coupling, 0, 1),
            )
        ]
    )

    def device(tm, space):
        return tm * strips + space % strips

    everyone = [(t, s) for t in range(tm_count) for s in range(strips)]
    partner = [(t, t ^ 1) for t in range(tm_count)]
    perm_a = [(device(t, s), device(t ^ 1, s + 1 if t % 2 else s - 1)) for t, s in everyone]
    perm_b = [(device(t, s), device(t, s - 1 if t % 2 else s + 1)) for t, s in everyone]
    got_f = lax.ppermute(send_f, "tm", partner)
    got_c = lax.ppermute(send_c, "tm", partner)
    got_a = lax.ppermute(pay_a, ("tm", "space"), perm_a)
    got_b = lax.ppermute(pay_b, ("tm", "space"), perm_b)

    def band_scratch(span):
        state = pltpu.VMEM((span + 2, z.fields, 2, SUB, z.lanes), F32)
        return [state] * 4

    def stencil(columns):
        return shape((columns // SUB + 2, 8, 2, SUB, z.lanes), F32)

    mixing = shape((z.fields**2, SUB, z.lanes), F32)

    def stencil_scratch(columns):
        return [pltpu.VMEM(stencil(columns).shape, F32)]

    rows_f_shape = shape((2, z.steps, z.fields, 2, z.window, z.lanes), F32)
    rows_c_shape = shape((2, 4, 2, z.window, z.lanes), F32)
    half_dims = (z.fields, 2, z.own, z.lanes)
    def tiles(columns):
        return shape((z.fields, columns // SUB, 2 * SUB, z.lanes), BF16)

    rows_f, rows_c, inner, core, mix_first, mix_last = pl.pallas_call(
        functools.partial(inner_kernel, z, 1),
        out_shape=[
            rows_f_shape,
            rows_c_shape,
            shape((2, z.fields, 2, z.main, z.lanes), F32),
            tiles(z.core),
            mixing,
            mixing,
        ],
        in_specs=in_vmem(4),
        out_specs=in_vmem(6),
        scratch_shapes=band_scratch(z.wide) + stencil_scratch(z.main) + [pltpu.VMEM((2, SUB, z.lanes), F32)],
        compiler_params=params,
        cost_estimate=pl.CostEstimate(flops=10**9, bytes_accessed=2 * 10**7, transcendentals=0),
        name="inner",
    )(keep_f, got_f, keep_c, got_c)
    down = [(device(t, s), device(t ^ 2, s)) for t, s in everyone]
    across = [(device(t, s), device((t ^ 1) - 2, s + 1 if t % 2 else s - 1) if t >= 2 else device(t + 2, s)) for t, s in everyone]
    core = lax.ppermute(core, ("tm", "space"), down)
    rows_f, rows_c, kept, sent, edge, co_core, co_rim, co_late = pl.pallas_call(
        functools.partial(rim_kernel, z, 1),
        out_shape=[
            rows_f_shape,
            rows_c_shape,
            shape(half_dims, F32),
            shape(half_dims, F32),
            tiles(z.halo),
            stencil(z.core),
            stencil(z.outer),
            stencil(z.main - z.halo),
        ],
        in_specs=in_vmem(7),
        out_specs=in_vmem(8),
        input_output_aliases={5: 0, 6: 1},
        scratch_shapes=[
            pltpu.VMEM((2,) + half_dims, F32),
            pltpu.VMEM((z.fields, 2, z.rim + SUB, z.lanes), F32),
            pltpu.VMEM((2, 2, SUB * z.payload, z.lanes), F32),
        ]
        + band_scratch(z.wide)
        + stencil_scratch(z.rim),
        compiler_params=params,
        cost_estimate=pl.CostEstimate(flops=10**9, bytes_accessed=2 * 10**7, transcendentals=0),
        name="rim",
    )(got_a, got_b, inner, mix_first, mix_last, rows_f, rows_c)
    state = pl.pallas_call(
        functools.partial(early_kernel, z, 0),
        out_shape=shape((z.fields, 2, z.core + SUB, z.lanes), F32),
        in_specs=in_vmem(4),
        out_specs=pl.BlockSpec(memory_space=pltpu.VMEM),
        scratch_shapes=[pltpu.VMEM((z.fields, 2, z.core, z.lanes), F32)] + band_scratch(z.core // SUB),
        compiler_params=params,
        name="early",
    )(core, rows_f, co_core, mix_first)
    far = lax.ppermute(edge, ("tm", "space"), across)
    near = lax.ppermute(edge, ("tm", "space"), down)
    kept, sent = pl.pallas_call(
        functools.partial(late_kernel, z, 0),
        out_shape=[shape(half_dims, F32), shape(half_dims, F32)],
        in_specs=in_vmem(11),
        out_specs=in_vmem(2),
        input_output_aliases={9: 0, 10: 1},
        scratch_shapes=[
            pltpu.VMEM((2,) + half_dims, F32),
            pltpu.VMEM((z.fields, 2, z.main, z.lanes), F32),
        ]
        + band_scratch(z.narrow),
        compiler_params=params,
        name="late",
    )(core, near, far, state, rows_f, co_rim, mix_first, co_late, mix_last, kept, sent)
    got = lax.ppermute(sent, "tm", partner)
    return pl.pallas_call(
        functools.partial(finish_kernel, z),
        out_shape=shape((1, z.fields, z.rows, z.strip), F32),
        in_specs=in_vmem(2),
        out_specs=pl.BlockSpec(memory_space=pltpu.HBM),
        scratch_shapes=[
            pltpu.VMEM((z.fields, z.rows, z.strip), F32),
            pltpu.SemaphoreType.DMA((z.fields,)),
        ],
        compiler_params=params,
        name="finish",
    )(kept, got)


def solution(mesh):
    return jax.shard_map(
        per_device,
        mesh=mesh,
        in_specs=(
            P("tm", None, None, None, "space"),
            P("tm", None, "space"),
            P("tm", None, "space"),
            P("tm", None, "space"),
            P("tm", None, "space"),
            P("tm", None, None),
        ),
        out_specs=P("tm", None, None, "space"),
        check_vma=False,
    )
```

```python
import functools

import jax
import jax.numpy as jnp
from jax import lax
from jax.experimental import pallas as pl
from jax.experimental.pallas import tpu as pltpu
from jax.sharding import PartitionSpec as P

SWEEPS = 2
OMEGA = 0.4
SUB = 8
REACH = SWEEPS + 1
VMEM_BYTES = 20 * 2**20
F32 = jnp.float32
BF16 = jnp.bfloat16


class Sizes:
    def __init__(self, forcing_shape):
        _, self.steps, self.fields, self.rows, self.strip = forcing_shape
        self.lanes = self.rows // 2
        self.halo = 2 * REACH * self.steps
        self.main = self.strip // 2 + 2 * self.halo
        self.window = self.main + self.halo
        self.span = self.window // SUB
        self.shift = self.strip - self.main
        self.own = self.strip // 2
        self.depths = [REACH * (self.steps + k) for k in range(self.steps)]
        self.depth = self.depths[-1]
        self.starts = [self.fields * sum(self.depths[:k]) for k in range(self.steps)]
        self.coef_start = self.fields * sum(self.depths)
        self.coef_depths = [self.halo - c for c in range(4)]
        self.coef_starts = [self.coef_start + sum(self.coef_depths[:c]) for c in range(4)]
        self.payload = -(-(self.coef_start + sum(self.coef_depths)) // SUB)
        self.message = self.own + self.halo
        self.core = self.message - self.halo
        self.wide, self.narrow = self.main // SUB, (self.main - self.halo) // SUB
        self.inset = self.halo // 2
        self.outer = 3 * self.halo
        self.rim = -(-3 * self.depth // SUB) * SUB
        self.rim_own = self.rim - 2 * self.depth
        self.base = -self.inset % SUB


def half_and_chip():
    tm = lax.axis_index("tm")
    return lax.rem(tm, 2), tm // 2


def prepare_kernel(z, fo_in, zc, mc, zf, mf, cp_in, keep_f, send_f, keep_c, send_c, pay_a, pay_b, fo, co, cp, buf, edges, sems):
    half, _ = half_and_chip()
    left = half == 0
    row = lax.broadcasted_iota(jnp.int32, (z.rows, z.strip), 0)
    coef_copies = [
        pltpu.make_async_copy(ref.at[0], co.at[c], sems.at[c]) for c, ref in enumerate((zf, mf, zc, mc))
    ]
    part = z.steps // 4
    forcing_copies = []
    for n in range(4):
        block = pl.ds(n * part, part)
        forcing_copies.append(pltpu.make_async_copy(fo_in.at[0, block], fo.at[block], sems.at[5 + n]))
    mixing_copy = pltpu.make_async_copy(cp_in, cp, sems.at[4])
    for copy in coef_copies + [mixing_copy] + forcing_copies:
        copy.start()

    def columns(values, slot):
        buf[slot] = values
        return [buf[slot, pl.ds(p, z.lanes, stride=2), :].T for p in range(2)]

    def split(both, depth, start, keep, send):
        for p in range(2):
            low, high = both[p][: z.main], both[p][z.shift :]
            keep[p] = jnp.where(left, low, high).astype(keep.dtype)
            send[p] = jnp.where(left, high, low).astype(send.dtype)
            edges[0, p, start : start + depth, :] = both[p][:depth]
            edges[1, p, start : start + depth, :] = both[p][z.strip - depth :]

    slots = buf.shape[0]
    count = 0
    for c in range(4):
        coef_copies[c].wait()
        values = co[c]
        if c == 1:
            values = jnp.where(row < z.rows - 1, values, jnp.zeros_like(values))
        both = columns(values, count % slots)
        split(both, z.coef_depths[c], z.coef_starts[c], keep_c.at[c], send_c.at[c])
        count += 1
    mixing_copy.wait()
    for ref in (keep_c, send_c):
        for g in range(z.fields):
            ref[4, 0, g : g + 1, : z.fields] = cp[g]
    for k in range(z.steps):
        if k % part == 0:
            forcing_copies[k // part].wait()
        for f in range(z.fields):
            both = columns(fo[k, f].astype(F32), count % slots)
            split(both, z.depths[k], z.starts[k] + f * z.depths[k], keep_f.at[k, f], send_f.at[k, f])
            count += 1
    for g in range(z.payload):
        at = slice(SUB * g, SUB * (g + 1))
        west, east = (jnp.concatenate([edges[n, p, at, :] for p in range(2)], axis=0) for n in range(2))
        pay_a[g] = jnp.where(left, west, east).astype(BF16)
        pay_b[g] = jnp.where(left, east, west).astype(BF16)


def fill_ghosts(ref, span, count):
    for n in range(count):
        for p in range(2):
            ref[0, n, p] = pltpu.roll(ref[span, n, p], 1, 0)
            ref[span + 1, n, p] = pltpu.roll(ref[1, n, p], SUB - 1, 0)


class Band:
    def __init__(self, z, scratch):
        self.z = z
        self.r, self.u1, self.u2, self.pz, self.co, self.kk = scratch
        self.lane = lax.broadcasted_iota(jnp.int32, (SUB, z.lanes), 1)

    def east(self, v):
        return pltpu.roll(v, 1, 1)

    def west(self, v):
        return pltpu.roll(v, self.z.lanes - 1, 1)

    def set_operators(self, rows_c, q, offset, span):
        z, u1, co = self.z, self.u1, self.co
        for c in range(4):
            for p in range(2):
                for i in range(span):
                    u1[i + 1, c, p] = rows_c[q, c, p, pl.ds(offset + i, SUB, stride=span), :]
        fill_ghosts(u1, span, 1)
        for i in range(1, span + 1):
            be, bo = u1[i, 1, 0], u1[i, 1, 1]
            south = (self.east(bo), be)
            for p in range(2):
                a, aw, b = u1[i, 0, p], u1[i - 1, 0, p], u1[i, 1, p]
                centre = 1.0 - OMEGA * (1.0 + (a + aw) + (b + south[p]))
                co[i, 0, p] = centre
                co[i, 7, p] = 1.0 + centre
                co[i, 1, p] = OMEGA * a
                co[i, 2, p] = OMEGA * aw
                co[i, 3, p] = OMEGA * b
                co[i, 4, p] = OMEGA * south[p]
                co[i, 5, p] = (0.5 * OMEGA) * u1[i, 2, p]
                co[i, 6, p] = (0.5 * OMEGA) * u1[i, 3, p]

    def load(self, at, offset, span):
        for i in range(span):
            for f in range(self.z.fields):
                for p in range(2):
                    self.r[i + 1, f, p] = at[f, p, pl.ds(offset + i, SUB, stride=span), :]

    def store(self, at, span, base=0):
        for i in range(span):
            for f in range(self.z.fields):
                for p in range(2):
                    at[f, p, pl.ds(base + i, SUB, stride=span), :] = self.r[i + 1, f, p]

    def sweep(self, src, dst, i, source):
        co = self.co
        first = 7 if source is None else 0
        ga = [co[i, c, 0] for c in (first, 1, 2, 3, 4)]
        gb = [co[i, c, 1] for c in (first, 1, 2, 3, 4)]
        for f in range(self.z.fields):
            a, b = src[i, f, 0], src[i, f, 1]
            va = ga[0] * a + ga[1] * src[i + 1, f, 0] + ga[2] * src[i - 1, f, 0] + ga[3] * b + ga[4] * self.east(b)
            vb = gb[0] * b + gb[1] * src[i + 1, f, 1] + gb[2] * src[i - 1, f, 1] + gb[3] * self.west(a) + gb[4] * a
            if source is not None:
                va = va + source[i, f, 0]
                vb = vb + source[i, f, 1]
                self.pz[i, f, 0] = co[i, 5, 0] * va
                self.pz[i, f, 1] = co[i, 5, 1] * vb
            dst[i, f, 0] = va
            dst[i, f, 1] = vb

    def step(self, forcing, offset, span):
        z, r, u1, u2, pz, co, kk = self.z, self.r, self.u1, self.u2, self.pz, self.co, self.kk
        zero = jnp.zeros((SUB, z.lanes), F32)
        fill_ghosts(r, span, z.fields)
        for i in range(1, span + 1):
            self.sweep(r, u1, i, None)
        fill_ghosts(u1, span, z.fields)
        for i in range(1, span + 1):
            self.sweep(u1, u2, i, r)
        fill_ghosts(pz, span, z.fields)
        for i in range(1, span + 1):
            us = [[u2[i, g, p] for p in range(2)] for g in range(z.fields)]
            for f in range(z.fields):
                qa, qb = co[i, 6, 0] * us[f][0], co[i, 6, 1] * us[f][1]
                qba = jnp.where(self.lane == 0, zero, self.east(qb))
                qab = jnp.where(self.lane == z.lanes - 1, zero, self.west(qa))
                oa = (pz[i + 1, f, 0] - pz[i - 1, f, 0]) + (qb - qba)
                ob = (pz[i + 1, f, 1] - pz[i - 1, f, 1]) + (qab - qa)
                for g in range(z.fields):
                    w = kk[g * z.fields + f]
                    oa = oa + w * us[g][0]
                    ob = ob + w * us[g][1]
                rows = pl.ds(offset + i - 1, SUB, stride=span)
                r[i, f, 0] = oa + forcing[f, 0, rows, :]
                r[i, f, 1] = ob + forcing[f, 1, rows, :]

    def steps(self, rows_f, q, begin, offset, span):
        last = self.z.steps - 1

        def one(n, carry):
            self.step(rows_f.at[q, last - n], offset, span)
            return carry

        lax.fori_loop(begin, last + 1, one, 0)


def set_mixing(z, mix, table):
    for g in range(z.fields):
        for f in range(z.fields):
            value = table[g : g + 1, f : f + 1]
            if f == g:
                value = value + 1.0
            mix[g * z.fields + f] = jnp.broadcast_to(OMEGA * value, (SUB, z.lanes))


def aligned(offset, count):
    return pl.ds(pl.multiple_of(offset, SUB), count)


def tile_of(ref, f, at):
    return jnp.concatenate([ref[f, p, at, :] for p in range(2)], axis=0).astype(BF16)


def put_rows(z, half, rows_f, rows_c, q, forcing, coefs):
    at = aligned(z.halo * (1 - half), z.main)
    for c in range(4):
        for p in range(2):
            rows_c[q, c, p, at, :] = coefs[c, p]
    for k in range(z.steps):
        for f in range(z.fields):
            for p in range(2):
                rows_f[q, k, f, p, at, :] = forcing[k, f, p].astype(F32)


def spread_kernel(z, kf, kc, rows_f, rows_c):
    half, _ = half_and_chip()
    put_rows(z, half, rows_f, rows_c, 1 - half, kf, kc)
    blank = jnp.zeros((z.halo, z.lanes), F32)
    edge = aligned(z.main * half, z.halo)
    for q in range(2):
        for p in range(2):
            for c in range(4):
                rows_c[q, c, p, edge, :] = blank
            for k in range(z.steps):
                for f in range(z.fields):
                    rows_f[q, k, f, p, edge, :] = blank


def inner_kernel(
    z, active, rf, rc, kc, rows_f_in, rows_c_in, rows_f, rows_c, inner, core, mix_first, mix_last, *scratch
):
    half, chip = half_and_chip()
    *scratch, tables = scratch
    main_at = z.halo * (1 - half)
    put_rows(z, half, rows_f, rows_c, half, rf, rc)
    for q, coefs in ((1 - half, kc), (half, rc)):
        tables[q, :, :] = coefs[4, 0, :SUB, :]
    set_mixing(z, mix_first, tables.at[0])
    set_mixing(z, mix_last, tables.at[1])

    @pl.when(chip == active)
    def _():
        band = Band(z, (*scratch, mix_first))
        span = z.main // SUB
        band.load(rows_f.at[0, z.steps - 1], main_at, span)
        band.set_operators(rows_c, 0, main_at, span)
        band.steps(rows_f, 0, 1, main_at, span)
        band.store(inner.at[0], span)
        cut = REACH * (z.steps - 1) // SUB * SUB
        span -= 2 * cut // SUB
        band = Band(z, (*scratch, mix_last))
        band.load(inner.at[0], cut, span)
        band.set_operators(rows_c, 1, main_at + cut, span)
        band.steps(rows_f, 1, 0, main_at + cut, span)
        band.store(inner.at[1], span, cut)
        for f in range(z.fields):
            for g in range(z.core // SUB):
                core[f, g] = tile_of(inner.at[1], f, slice(z.halo + SUB * g, z.halo + SUB * (g + 1)))


def place_halo(z, half, second, pay, edges, rows_f, rows_c):
    for g in range(z.payload):
        tile = pay[g].astype(F32)
        for p in range(2):
            edges[p, SUB * g : SUB * (g + 1), :] = tile[SUB * p : SUB * (p + 1)]

    def place(side):
        q = 1 - side if second else side
        blocks = [(rows_c.at[q, c], z.coef_starts[c], z.coef_depths[c]) for c in range(4)]
        for k in range(z.steps):
            for f in range(z.fields):
                blocks.append((rows_f.at[q, k, f], z.starts[k] + f * z.depths[k], z.depths[k]))
        for ref, start, depth in blocks:
            at = z.main if side else z.halo - depth
            for p in range(2):
                ref[p, at : at + depth, :] = edges[p, start : start + depth, :]

    for side in range(2):
        pl.when(half == side)(functools.partial(place, side))


def halo_kernel(z, ra, rows_f_in, rows_c_in, rows_f, rows_c, edges):
    half, _ = half_and_chip()
    place_halo(z, half, False, ra, edges, rows_f, rows_c)


def rim_kernel(z, active, rb, inner, mix_first, mix_last, rows_f_in, rows_c_in, rows_f, rows_c, ko, so, edge, *refs):
    (co_core, co_rim, co_late), (obuf, tmp, edges), scratch = refs[:3], refs[3:6], refs[6:]
    half, chip = half_and_chip()
    place_halo(z, half, True, rb, edges, rows_f, rows_c)

    @pl.when(chip != active)
    def _():
        for q, co, mix, columns, offset in (
            (0, co_core, mix_first, z.core, z.halo * (2 - half)),
            (0, co_rim, mix_first, z.outer, (z.window - z.outer) * half),
            (1, co_late, mix_last, z.main - z.halo, z.halo * half + z.inset),
        ):
            Band(z, (*scratch[:4], co, mix)).set_operators(rows_c, q, offset, columns // SUB)

    @pl.when(chip == active)
    def _():
        band = Band(z, (*scratch, mix_first))
        start = z.halo - z.depth
        offset = start + (z.main + z.depth - z.rim - start) * half
        base = start + (2 * z.halo + z.depth - z.rim - start) * half
        sublane = lax.broadcasted_iota(jnp.int32, (SUB, z.lanes), 0)
        mine = []
        for g in range(z.halo // SUB):
            at = sublane + SUB * g
            mine.append(jnp.where(half == 0, at, z.halo - 1 - at) < z.rim_own)

        def keep(q):
            place = jnp.where(half == q, 1, 0)
            for f in range(z.fields):
                merged = []
                for p in range(2):
                    obuf[place, f, p] = inner[q, f, p, aligned((z.main - z.own) * half, z.own), :]
                    for g in range(z.halo // SUB):
                        rim = tmp[f, p, z.halo + SUB * g : z.halo + SUB * (g + 1), :]
                        own = inner[q, f, p, aligned((z.main - z.halo) * half + SUB * g, SUB), :]
                        merged.append(jnp.where(mine[g], rim, own))
                        obuf[place, f, p, aligned((z.own - z.halo) * half + SUB * g, SUB), :] = merged[-1]
                if q == 1:
                    for g in range(z.halo // SUB):
                        edge[f, g] = jnp.concatenate([merged[g], merged[g + z.halo // SUB]], axis=0).astype(BF16)

        band.load(rows_f.at[0, z.steps - 1], offset, z.rim // SUB)
        band.set_operators(rows_c, 0, offset, z.rim // SUB)
        band.steps(rows_f, 0, 1, offset, z.rim // SUB)
        band.store(tmp, z.rim // SUB, base)
        keep(0)
        band = Band(z, (*scratch, mix_last))
        offset = z.inset + (z.main - 2 * z.halo) * half
        band.load(tmp, z.inset, 2 * z.halo // SUB)
        band.set_operators(rows_c, 1, offset, 2 * z.halo // SUB)
        band.steps(rows_f, 1, 0, offset, 2 * z.halo // SUB)
        band.store(tmp, 2 * z.halo // SUB, z.inset)
        keep(1)
        ko[...] = obuf[0]
        so[...] = obuf[1]


def put_tiles(z, tmp, tiles, at):
    for f in range(z.fields):
        for n, tile in enumerate(tiles(f)):
            for p in range(2):
                tmp[f, p, aligned(at + SUB * n, SUB), :] = tile.astype(F32)[SUB * p : SUB * (p + 1)]


def early_kernel(z, active, core, rows_f, co, mix, state, tmp, *scratch):
    half, chip = half_and_chip()

    @pl.when(chip == active)
    def _():
        band = Band(z, scratch + (co, mix))
        span = z.core // SUB
        put_tiles(z, tmp, lambda f: [core[f, g] for g in range(z.core // SUB)], 0)
        band.load(tmp, 0, span)
        band.steps(rows_f, 0, 0, z.halo * (2 - half), span)
        band.store(state, span, z.base)


def late_kernel(
    z, active, core, near, far, state, rows_f, co_rim, mix_first, co_late, mix_last, ko_in, so_in, ko, so, obuf, tmp, *scratch
):
    half, chip = half_and_chip()

    @pl.when(chip == active)
    def _():
        groups = z.halo // SUB
        span = z.outer // SUB
        put_tiles(z, tmp, lambda f: [far[f, g] for g in range(groups)], 2 * z.halo * half)
        put_tiles(z, tmp, lambda f: [near[f, g] for g in range(groups)], z.halo)
        first = (z.core // SUB - groups) * half
        put_tiles(z, tmp, lambda f: [core[f, first + g] for g in range(groups)], 2 * z.halo * (1 - half))
        band = Band(z, scratch + (co_rim, mix_first))
        band.load(tmp, 0, span)
        band.steps(rows_f, 0, 0, (z.window - z.outer) * half, span)
        band.store(tmp, span, z.base)
        outer, inner = 2 * z.halo, z.core - z.halo
        start = z.inset + z.base
        for f in range(z.fields):
            for p in range(2):
                rim = tmp[f, p, start : start + outer, :]
                tmp[f, p, aligned(inner * half, outer), :] = rim
                tmp[f, p, aligned(outer * (1 - half), inner), :] = state[f, p, start : start + inner, :]
                obuf[1 - half, f, p] = tmp[f, p, z.inset : z.inset + z.own, :]
        band = Band(z, scratch + (co_late, mix_last))
        band.load(tmp, 0, z.narrow)
        band.steps(rows_f, 1, 0, z.halo * half + z.inset, z.narrow)
        band.store(tmp, z.narrow)
        for f in range(z.fields):
            for p in range(2):
                obuf[half, f, p] = tmp[f, p, z.inset : z.inset + z.own, :]
        ko[...] = obuf[0]
        so[...] = obuf[1]


def finish_kernel(z, keep, got, out, rows, sems):
    half, _ = half_and_chip()
    copies = []
    for f in range(z.fields):
        for p in range(2):
            a, b = keep[f, p], got[f, p]
            west = jnp.where(half == 0, a, b)
            east = jnp.where(half == 0, b, a)
            rows[f, pl.ds(p, z.lanes, stride=2), :] = jnp.concatenate([west, east], axis=0).T
        copies.append(pltpu.make_async_copy(rows.at[f], out.at[0, f], sems.at[f]))
        copies[-1].start()
    for copy in copies:
        copy.wait()


def shape(dims, dtype):
    return jax.ShapeDtypeStruct(tuple(dims), dtype)


def in_vmem(count):
    return [pl.BlockSpec(memory_space=pltpu.VMEM)] * count


def in_hbm(count):
    return [pl.BlockSpec(memory_space=pltpu.HBM)] * count


def per_device(forcing, zonal_courant, meridional_courant, zonal_faces, meridional_faces, coupling):
    z = Sizes(forcing.shape)
    tm_count, strips = lax.axis_size("tm"), lax.axis_size("space")
    assert tm_count == 4 and z.main % 16 == 0 and z.shift % 16 == 0
    params = pltpu.CompilerParams(vmem_limit_bytes=VMEM_BYTES)
    f_shape = (z.steps, z.fields, 2, z.main, z.lanes)
    c_shape = (5, 2, z.main, z.lanes)
    pay_shape = (z.payload, 2 * SUB, z.lanes)
    keep_f, send_f, keep_c, send_c, pay_a, pay_b = pl.pallas_call(
        functools.partial(prepare_kernel, z),
        out_shape=[
            shape(f_shape, BF16),
            shape(f_shape, BF16),
            shape(c_shape, F32),
            shape(c_shape, F32),
            shape(pay_shape, BF16),
            shape(pay_shape, BF16),
        ],
        in_specs=in_hbm(6),
        out_specs=in_vmem(6),
        scratch_shapes=[
            pltpu.VMEM(forcing.shape[1:], BF16),
            pltpu.VMEM((4, z.rows, z.strip), F32),
            pltpu.VMEM((z.fields, 1, z.fields), F32),
            pltpu.VMEM((4, z.rows, z.strip), F32),
            pltpu.VMEM((2, 2, SUB * z.payload, z.lanes), F32),
            pltpu.SemaphoreType.DMA((5 + 2 * z.steps,)),
        ],
        compiler_params=params,
        name="prepare",
    )(
        *[
            pltpu.with_memory_space_constraint(array, pltpu.HBM)
            for array in (
                forcing,
                zonal_courant,
                meridional_courant,
                zonal_faces,
                meridional_faces,
                jnp.swapaxes(coupling, 0, 1),
            )
        ]
    )

    def device(tm, space):
        return tm * strips + space % strips

    everyone = [(t, s) for t in range(tm_count) for s in range(strips)]
    partner = [(t, t ^ 1) for t in range(tm_count)]
    perm_a = [(device(t, s), device(t ^ 1, s + 1 if t % 2 else s - 1)) for t, s in everyone]
    perm_b = [(device(t, s), device(t, s - 1 if t % 2 else s + 1)) for t, s in everyone]
    got_f = lax.ppermute(send_f, "tm", partner)
    got_c = lax.ppermute(send_c, "tm", partner)
    got_a = lax.ppermute(pay_a, ("tm", "space"), perm_a)
    got_b = lax.ppermute(pay_b, ("tm", "space"), perm_b)

    def band_scratch(span):
        state = pltpu.VMEM((span + 2, z.fields, 2, SUB, z.lanes), F32)
        return [state] * 4

    def stencil(columns):
        return shape((columns // SUB + 2, 8, 2, SUB, z.lanes), F32)

    mixing = shape((z.fields**2, SUB, z.lanes), F32)

    def stencil_scratch(columns):
        return [pltpu.VMEM(stencil(columns).shape, F32)]

    rows_f_shape = shape((2, z.steps, z.fields, 2, z.window, z.lanes), F32)
    rows_c_shape = shape((2, 4, 2, z.window, z.lanes), F32)
    half_dims = (z.fields, 2, z.own, z.lanes)
    def tiles(columns):
        return shape((z.fields, columns // SUB, 2 * SUB, z.lanes), BF16)

    rows_f, rows_c = pl.pallas_call(
        functools.partial(spread_kernel, z),
        out_shape=[rows_f_shape, rows_c_shape],
        in_specs=in_vmem(2),
        out_specs=in_vmem(2),
        compiler_params=params,
        name="spread",
    )(keep_f, keep_c)
    rows_f, rows_c, inner, core, mix_first, mix_last = pl.pallas_call(
        functools.partial(inner_kernel, z, 1),
        out_shape=[
            rows_f_shape,
            rows_c_shape,
            shape((2, z.fields, 2, z.main, z.lanes), F32),
            tiles(z.core),
            mixing,
            mixing,
        ],
        in_specs=in_vmem(5),
        out_specs=in_vmem(6),
        input_output_aliases={3: 0, 4: 1},
        scratch_shapes=band_scratch(z.wide) + stencil_scratch(z.main) + [pltpu.VMEM((2, SUB, z.lanes), F32)],
        compiler_params=params,
        cost_estimate=pl.CostEstimate(flops=10**9, bytes_accessed=2 * 10**7, transcendentals=0),
        name="inner",
    )(got_f, got_c, keep_c, rows_f, rows_c)
    down = [(device(t, s), device(t ^ 2, s)) for t, s in everyone]
    across = [(device(t, s), device((t ^ 1) - 2, s + 1 if t % 2 else s - 1) if t >= 2 else device(t + 2, s)) for t, s in everyone]
    core = lax.ppermute(core, ("tm", "space"), down)
    rows_f, rows_c = pl.pallas_call(
        functools.partial(halo_kernel, z),
        out_shape=[rows_f_shape, rows_c_shape],
        in_specs=in_vmem(3),
        out_specs=in_vmem(2),
        input_output_aliases={1: 0, 2: 1},
        scratch_shapes=[pltpu.VMEM((2, SUB * z.payload, z.lanes), F32)],
        compiler_params=params,
        name="halo",
    )(got_a, rows_f, rows_c)
    rows_f, rows_c, kept, sent, edge, co_core, co_rim, co_late = pl.pallas_call(
        functools.partial(rim_kernel, z, 1),
        out_shape=[
            rows_f_shape,
            rows_c_shape,
            shape(half_dims, F32),
            shape(half_dims, F32),
            tiles(z.halo),
            stencil(z.core),
            stencil(z.outer),
            stencil(z.main - z.halo),
        ],
        in_specs=in_vmem(6),
        out_specs=in_vmem(8),
        input_output_aliases={4: 0, 5: 1},
        scratch_shapes=[
            pltpu.VMEM((2,) + half_dims, F32),
            pltpu.VMEM((z.fields, 2, z.rim + SUB, z.lanes), F32),
            pltpu.VMEM((2, SUB * z.payload, z.lanes), F32),
        ]
        + band_scratch(z.wide)
        + stencil_scratch(z.rim),
        compiler_params=params,
        cost_estimate=pl.CostEstimate(flops=10**9, bytes_accessed=2 * 10**7, transcendentals=0),
        name="rim",
    )(got_b, inner, mix_first, mix_last, rows_f, rows_c)
    state = pl.pallas_call(
        functools.partial(early_kernel, z, 0),
        out_shape=shape((z.fields, 2, z.core + SUB, z.lanes), F32),
        in_specs=in_vmem(4),
        out_specs=pl.BlockSpec(memory_space=pltpu.VMEM),
        scratch_shapes=[pltpu.VMEM((z.fields, 2, z.core, z.lanes), F32)] + band_scratch(z.core // SUB),
        compiler_params=params,
        name="early",
    )(core, rows_f, co_core, mix_first)
    far = lax.ppermute(edge, ("tm", "space"), across)
    near = lax.ppermute(edge, ("tm", "space"), down)
    kept, sent = pl.pallas_call(
        functools.partial(late_kernel, z, 0),
        out_shape=[shape(half_dims, F32), shape(half_dims, F32)],
        in_specs=in_vmem(11),
        out_specs=in_vmem(2),
        input_output_aliases={9: 0, 10: 1},
        scratch_shapes=[
            pltpu.VMEM((2,) + half_dims, F32),
            pltpu.VMEM((z.fields, 2, z.main, z.lanes), F32),
        ]
        + band_scratch(z.narrow),
        compiler_params=params,
        name="late",
    )(core, near, far, state, rows_f, co_rim, mix_first, co_late, mix_last, kept, sent)
    got = lax.ppermute(sent, "tm", partner)
    return pl.pallas_call(
        functools.partial(finish_kernel, z),
        out_shape=shape((1, z.fields, z.rows, z.strip), F32),
        in_specs=in_vmem(2),
        out_specs=pl.BlockSpec(memory_space=pltpu.HBM),
        scratch_shapes=[
            pltpu.VMEM((z.fields, z.rows, z.strip), F32),
            pltpu.SemaphoreType.DMA((z.fields,)),
        ],
        compiler_params=params,
        name="finish",
    )(kept, got)


def solution(mesh):
    return jax.shard_map(
        per_device,
        mesh=mesh,
        in_specs=(
            P("tm", None, None, None, "space"),
            P("tm", None, "space"),
            P("tm", None, "space"),
            P("tm", None, "space"),
            P("tm", None, "space"),
            P("tm", None, None),
        ),
        out_specs=P("tm", None, None, "space"),
        check_vma=False,
    )
```
